256 devices in a mesh: group: 64 (over y_lo, x, z), mp: 4 (over y_hi, core).
Axes of the slice: x: 4, y: 4 (y_hi: 2, y_lo: 2; y = y_hi * 2 + y_lo), z: 8, core: 2. Of those that a mesh axis runs over, the one named last changes fastest.
Arguments:
- tokens: bfloat16 [24576, 1024], P('group', 'mp'), may hold values from -6 to 6
- cotangent: bfloat16 [24576, 1024], P('group', 'mp'), may hold values from -6 to 6
- tags: int32 [24576], P('group'), may hold values from 0 to 2, as said below
- counts: int32 [3], replicated, may hold values from 384 to 12288, as said below
- target: int32 [24576], P('group'), may hold values from 0 to 31, as said below
- gate_weight: bfloat16 [3, 1024, 4096], P(None, 'group', 'mp'), may hold values from -0.1875 to 0.1875
- up_weight: bfloat16 [3, 1024, 4096], P(None, 'group', 'mp'), may hold values from -0.1875 to 0.1875
- down_weight: bfloat16 [3, 1024, 4096], P(None, 'group', 'mp'), may hold values from -0.09375 to 0.09375
Outputs:
- mixed: bfloat16 [24576, 1024], P('group', 'mp')
- token_grad: bfloat16 [24576, 1024], P('group', 'mp')
- gate_grad: float32 [3, 1024, 4096], P(None, 'group', 'mp')
- up_grad: float32 [3, 1024, 4096], P(None, 'group', 'mp')
- down_grad: float32 [3, 1024, 4096], P(None, 'group', 'mp')
The draws below stay inside these ranges and needn't reach their ends.
Inputs may be any that keep to these rules, and one draw needn't show every extreme that they name: tags[t] is the modality of token t. counts[m] is the number of tokens tagged m and a multiple of 384; every modality is served by 1 to 32 devices, exactly one of them by 32. start[tags] + target lies in the range of devices that serve the token's modality; of the 384 tokens of one index of group at most 12 go to any one device, exactly 12 to some device in every owner and from some owner to every device; every device receives exactly 384 tokens in all.
All inputs are finite; a program needn't handle non-finite values.
Results may differ from the reference program's by a relative error of at most 0.005.
Values may be sent and summed in bfloat16 or wider, within the bound.
A program may use at most 128 MiB of HBM per device.

```python
import jax
import jax.numpy as jnp
from jax import lax

D = 1024
FF = 4096
MODS = 3
TOK_DEV = 384
TOKENS = 24576
N_GROUP = 64


def route_plan(key):
    groups = N_GROUP
    mean = TOK_DEV // groups
    key_shift, key_vals, key_perm, key_rows, key_sizes = jax.random.split(key, 5)
    shift = jax.random.permutation(key_shift, groups).astype(jnp.int32)
    spread = jax.random.randint(key_vals, (groups // 2,), -mean, mean + 1).astype(jnp.int32)
    spread = spread.at[0].set(mean)
    values = jnp.concatenate([mean + spread, mean - spread]).astype(jnp.int32)
    values = jax.random.permutation(key_perm, values)
    cols = jnp.arange(groups, dtype=jnp.int32)
    table = values[(cols[None, :] - shift[:, None]) % groups]
    bounds = jnp.cumsum(table, axis=1)
    places = jnp.arange(TOK_DEV, dtype=jnp.int32)
    ordered = jnp.sum((bounds[:, None, :] <= places[None, :, None]).astype(jnp.int32), axis=2)
    row_keys = jax.random.split(key_rows, groups)
    mixed_rows = jax.vmap(jax.random.permutation)(row_keys, ordered)
    dest = mixed_rows.reshape(groups * TOK_DEV).astype(jnp.int32)
    key_a, key_b = jax.random.split(key_sizes)
    half = groups // 2
    split_size = jax.random.randint(key_a, (), 1, half).astype(jnp.int32)
    three = jnp.stack([jnp.asarray(half, jnp.int32), split_size, half - split_size]).astype(jnp.int32)
    sizes = three[jax.random.permutation(key_b, 3)].astype(jnp.int32)
    size_a = sizes[0]
    size_b = sizes[1]
    first_b = size_a
    first_c = size_a + size_b
    mods = ((dest >= first_b).astype(jnp.int32) + (dest >= first_c).astype(jnp.int32)).astype(jnp.int32)
    base = jnp.where(mods == 0, 0, jnp.where(mods == 1, first_b, first_c)).astype(jnp.int32)
    target = (dest - base).astype(jnp.int32)
    counts = (sizes * TOK_DEV).astype(jnp.int32)
    return (mods, counts, target)


def draw_tags(key, part):
    return route_plan(key)[0]


def draw_counts(key, part):
    return route_plan(key)[1]


def draw_target(key, part):
    return route_plan(key)[2]


def shard_levels(rng, shape, pieces, smallest, top_value):
    def one(axis_at, blocks):
        heights = jax.random.uniform(jax.random.fold_in(jax.random.fold_in(rng, 6), axis_at), (blocks,), jnp.float32, smallest / len(pieces), top_value / len(pieces))
        return jnp.repeat(jnp.exp(heights), shape[axis_at] // blocks).reshape((-1,) + (1,) * (len(shape) - axis_at - 1))

    level = one(*pieces[0])
    for cut in pieces[1:]:
        level = level * one(*cut)
    return level


def noise(key, dims, scale, reach, cuts=(), kind=jnp.bfloat16):
    drawn = jax.random.normal(key, dims, jnp.float32) * scale
    if len(cuts) > 0:
        drawn = shard_levels(key, dims, cuts, -0.22, 0.18) * drawn
    return jnp.clip(drawn, min=-reach, max=reach).astype(kind)


def setup_inputs(seed: int = 0) -> dict:
    keys = jax.random.split(jax.random.key(seed), 9)
    tokens = noise(keys[0], (TOKENS, D), 1.0, 6.0, ((0, 64), (1, 4)))
    cotangent = noise(keys[1], (TOKENS, D), 1.0, 6.0, ((0, 64), (1, 4)))
    tags = draw_tags(jax.random.fold_in(keys[8], 71), 0)
    counts = draw_counts(jax.random.fold_in(keys[8], 71), 0)
    target = draw_target(jax.random.fold_in(keys[8], 71), 0)
    gate_weight = noise(keys[5], (MODS, D, FF), D ** -0.5, 0.1875, ((1, 64), (2, 4)))
    up_weight = noise(keys[6], (MODS, D, FF), D ** -0.5, 0.1875, ((1, 64), (2, 4)))
    down_weight = noise(keys[7], (MODS, D, FF), FF ** -0.5, 0.09375, ((1, 64), (2, 4)))
    return {"tokens": tokens, "cotangent": cotangent, "tags": tags, "counts": counts, "target": target, "gate_weight": gate_weight, "up_weight": up_weight, "down_weight": down_weight}


def layer_rows(x, dy, wg, wu, wd):
    gate = jnp.dot(x, wg, preferred_element_type=jnp.float32)
    up = jnp.dot(x, wu, preferred_element_type=jnp.float32)
    sig = jax.nn.sigmoid(gate)
    silu = gate * sig
    hidden = (silu * up).astype(jnp.bfloat16)
    out = lax.dot_general(hidden, wd, (((1,), (1,)), ((), ())), preferred_element_type=jnp.float32)
    dhidden = jnp.dot(dy, wd, preferred_element_type=jnp.float32)
    dgate = (dhidden * up * sig * (1.0 + gate * (1.0 - sig))).astype(jnp.bfloat16)
    dup = (dhidden * silu).astype(jnp.bfloat16)
    dx = lax.dot_general(dgate, wg, (((1,), (1,)), ((), ())), preferred_element_type=jnp.float32)
    dx = dx + lax.dot_general(dup, wu, (((1,), (1,)), ((), ())), preferred_element_type=jnp.float32)
    grad_g = lax.dot_general(x, dgate, (((0,), (0,)), ((), ())), preferred_element_type=jnp.float32).astype(jnp.bfloat16)
    grad_u = lax.dot_general(x, dup, (((0,), (0,)), ((), ())), preferred_element_type=jnp.float32).astype(jnp.bfloat16)
    grad_d = lax.dot_general(dy, hidden, (((0,), (0,)), ((), ())), preferred_element_type=jnp.float32).astype(jnp.bfloat16)
    return out.astype(jnp.bfloat16), dx.astype(jnp.bfloat16), grad_g, grad_u, grad_d


def reference(tokens, cotangent, tags, counts, target, gate_weight, up_weight, down_weight):
    groups = N_GROUP
    total = TOKENS
    first = jnp.stack([jnp.zeros((), jnp.int32), counts[0], counts[0] + counts[1]]).astype(jnp.int32)
    start = (groups * first) // total
    base = jnp.where(tags == 0, start[0], jnp.where(tags == 1, start[1], start[2]))
    dest = (base + target).astype(jnp.int32)
    devices = jnp.arange(groups, dtype=jnp.int32)
    device_mod = ((devices >= start[1]).astype(jnp.int32) + (devices >= start[2]).astype(jnp.int32)).astype(jnp.int32)
    order = jnp.argsort(dest, stable=True).astype(jnp.int32)
    xs = tokens[order].reshape(groups, TOK_DEV, D)
    dys = cotangent[order].reshape(groups, TOK_DEV, D)
    zero = jnp.zeros((MODS, D, FF), jnp.float32)

    def step(carry, item):
        acc_g, acc_u, acc_d = carry
        x, dy, mod = item
        wg = lax.dynamic_index_in_dim(gate_weight, mod, 0, keepdims=False)
        wu = lax.dynamic_index_in_dim(up_weight, mod, 0, keepdims=False)
        wd = lax.dynamic_index_in_dim(down_weight, mod, 0, keepdims=False)
        out, dx, grad_g, grad_u, grad_d = layer_rows(x, dy, wg, wu, wd)

        def add(acc, grad):
            old = lax.dynamic_index_in_dim(acc, mod, 0, keepdims=False)
            return lax.dynamic_update_index_in_dim(acc, old + grad.astype(jnp.float32), mod, 0)

        return (add(acc_g, grad_g), add(acc_u, grad_u), add(acc_d, grad_d)), (out, dx)

    (acc_g, acc_u, acc_d), (outs, dxs) = lax.scan(step, (zero, zero, zero), (xs, dys, device_mod))
    inverse = jnp.argsort(order).astype(jnp.int32)
    mixed = outs.reshape(total, D)[inverse]
    token_grad = dxs.reshape(total, D)[inverse]
    return mixed, token_grad, acc_g, acc_u, acc_d
```

```python
import jax
import jax.numpy as jnp
from jax import lax
from jax.experimental import pallas as pl
from jax.experimental.pallas import tpu as pltpu
from jax.sharding import PartitionSpec as P

BF = jnp.bfloat16
F32 = jnp.float32
NX, NZ = 4, 8
HALF = NX * NZ
CAP = 12
SLOT = 16


def place():
    g = lax.axis_index("group")
    p = lax.axis_index("mp")
    h = lax.div(g, HALF)
    x = lax.rem(lax.div(g, NZ), NX)
    z = lax.rem(g, NZ)
    return p, h, x, z


def around(v, by, size):
    return lax.rem(v + (by + size), size)


def rows16(c):
    return pl.ds(pl.multiple_of(c * 16, 16), 16)


def greet(peers):
    barrier = pltpu.get_barrier_semaphore()
    for peer in peers:
        pl.semaphore_signal(barrier, inc=1, device_id=peer, device_id_type=pl.DeviceIdType.MESH)
    pl.semaphore_wait(barrier, len(peers))


def remote(src, dst, send, recv, peer):
    copy = pltpu.make_async_remote_copy(
        src_ref=src,
        dst_ref=dst,
        send_sem=send,
        recv_sem=recv,
        device_id=peer,
        device_id_type=pl.DeviceIdType.MESH,
    )
    copy.start()
    return copy


def gather_kernel(
    flags, wg, wu, wd, og, ou, od, zg, zu, zd, sbuf, relay, ys, yr, zs, zr, xs, xr, own
):
    p, h, x, z = place()

    def at(hh, xx, zz):
        return (hh * HALF + xx * NZ + zz, p)

    over = at(1 - h, x, z)
    zright, zleft = at(h, x, around(z, 1, NZ)), at(h, x, around(z, -1, NZ))
    xright, xleft = at(h, around(x, 1, NX), z), at(h, around(x, -1, NX), z)
    greet([over, zright, zleft, xright, xleft])
    weights = (wg, wu, wd)
    outs = (og, ou, od)
    zbuf = (zg, zu, zd)
    sends = []

    cross = []
    for w in range(3):
        cross.append(
            remote(
                weights[w].at[pl.ds(1 - h, 2)],
                zbuf[w].at[:, h, rows16(z), :],
                ys.at[w],
                yr.at[w],
                over,
            )
        )
        zbuf[w][:, h, rows16(z), :] = weights[w][pl.ds(h, 2)]

    def ring(w):
        cross[w].wait_recv()
        sends.append(cross[w])
        right = left = None
        for s in range(4):
            if s > 0:
                right.wait_recv()
                left.wait_recv()
            cr, cl = rows16(around(z, -s, NZ)), rows16(around(z, s, NZ))
            if s < 3:
                r, l = zbuf[w].at[:, :, cr, :], zbuf[w].at[:, :, cl, :]
            else:
                r, l = zbuf[w].at[:, 0, cr, :], zbuf[w].at[:, 1, cl, :]
            right = remote(r, r, zs.at[w, 0, s], zr.at[w, 0, s], zright)
            left = remote(l, l, zs.at[w, 1, s], zr.at[w, 1, s], zleft)
            sends.extend([right, left])
        right.wait_recv()
        left.wait_recv()

    waits = []
    far = {}

    def spread(w):
        for d in (2, 1, 3, 0):
            f = flags[h * HALF + around(x, d, NX) * NZ + z]
            sbuf[w, d] = zbuf[w][f]
            if d == 2:
                a = remote(sbuf.at[w, 2, 0], relay.at[w, 0], xs.at[w, 0], xr.at[w, 0], xright)
                b = remote(sbuf.at[w, 2, 1], relay.at[w, 1], xs.at[w, 1], xr.at[w, 1], xleft)
                far[w] = (a, b)
                sends.extend([a, b])
            elif d == 1:
                a = remote(sbuf.at[w, 1], outs[w].at[:, x], xs.at[w, 2], xr.at[w, 2], xright)
                sends.append(a)
                waits.append(a)
            elif d == 3:
                a = remote(sbuf.at[w, 3], outs[w].at[:, x], xs.at[w, 3], xr.at[w, 3], xleft)
                sends.append(a)
                waits.append(a)
            else:
                a = pltpu.make_async_copy(sbuf.at[w, 0], outs[w].at[:, x], own.at[w])
                a.start()
                far[w] = far[w] + (a,)

    def pass_on(w):
        a, b, c = far[w]
        a.wait_recv()
        r = remote(
            relay.at[w, 0],
            outs[w].at[0, around(x, -1, NX)],
            xs.at[w, 4],
            xr.at[w, 4],
            xright,
        )
        b.wait_recv()
        l = remote(
            relay.at[w, 1],
            outs[w].at[1, around(x, 1, NX)],
            xs.at[w, 5],
            xr.at[w, 5],
            xleft,
        )
        sends.extend([r, l])
        waits.extend([r, l])

    ring(0)
    spread(0)
    ring(1)
    pass_on(0)
    spread(1)
    ring(2)
    pass_on(1)
    spread(2)
    pass_on(2)
    for c in waits:
        c.wait_recv()
    for c in sends:
        c.wait_send()
    for w in range(3):
        far[w][2].wait()


def gather_weights(flags, wg, wu, wd):
    cols = wg.shape[2]
    vm = pl.BlockSpec(memory_space=pltpu.VMEM)
    dma = pltpu.SemaphoreType.DMA
    out = jax.ShapeDtypeStruct((2, NX, 16 * NZ, cols), BF)
    return pl.pallas_call(
        gather_kernel,
        out_shape=(out, out, out),
        in_specs=[pl.BlockSpec(memory_space=pltpu.SMEM), vm, vm, vm],
        out_specs=[pl.BlockSpec(memory_space=pl.ANY)] * 3,
        scratch_shapes=[
            pltpu.VMEM((2, 2, 16 * NZ, cols), BF),
            pltpu.VMEM((2, 2, 16 * NZ, cols), BF),
            pltpu.VMEM((2, 2, 16 * NZ, cols), BF),
            pltpu.VMEM((3, 4, 2, 16 * NZ, cols), BF),
            pltpu.VMEM((3, 2, 16 * NZ, cols), BF),
            dma((3,)),
            dma((3,)),
            dma((3, 2, 4)),
            dma((3, 2, 4)),
            dma((3, 6)),
            dma((3, 6)),
            dma((3,)),
        ],
        compiler_params=pltpu.CompilerParams(
            collective_id=0, has_side_effects=True, vmem_limit_bytes=48 * 1024 * 1024
        ),
        cost_estimate=pl.CostEstimate(flops=0, bytes_accessed=200_000_000, transcendentals=0),
        name="gather_weights",
    )(flags, wg, wu, wd)


def reduce_kernel(
    flags,
    gg,
    gu,
    gd,
    og,
    ou,
    od,
    rbuf,
    relay,
    zsum,
    zin,
    keep,
    ysend,
    yin,
    ys,
    yr,
    zs,
    zr,
    xs,
    xr,
    own,
):
    p, h, x, z = place()

    def at(hh, xx, zz):
        return (hh * HALF + xx * NZ + zz, p)

    over = at(1 - h, x, z)
    zright, zleft = at(h, x, around(z, 1, NZ)), at(h, x, around(z, -1, NZ))
    xr1, xl1 = around(x, 1, NX), around(x, -1, NX)
    xright, xleft = at(h, xr1, z), at(h, xl1, z)
    greet([over, zright, zleft, xright, xleft])
    grads = (gg, gu, gd)
    outs = (og, ou, od)
    sends = []
    first = {}

    def spread(w):
        g = grads[w]
        x2 = around(x, 2, NX)
        a = remote(g.at[0, x2], relay.at[w, 0], xs.at[w, 0], xr.at[w, 0], xright)
        b = remote(g.at[1, x2], relay.at[w, 1], xs.at[w, 1], xr.at[w, 1], xleft)
        c = remote(g.at[:, xr1], rbuf.at[w, 1], xs.at[w, 2], xr.at[w, 2], xright)
        d = remote(g.at[:, xl1], rbuf.at[w, 3], xs.at[w, 3], xr.at[w, 3], xleft)
        e = pltpu.make_async_copy(g.at[:, x], rbuf.at[w, 0], own.at[w])
        e.start()
        sends.extend([a, b, c, d])
        first[w] = (a, b, c, d, e)

    def pass_on(w):
        a, b, c, d, e = first[w]
        a.wait_recv()
        r = remote(relay.at[w, 0], rbuf.at[w, 2, 0], xs.at[w, 4], xr.at[w, 4], xright)
        b.wait_recv()
        l = remote(relay.at[w, 1], rbuf.at[w, 2, 1], xs.at[w, 5], xr.at[w, 5], xleft)
        sends.extend([r, l])
        first[w] = (c, d, r, l, e)

    def bins(w):
        c, d, r, l, e = first[w]
        e.wait()
        c.wait_recv()
        d.wait_recv()
        r.wait_recv()
        l.wait_recv()
        marks = [
            flags[h * HALF + around(x, by, NX) * NZ + z].astype(F32) for by in (0, -1, 2, 1)
        ]

        def body(i, _):
            y = lax.div(i, NZ)
            at_rows = rows16(lax.rem(i, NZ))
            low = high = None
            for k in range(4):
                v = rbuf[w, k, y, at_rows, :].astype(F32)
                b = v * marks[k]
                a = v - b
                low = a if low is None else low + a
                high = b if high is None else high + b
            zsum[w, 0, y, at_rows, :] = low.astype(BF)
            zsum[w, 1, y, at_rows, :] = high.astype(BF)
            return 0

        lax.fori_loop(0, 2 * NZ, body, 0)

    steps = {}

    def plus(a, b):
        return (a.astype(F32) + b.astype(F32)).astype(BF)

    def ring(w, s):
        for way, (peer, sign) in enumerate(((zright, 1), (zleft, -1))):
            part = rows16(around(z, sign * (4 - s), NZ))
            if s == 0:
                c = remote(
                    zsum.at[w, :, way, part, :],
                    zin.at[w, way, 0, :, way],
                    zs.at[w, way, 0],
                    zr.at[w, way, 0],
                    peer,
                )
            else:
                steps[w, way].wait_recv()
                if s == 1:
                    zin[w, way, 0, :, way] = plus(
                        zin[w, way, 0, :, way], zsum[w, :, way, part, :]
                    )
                    zin[w, way, 0, :, 1 - way] = zsum[w, :, 1 - way, part, :]
                else:
                    zin[w, way, s - 1] = plus(zin[w, way, s - 1], zsum[w, :, :, part, :])
                c = remote(
                    zin.at[w, way, s - 1],
                    zin.at[w, way, s],
                    zs.at[w, way, s],
                    zr.at[w, way, s],
                    peer,
                )
            steps[w, way] = c
            sends.append(c)

    cross = {}

    def total(w, y):
        part = rows16(z)
        v = zsum[w, :, y, part, :].astype(F32)
        v = v + zin[w, 0, 3, :, y].astype(F32)
        return v + zin[w, 1, 3, :, y].astype(F32)

    def swap(w):
        steps[w, 0].wait_recv()
        steps[w, 1].wait_recv()
        ysend[w] = total(w, 1 - h).astype(BF)
        cross[w] = remote(ysend.at[w], yin.at[w], ys.at[w], yr.at[w], over)
        sends.append(cross[w])
        keep[w] = total(w, h)

    def finish(w):
        cross[w].wait_recv()
        out = outs[w]
        out[2 * h] = keep[w, h]
        out[1] = keep[w, 1 - h] + yin[w, h].astype(F32)
        out[2 - 2 * h] = yin[w, 1 - h].astype(F32)

    for w in range(3):
        spread(w)
    for w in range(3):
        pass_on(w)
        bins(w)
        if w > 0:
            for s in range(2, 4):
                ring(w - 1, s)
        for s in range(2):
            ring(w, s)
        if w > 0:
            swap(w - 1)
    for s in range(2, 4):
        ring(2, s)
    swap(2)
    for w in range(3):
        finish(w)
    for c in sends:
        c.wait_send()


def reduce_grads(flags, gg, gu, gd):
    cols = gg.shape[1]
    shape = (2, NX, 16 * NZ, cols)
    vm = pl.BlockSpec(memory_space=pltpu.VMEM)
    dma = pltpu.SemaphoreType.DMA
    out = jax.ShapeDtypeStruct((3, 16, cols), F32)
    return pl.pallas_call(
        reduce_kernel,
        out_shape=(out, out, out),
        in_specs=[pl.BlockSpec(memory_space=pltpu.SMEM)]
        + [pl.BlockSpec(memory_space=pl.ANY)] * 3,
        out_specs=[vm] * 3,
        scratch_shapes=[
            pltpu.VMEM((3, 4, 2, 16 * NZ, cols), BF),
            pltpu.VMEM((3, 2, 16 * NZ, cols), BF),
            pltpu.VMEM((3, 2, 2, 16 * NZ, cols), BF),
            pltpu.VMEM((3, 2, 4, 2, 2, 16, cols), BF),
            pltpu.VMEM((3, 2, 16, cols), F32),
            pltpu.VMEM((3, 2, 16, cols), BF),
            pltpu.VMEM((3, 2, 16, cols), BF),
            dma((3,)),
            dma((3,)),
            dma((3, 2, 4)),
            dma((3, 2, 4)),
            dma((3, 6)),
            dma((3, 6)),
            dma((3,)),
        ],
        compiler_params=pltpu.CompilerParams(
            collective_id=1, has_side_effects=True, vmem_limit_bytes=48 * 1024 * 1024
        ),
        cost_estimate=pl.CostEstimate(flops=0, bytes_accessed=200_000_000, transcendentals=0),
        name="reduce_grads",
    )(flags, gg.reshape(shape), gu.reshape(shape), gd.reshape(shape))


def project_rows(x, dy, wg, wu, wd):
    gate = jnp.dot(x, wg, preferred_element_type=F32)
    up = jnp.dot(x, wu, preferred_element_type=F32)
    sig = jax.nn.sigmoid(gate)
    silu = gate * sig
    hidden = (silu * up).astype(BF)
    out = lax.dot_general(hidden, wd, (((1,), (1,)), ((), ())), preferred_element_type=F32)
    dhidden = jnp.dot(dy, wd, preferred_element_type=F32)
    dgate = (dhidden * up * sig * (1.0 + gate * (1.0 - sig))).astype(BF)
    dup = (dhidden * silu).astype(BF)
    dx = lax.dot_general(dgate, wg, (((1,), (1,)), ((), ())), preferred_element_type=F32)
    dx = dx + lax.dot_general(dup, wu, (((1,), (1,)), ((), ())), preferred_element_type=F32)
    over_rows = (((0,), (0,)), ((), ()))
    grad_g = lax.dot_general(x, dgate, over_rows, preferred_element_type=F32).astype(BF)
    grad_u = lax.dot_general(x, dup, over_rows, preferred_element_type=F32).astype(BF)
    grad_d = lax.dot_general(dy, hidden, over_rows, preferred_element_type=F32).astype(BF)
    return out, dx, grad_g, grad_u, grad_d


def pick(onehot, rows):
    return jnp.dot(onehot, rows, preferred_element_type=F32).astype(BF)


def shards(tokens, cotangent, tags, counts, target, gate_weight, up_weight, down_weight):
    groups = lax.axis_size("group")
    parts = lax.axis_size("mp")
    rows, feats = tokens.shape
    total = rows * groups
    start_b = groups * counts[0] // total
    start_c = groups * (counts[0] + counts[1]) // total
    devices = jnp.arange(groups, dtype=jnp.int32)
    device_mod = (devices >= start_b).astype(jnp.int32) + (devices >= start_c).astype(jnp.int32)
    flags = device_mod - devices // HALF
    base = jnp.where(tags == 0, 0, jnp.where(tags == 1, start_b, start_c))
    dest = base + target
    onehot = (dest[:, None] == devices[None, :]).astype(BF)
    places = jnp.arange(rows, dtype=jnp.int32)
    lower = (places[:, None] > places[None, :]).astype(BF)
    earlier = jnp.dot(lower, onehot, preferred_element_type=F32)
    slot = jnp.sum(earlier * onehot.astype(F32), axis=1).astype(jnp.int32)
    sent = jnp.sum(onehot.astype(F32), axis=0)
    position = dest * SLOT + slot
    wide = groups * SLOT
    lanes = jnp.arange(wide, dtype=jnp.int32)
    both = jnp.concatenate([tokens, cotangent], axis=1)
    into = (lanes[:, None] == position[None, :]).astype(BF)
    send = jnp.dot(into, both, preferred_element_type=F32).reshape(groups, SLOT, 2 * feats)
    tail = (jnp.arange(SLOT, dtype=jnp.int32) >= CAP)[None, :, None]
    send = jnp.where(tail, sent[:, None, None], send).astype(BF).reshape(wide, 2 * feats)
    recv = lax.all_to_all(send, "group", split_axis=0, concat_axis=0, tiled=True)
    got = recv.reshape(groups, SLOT, 2 * feats)[:, CAP, 0].astype(jnp.int32)
    before = jnp.sum(jnp.where(devices[:, None] > devices[None, :], got[None, :], 0), axis=1)
    spot = jnp.arange(SLOT, dtype=jnp.int32)[None, :]
    rank = jnp.where(spot < got[:, None], before[:, None] + spot, -1).reshape(wide)
    close = (places[:, None] == rank[None, :]).astype(BF)
    open_up = (rank[:, None] == places[None, :]).astype(BF)
    mine = pick(close, recv)
    full = lax.all_gather(mine, "mp", axis=0, tiled=False)
    full = full.transpose(1, 0, 2)
    full_x = full[:, :, :feats].reshape(rows, parts * feats)
    full_dy = full[:, :, feats:].reshape(rows, parts * feats)
    w_gate, w_up, w_down = gather_weights(flags, gate_weight, up_weight, down_weight)
    depth = parts * feats
    w_gate, w_up, w_down = (w.reshape(depth, -1) for w in (w_gate, w_up, w_down))
    out, dx, grad_g, grad_u, grad_d = project_rows(full_x, full_dy, w_gate, w_up, w_down)
    pieces = jnp.concatenate(
        [out.reshape(rows, parts, feats), dx.reshape(rows, parts, feats)], axis=2
    )
    pieces = pieces.astype(BF).transpose(1, 0, 2)
    pieces = lax.all_to_all(pieces, "mp", split_axis=0, concat_axis=0, tiled=True)
    summed = jnp.sum(pieces.astype(F32), axis=0).astype(BF)
    back = pick(open_up, summed)
    back = lax.all_to_all(back, "group", split_axis=0, concat_axis=0, tiled=True)
    result = pick(into.T, back)
    mixed, token_grad = result[:, :feats], result[:, feats:]
    gate_grad, up_grad, down_grad = reduce_grads(flags, grad_g, grad_u, grad_d)
    return mixed, token_grad, gate_grad, up_grad, down_grad


def solution(mesh):
    in_specs = (
        P("group", "mp"),
        P("group", "mp"),
        P("group"),
        P(),
        P("group"),
        P(None, "group", "mp"),
        P(None, "group", "mp"),
        P(None, "group", "mp"),
    )
    out_specs = (
        P("group", "mp"),
        P("group", "mp"),
        P(None, "group", "mp"),
        P(None, "group", "mp"),
        P(None, "group", "mp"),
    )
    return jax.shard_map(shards, mesh=mesh, in_specs=in_specs, out_specs=out_specs, check_vma=False)
```

```python
import jax
import jax.numpy as jnp
from jax import lax
from jax.experimental import pallas as pl
from jax.experimental.pallas import tpu as pltpu
from jax.sharding import PartitionSpec as P

BF = jnp.bfloat16
F32 = jnp.float32
NX, NZ = 4, 8
HALF = NX * NZ
CAP = 12
SLOT = 16
SPLIT = 2
HOOKS = (1, 6, 9, 12, 1, 3)


def place():
    g = lax.axis_index("group")
    p = lax.axis_index("mp")
    h = lax.div(g, HALF)
    x = lax.rem(lax.div(g, NZ), NX)
    z = lax.rem(g, NZ)
    return p, h, x, z


def around(v, by, size):
    return lax.rem(v + (by + size), size)


def rows16(c):
    return pl.ds(pl.multiple_of(c * 16, 16), 16)


def greet(peers):
    barrier = pltpu.get_barrier_semaphore()
    for peer in peers:
        pl.semaphore_signal(barrier, inc=1, device_id=peer, device_id_type=pl.DeviceIdType.MESH)
    pl.semaphore_wait(barrier, len(peers))


def remote(src, dst, send, recv, peer):
    copy = pltpu.make_async_remote_copy(
        src_ref=src,
        dst_ref=dst,
        send_sem=send,
        recv_sem=recv,
        device_id=peer,
        device_id_type=pl.DeviceIdType.MESH,
    )
    copy.start()
    return copy


def units(cols):
    wide = cols // SPLIT
    return [(w, pl.ds(i * wide, wide)) for w in range(3) for i in range(SPLIT)]


def peers_of(p, h, x, z):
    def at(hh, xx, zz):
        return (hh * HALF + xx * NZ + zz, p)

    zline = [at(h, x, around(z, d, NZ)) for d in range(1, NZ)]
    yx = h * NX + x
    plane = []
    for d in range(1, 2 * NX):
        k = around(yx, d, 2 * NX)
        plane.append((k, at(lax.div(k, NX), lax.rem(k, NX), z)))
    g = h * HALF + x * NZ + z
    core = p + 1 - 2 * lax.rem(p, 2)
    opposite = around(p, 2, 4)
    both = around(core, 2, 4)
    parts = [(core, (g, core)), (opposite, (g, opposite)), (both, (g, both))]
    return at, zline, plane, parts


def lanes_of(p, feats):
    return pl.ds(pl.multiple_of(p * feats, 128), feats)


def gather_kernel(flags, wg, wu, wd, tok, og, ou, od, fx, fdy, close, *scratch):
    n = 3 * SPLIT
    zbuf = scratch[:n]
    sbuf, relay, tmid, rows, mine = scratch[n : n + 5]
    ys, yr, zs, zr, xs, xr, own, ts, tr, tl, ms, mr, ml = scratch[n + 5 :]
    p, h, x, z = place()
    at, zline, plane, parts = peers_of(p, h, x, z)
    over = at(1 - h, x, z)
    zright, zleft = at(h, x, around(z, 1, NZ)), at(h, x, around(z, -1, NZ))
    xright, xleft = at(h, around(x, 1, NX), z), at(h, around(x, -1, NX), z)
    greet(zline + [q for _, q in plane] + [q for _, q in parts])
    weights = (wg, wu, wd)
    outs = (og, ou, od)
    todo = units(wg.shape[2])
    sends, waits, local = [], [], []
    cross, right, left, far = {}, {}, {}, {}

    def begin(u):
        w, c = todo[u]
        cross[u] = remote(
            weights[w].at[pl.ds(1 - h, 2), :, c],
            zbuf[u].at[:, h, rows16(z), :],
            ys.at[u],
            yr.at[u],
            over,
        )
        sends.append(cross[u])
        zbuf[u][:, h, rows16(z), :] = weights[w][pl.ds(h, 2), :, c]

    def ring(u, s):
        if s == 0:
            cross[u].wait_recv()
        else:
            right[u].wait_recv()
            left[u].wait_recv()
        if s == 4:
            return
        cr, cl = rows16(around(z, -s, NZ)), rows16(around(z, s, NZ))
        if s < 3:
            r, l = zbuf[u].at[:, :, cr, :], zbuf[u].at[:, :, cl, :]
        else:
            r, l = zbuf[u].at[:, 0, cr, :], zbuf[u].at[:, 1, cl, :]
        right[u] = remote(r, r, zs.at[u, 0, s], zr.at[u, 0, s], zright)
        left[u] = remote(l, l, zs.at[u, 1, s], zr.at[u, 1, s], zleft)
        sends.extend([right[u], left[u]])

    def spread(u):
        w, c = todo[u]
        out = outs[w]
        for d in (2, 1, 3, 0):
            f = flags[h * HALF + around(x, d, NX) * NZ + z]
            sbuf[u, d] = zbuf[u][f]
            if d == 2:
                a = remote(sbuf.at[u, 2, 0], relay.at[u, 0], xs.at[u, 0], xr.at[u, 0], xright)
                b = remote(sbuf.at[u, 2, 1], relay.at[u, 1], xs.at[u, 1], xr.at[u, 1], xleft)
                far[u] = (a, b)
                sends.extend([a, b])
            elif d == 0:
                a = pltpu.make_async_copy(sbuf.at[u, 0], out.at[:, x, :, c], own.at[u])
                a.start()
                local.append(a)
            else:
                i, peer = (2, xright) if d == 1 else (3, xleft)
                a = remote(sbuf.at[u, d], out.at[:, x, :, c], xs.at[u, i], xr.at[u, i], peer)
                sends.append(a)
                waits.append(a)

    def pass_on(u):
        w, c = todo[u]
        a, b = far[u]
        for i, (got, by, peer) in enumerate(((a, -1, xright), (b, 1, xleft))):
            got.wait_recv()
            a = remote(
                relay.at[u, i],
                outs[w].at[i, around(x, by, NX), :, c],
                xs.at[u, 4 + i],
                xr.at[u, 4 + i],
                peer,
            )
            sends.append(a)
            waits.append(a)

    yx = h * NX + x
    stage = {}

    def tokens_z():
        stage["z"] = []
        for d in range(1, NZ):
            to = around(z, d, NZ)
            stage["z"].append(
                remote(tok.at[:, to], tmid.at[z], ts.at[d], tr.at[d], zline[d - 1])
            )
        a = pltpu.make_async_copy(tok.at[:, z], tmid.at[z], tl.at[0])
        a.start()
        stage["zl"] = a

    def tokens_plane():
        stage["zl"].wait()
        for c in stage["z"]:
            c.wait_recv()
        sends.extend(stage["z"])
        stage["p"] = []
        to = rows.at[pl.ds(yx * NZ, NZ)]
        for d in range(1, 2 * NX):
            k, peer = plane[d - 1]
            stage["p"].append(
                remote(tmid.at[:, k], to, ts.at[NZ + d], tr.at[NZ + d], peer)
            )
        a = pltpu.make_async_copy(tmid.at[:, yx], to, tl.at[1])
        a.start()
        stage["pl"] = a

    def compact():
        stage["pl"].wait()
        for c in stage["p"]:
            c.wait_recv()
        sends.extend(stage["p"])
        groups = rows.shape[0]
        spot = lax.broadcasted_iota(jnp.int32, (groups, SLOT, 128), 1)
        head = rows[:, :, 0:128].astype(F32)
        count = jnp.sum(jnp.where(spot == CAP, head, 0.0), axis=1)
        i = lax.broadcasted_iota(jnp.int32, (groups, groups), 0)
        j = lax.broadcasted_iota(jnp.int32, (groups, groups), 1)
        lower = jnp.where(i > j, 1.0, 0.0).astype(BF)
        before = jnp.dot(lower, count.astype(BF), preferred_element_type=F32)
        spot = spot.astype(F32)
        rank = jnp.where(spot < count[:, None, :], before[:, None, :] + spot, -1.0)
        rank = rank.reshape(groups * SLOT, 128)
        lane = lax.broadcasted_iota(jnp.int32, (groups * SLOT, 128), 1)
        for b in range(close.shape[1] // 128):
            hit = rank == (lane + b * 128).astype(F32)
            close[:, b * 128 : (b + 1) * 128] = jnp.where(hit, 1.0, 0.0).astype(BF)
        feats = rows.shape[2] // 2
        for b in range(2):
            part = rows[:, :, b * feats : (b + 1) * feats].reshape(groups * SLOT, feats)
            picked = lax.dot_general(
                close[...], part, (((0,), (0,)), ((), ())), preferred_element_type=F32
            )
            mine[b] = picked.astype(BF)
        here = lanes_of(p, feats)
        stage["m"] = []
        for b, full in enumerate((fx, fdy)):
            a = pltpu.make_async_copy(mine.at[b], full.at[:, here], ml.at[b])
            a.start()
            local.append(a)
            for i in (1, 0):
                a = remote(mine.at[b], full.at[:, here], ms.at[i, b], mr.at[i, b], parts[i][1])
                sends.append(a)
                stage["m"].append(a)

    def share():
        for c in stage["m"]:
            c.wait_recv()
        there = lanes_of(parts[1][0], fx.shape[1] // 4)
        for b, full in enumerate((fx, fdy)):
            view = full.at[:, there]
            a = remote(view, view, ms.at[2, b], mr.at[2, b], parts[0][1])
            sends.append(a)
            waits.append(a)

    for u in range(n):
        begin(u)
    for t in range(2 * n + 4):
        for u in range(n):
            s = t - 2 * u
            if s == 4 and u > 0:
                pass_on(u - 1)
            if 0 <= s <= 4:
                ring(u, s)
            if s == 4:
                spread(u)
        if t == HOOKS[0]:
            tokens_z()
        elif t == HOOKS[1]:
            tokens_plane()
        elif t == HOOKS[2]:
            compact()
        elif t == HOOKS[3]:
            share()
    pass_on(n - 1)
    for c in waits:
        c.wait_recv()
    for c in sends:
        c.wait_send()
    for c in local:
        c.wait()


def gather_all(flags, wg, wu, wd, tok, rows, feats):
    cols = wg.shape[2]
    n = 3 * SPLIT
    wide = cols // SPLIT
    vm = pl.BlockSpec(memory_space=pltpu.VMEM)
    hbm = pl.BlockSpec(memory_space=pl.ANY)
    dma = pltpu.SemaphoreType.DMA
    out = jax.ShapeDtypeStruct((2, NX, 16 * NZ, cols), BF)
    full = jax.ShapeDtypeStruct((rows, 4 * feats), BF)
    close = jax.ShapeDtypeStruct((2 * HALF * SLOT, rows), BF)
    return pl.pallas_call(
        gather_kernel,
        out_shape=(out, out, out, full, full, close),
        in_specs=[pl.BlockSpec(memory_space=pltpu.SMEM), vm, vm, vm, vm],
        out_specs=[hbm] * 5 + [vm],
        scratch_shapes=[pltpu.VMEM((2, 2, 16 * NZ, wide), BF)] * n
        + [
            pltpu.VMEM((n, 4, 2, 16 * NZ, wide), BF),
            pltpu.VMEM((n, 2, 16 * NZ, wide), BF),
            pltpu.VMEM((NZ, 2 * NX, SLOT, 2 * feats), BF),
            pltpu.VMEM((2 * HALF, SLOT, 2 * feats), BF),
            pltpu.VMEM((2, rows, feats), BF),
            dma((n,)),
            dma((n,)),
            dma((n, 2, 4)),
            dma((n, 2, 4)),
            dma((n, 6)),
            dma((n, 6)),
            dma((n,)),
            dma((16,)),
            dma((16,)),
            dma((2,)),
            dma((3, 2)),
            dma((3, 2)),
            dma((2,)),
        ],
        compiler_params=pltpu.CompilerParams(
            collective_id=0, has_side_effects=True, vmem_limit_bytes=48 * 1024 * 1024
        ),
        cost_estimate=pl.CostEstimate(flops=0, bytes_accessed=200_000_000, transcendentals=0),
        name="gather_all",
    )(flags, wg, wu, wd, tok.reshape(2 * NX, NZ, SLOT, 2 * feats))


def reduce_kernel(flags, gg, gu, gd, res, dx, close, og, ou, od, back, *scratch):
    n = 3 * SPLIT
    rbuf, relay, zsum, zin, keep, ysend, yin, pin, spread_rows, tmid = scratch[:10]
    ys, yr, zs, zr, xs, xr, own, ts, tr, tl, ms, mr, ml = scratch[10:]
    p, h, x, z = place()
    at, zline, plane, parts = peers_of(p, h, x, z)
    over = at(1 - h, x, z)
    zright, zleft = at(h, x, around(z, 1, NZ)), at(h, x, around(z, -1, NZ))
    xr1, xl1 = around(x, 1, NX), around(x, -1, NX)
    xright, xleft = at(h, xr1, z), at(h, xl1, z)
    greet(zline + [q for _, q in plane] + [q for _, q in parts])
    grads = (gg, gu, gd)
    outs = (og, ou, od)
    todo = units(gg.shape[3])
    sends = []
    first, steps, cross, stage = {}, {}, {}, {}

    def spread(u):
        w, c = todo[u]
        g = grads[w]
        x2 = around(x, 2, NX)
        a = remote(g.at[0, x2, :, c], relay.at[u, 0], xs.at[u, 0], xr.at[u, 0], xright)
        b = remote(g.at[1, x2, :, c], relay.at[u, 1], xs.at[u, 1], xr.at[u, 1], xleft)
        i = remote(g.at[:, xr1, :, c], rbuf.at[u, 1], xs.at[u, 2], xr.at[u, 2], xright)
        j = remote(g.at[:, xl1, :, c], rbuf.at[u, 3], xs.at[u, 3], xr.at[u, 3], xleft)
        e = pltpu.make_async_copy(g.at[:, x, :, c], rbuf.at[u, 0], own.at[u])
        e.start()
        sends.extend([a, b, i, j])
        first[u] = (a, b, i, j, e)

    def pass_on(u):
        a, b, i, j, e = first[u]
        a.wait_recv()
        r = remote(relay.at[u, 0], rbuf.at[u, 2, 0], xs.at[u, 4], xr.at[u, 4], xright)
        b.wait_recv()
        l = remote(relay.at[u, 1], rbuf.at[u, 2, 1], xs.at[u, 5], xr.at[u, 5], xleft)
        sends.extend([r, l])
        first[u] = (i, j, r, l, e)

    marks = [flags[h * HALF + around(x, by, NX) * NZ + z].astype(F32) for by in (0, -1, 2, 1)]

    def bins(u):
        i, j, r, l, e = first[u]
        e.wait()
        for c in (i, j, r, l):
            c.wait_recv()

        def body(i, _):
            y = lax.div(i, NZ)
            at_rows = rows16(lax.rem(i, NZ))
            low = high = None
            for k in range(4):
                v = rbuf[u, k, y, at_rows, :].astype(F32)
                b = v * marks[k]
                a = v - b
                low = a if low is None else low + a
                high = b if high is None else high + b
            zsum[u, 0, y, at_rows, :] = low.astype(BF)
            zsum[u, 1, y, at_rows, :] = high.astype(BF)
            return 0

        lax.fori_loop(0, 2 * NZ, body, 0)

    def plus(a, b):
        return (a.astype(F32) + b.astype(F32)).astype(BF)

    def ring(u, s):
        for way, (peer, sign) in enumerate(((zright, 1), (zleft, -1))):
            part = rows16(around(z, sign * (4 - s), NZ))
            if s == 0:
                c = remote(
                    zsum.at[u, :, way, part, :],
                    zin.at[u, way, 0, :, way],
                    zs.at[u, way, 0],
                    zr.at[u, way, 0],
                    peer,
                )
            else:
                steps[u, way].wait_recv()
                if s == 1:
                    zin[u, way, 0, :, way] = plus(
                        zin[u, way, 0, :, way], zsum[u, :, way, part, :]
                    )
                    zin[u, way, 0, :, 1 - way] = zsum[u, :, 1 - way, part, :]
                else:
                    zin[u, way, s - 1] = plus(zin[u, way, s - 1], zsum[u, :, :, part, :])
                c = remote(
                    zin.at[u, way, s - 1],
                    zin.at[u, way, s],
                    zs.at[u, way, s],
                    zr.at[u, way, s],
                    peer,
                )
            steps[u, way] = c
            sends.append(c)

    def total(u, y):
        part = rows16(z)
        v = zsum[u, :, y, part, :].astype(F32)
        v = v + zin[u, 0, 3, :, y].astype(F32)
        return v + zin[u, 1, 3, :, y].astype(F32)

    def swap(u):
        steps[u, 0].wait_recv()
        steps[u, 1].wait_recv()
        ysend[u] = total(u, 1 - h).astype(BF)
        cross[u] = remote(ysend.at[u], yin.at[u], ys.at[u], yr.at[u], over)
        sends.append(cross[u])
        keep[u] = total(u, h)

    def finish(u):
        w, c = todo[u]
        cross[u].wait_recv()
        out = outs[w]
        out[2 * h, :, c] = keep[u, h]
        out[1, :, c] = keep[u, 1 - h] + yin[u, h].astype(F32)
        out[2 - 2 * h, :, c] = yin[u, 1 - h].astype(F32)

    yx = h * NX + x
    feats = res.shape[1] // 4

    def sums_out():
        stage["m"] = []
        for i in (1, 2, 0):
            q, peer = parts[i]
            for b, v in enumerate((res, dx)):
                stage["m"].append(
                    remote(v.at[:, lanes_of(q, feats)], pin.at[i, b], ms.at[i, b], mr.at[i, b], peer)
                )
        here = lanes_of(p, feats)
        stage["ml"] = []
        for b, v in enumerate((res, dx)):
            a = pltpu.make_async_copy(v.at[:, here], pin.at[3, b], ml.at[b])
            a.start()
            stage["ml"].append(a)

    def widen():
        for c in stage["ml"]:
            c.wait()
        for c in stage["m"]:
            c.wait_recv()
        sends.extend(stage["m"])
        groups = spread_rows.shape[0]
        for b in range(2):
            v = pin[3, b].astype(F32)
            for i in range(3):
                v = v + pin[i, b].astype(F32)
            v = jnp.dot(close[...], v.astype(BF), preferred_element_type=F32).astype(BF)
            spread_rows[:, :, b * feats : (b + 1) * feats] = v.reshape(groups, SLOT, feats)
        stage["p"] = []
        for d in range(1, 2 * NX):
            k, peer = plane[d - 1]
            stage["p"].append(
                remote(
                    spread_rows.at[pl.ds(k * NZ, NZ)],
                    tmid.at[:, yx],
                    ts.at[NZ + d],
                    tr.at[NZ + d],
                    peer,
                )
            )
        a = pltpu.make_async_copy(spread_rows.at[pl.ds(yx * NZ, NZ)], tmid.at[:, yx], tl.at[0])
        a.start()
        stage["pl"] = a

    def homeward():
        stage["pl"].wait()
        for c in stage["p"]:
            c.wait_recv()
        sends.extend(stage["p"])
        stage["z"] = []
        for d in range(1, NZ):
            to = around(z, d, NZ)
            stage["z"].append(
                remote(tmid.at[to], back.at[:, z], ts.at[d], tr.at[d], zline[d - 1])
            )
        a = pltpu.make_async_copy(tmid.at[z], back.at[:, z], tl.at[1])
        a.start()
        stage["zl"] = a

    spread(0)
    sums_out()
    spread(1)
    pass_on(0)
    for u in range(n):
        if u + 2 < n:
            spread(u + 2)
        if u + 1 < n:
            pass_on(u + 1)
        bins(u)
        ring(u, 0)
        if u > 0:
            ring(u - 1, 2)
        ring(u, 1)
        if u > 0:
            ring(u - 1, 3)
            swap(u - 1)
        if u == HOOKS[4]:
            widen()
        if u == HOOKS[5]:
            homeward()
    ring(n - 1, 2)
    ring(n - 1, 3)
    swap(n - 1)
    for u in range(n):
        finish(u)
    stage["zl"].wait()
    for c in stage["z"]:
        c.wait_recv()
        c.wait_send()
    for c in sends:
        c.wait_send()


def reduce_all(flags, gg, gu, gd, res, dx, close):
    cols = gg.shape[1]
    rows = res.shape[0]
    feats = res.shape[1] // 4
    n = 3 * SPLIT
    wide = cols // SPLIT
    shape = (2, NX, 16 * NZ, cols)
    vm = pl.BlockSpec(memory_space=pltpu.VMEM)
    hbm = pl.BlockSpec(memory_space=pl.ANY)
    dma = pltpu.SemaphoreType.DMA
    out = jax.ShapeDtypeStruct((3, 16, cols), F32)
    back = jax.ShapeDtypeStruct((2 * NX, NZ, SLOT, 2 * feats), BF)
    return pl.pallas_call(
        reduce_kernel,
        out_shape=(out, out, out, back),
        in_specs=[pl.BlockSpec(memory_space=pltpu.SMEM)] + [hbm] * 5 + [vm],
        out_specs=[vm] * 3 + [hbm],
        scratch_shapes=[
            pltpu.VMEM((n, 4, 2, 16 * NZ, wide), BF),
            pltpu.VMEM((n, 2, 16 * NZ, wide), BF),
            pltpu.VMEM((n, 2, 2, 16 * NZ, wide), BF),
            pltpu.VMEM((n, 2, 4, 2, 2, 16, wide), BF),
            pltpu.VMEM((n, 2, 16, wide), F32),
            pltpu.VMEM((n, 2, 16, wide), BF),
            pltpu.VMEM((n, 2, 16, wide), BF),
            pltpu.VMEM((4, 2, rows, feats), BF),
            pltpu.VMEM((2 * HALF, SLOT, 2 * feats), BF),
            pltpu.VMEM((NZ, 2 * NX, SLOT, 2 * feats), BF),
            dma((n,)),
            dma((n,)),
            dma((n, 2, 4)),
            dma((n, 2, 4)),
            dma((n, 6)),
            dma((n, 6)),
            dma((n,)),
            dma((16,)),
            dma((16,)),
            dma((2,)),
            dma((3, 2)),
            dma((3, 2)),
            dma((2,)),
        ],
        compiler_params=pltpu.CompilerParams(
            collective_id=1, has_side_effects=True, vmem_limit_bytes=48 * 1024 * 1024
        ),
        cost_estimate=pl.CostEstimate(flops=0, bytes_accessed=200_000_000, transcendentals=0),
        name="reduce_all",
    )(flags, gg.reshape(shape), gu.reshape(shape), gd.reshape(shape), res, dx, close)


def project_rows(x, dy, wg, wu, wd):
    gate = jnp.dot(x, wg, preferred_element_type=F32)
    up = jnp.dot(x, wu, preferred_element_type=F32)
    sig = jax.nn.sigmoid(gate)
    silu = gate * sig
    hidden = (silu * up).astype(BF)
    out = lax.dot_general(hidden, wd, (((1,), (1,)), ((), ())), preferred_element_type=F32)
    dhidden = jnp.dot(dy, wd, preferred_element_type=F32)
    dgate = (dhidden * up * sig * (1.0 + gate * (1.0 - sig))).astype(BF)
    dup = (dhidden * silu).astype(BF)
    dx = lax.dot_general(dgate, wg, (((1,), (1,)), ((), ())), preferred_element_type=F32)
    dx = dx + lax.dot_general(dup, wu, (((1,), (1,)), ((), ())), preferred_element_type=F32)
    over_rows = (((0,), (0,)), ((), ()))
    grad_g = lax.dot_general(x, dgate, over_rows, preferred_element_type=F32).astype(BF)
    grad_u = lax.dot_general(x, dup, over_rows, preferred_element_type=F32).astype(BF)
    grad_d = lax.dot_general(dy, hidden, over_rows, preferred_element_type=F32).astype(BF)
    return out, dx, grad_g, grad_u, grad_d


def shards(tokens, cotangent, tags, counts, target, gate_weight, up_weight, down_weight):
    groups = lax.axis_size("group")
    rows, feats = tokens.shape
    total = rows * groups
    start_b = groups * counts[0] // total
    start_c = groups * (counts[0] + counts[1]) // total
    devices = jnp.arange(groups, dtype=jnp.int32)
    device_mod = (devices >= start_b).astype(jnp.int32) + (devices >= start_c).astype(jnp.int32)
    flags = device_mod - devices // HALF
    base = jnp.where(tags == 0, 0, jnp.where(tags == 1, start_b, start_c))
    dest = base + target
    onehot = (dest[:, None] == devices[None, :]).astype(BF)
    places = jnp.arange(rows, dtype=jnp.int32)
    lower = (places[:, None] > places[None, :]).astype(BF)
    earlier = jnp.dot(lower, onehot, preferred_element_type=F32)
    slot = jnp.sum(earlier * onehot.astype(F32), axis=1).astype(jnp.int32)
    sent = jnp.sum(onehot.astype(F32), axis=0)
    position = dest * SLOT + slot
    wide = groups * SLOT
    lanes = jnp.arange(wide, dtype=jnp.int32)
    both = jnp.concatenate([tokens, cotangent], axis=1)
    into = (lanes[:, None] == position[None, :]).astype(BF)
    send = jnp.dot(into, both, preferred_element_type=F32).reshape(groups, SLOT, 2 * feats)
    tail = (jnp.arange(SLOT, dtype=jnp.int32) >= CAP)[None, :, None]
    send = jnp.where(tail, sent[:, None, None], send).astype(BF).reshape(wide, 2 * feats)
    w_gate, w_up, w_down, full_x, full_dy, close = gather_all(
        flags, gate_weight, up_weight, down_weight, send, rows, feats
    )
    depth = full_x.shape[1]
    w_gate, w_up, w_down = (w.reshape(depth, -1) for w in (w_gate, w_up, w_down))
    out, dx, grad_g, grad_u, grad_d = project_rows(full_x, full_dy, w_gate, w_up, w_down)
    gate_grad, up_grad, down_grad, back = reduce_all(
        flags, grad_g, grad_u, grad_d, out.astype(BF), dx.astype(BF), close
    )
    out_of = (position[:, None] == lanes[None, :]).astype(BF)
    result = jnp.dot(out_of, back.reshape(wide, 2 * feats), preferred_element_type=F32).astype(BF)
    return result[:, :feats], result[:, feats:], gate_grad, up_grad, down_grad


def solution(mesh):
    in_specs = (
        P("group", "mp"),
        P("group", "mp"),
        P("group"),
        P(),
        P("group"),
        P(None, "group", "mp"),
        P(None, "group", "mp"),
        P(None, "group", "mp"),
    )
    out_specs = (
        P("group", "mp"),
        P("group", "mp"),
        P(None, "group", "mp"),
        P(None, "group", "mp"),
        P(None, "group", "mp"),
    )
    return jax.shard_map(shards, mesh=mesh, in_specs=in_specs, out_specs=out_specs, check_vma=False)
```

```python
import jax
import jax.numpy as jnp
from jax import lax
from jax.experimental import pallas as pl
from jax.experimental.pallas import tpu as pltpu
from jax.sharding import PartitionSpec as P

BF = jnp.bfloat16
F32 = jnp.float32
NX, NZ = 4, 8
HALF = NX * NZ
CAP = 12
SLOT = 16
UNITS = (
    (0, 0, 256),
    (0, 256, 384),
    (0, 640, 384),
    (1, 0, 512),
    (1, 512, 512),
    (2, 0, 640),
)
FLIP = (2, 640, 384)


def place():
    g = lax.axis_index("group")
    p = lax.axis_index("mp")
    h = lax.div(g, HALF)
    x = lax.rem(lax.div(g, NZ), NX)
    z = lax.rem(g, NZ)
    return p, h, x, z


def around(v, by, size):
    return lax.rem(v + (by + size), size)


def rows16(c):
    return pl.ds(pl.multiple_of(c * 16, 16), 16)


def greet(peers):
    barrier = pltpu.get_barrier_semaphore()
    for peer in peers:
        pl.semaphore_signal(barrier, inc=1, device_id=peer, device_id_type=pl.DeviceIdType.MESH)
    pl.semaphore_wait(barrier, len(peers))


def remote(src, dst, send, recv, peer):
    copy = pltpu.make_async_remote_copy(
        src_ref=src,
        dst_ref=dst,
        send_sem=send,
        recv_sem=recv,
        device_id=peer,
        device_id_type=pl.DeviceIdType.MESH,
    )
    copy.start()
    return copy


def peers_of(p, h, x, z):
    def at(hh, xx, zz):
        return (hh * HALF + xx * NZ + zz, p)

    zline = [at(h, x, around(z, d, NZ)) for d in range(1, NZ)]
    yx = h * NX + x
    plane = []
    for d in range(1, 2 * NX):
        k = around(yx, d, 2 * NX)
        plane.append((k, at(lax.div(k, NX), lax.rem(k, NX), z)))
    g = h * HALF + x * NZ + z
    core = p + 1 - 2 * lax.rem(p, 2)
    opposite = around(p, 2, 4)
    both = around(core, 2, 4)
    parts = [(core, (g, core)), (opposite, (g, opposite)), (both, (g, both))]
    return at, zline, plane, parts


def lanes_of(p, feats):
    return pl.ds(pl.multiple_of(p * feats, 128), feats)


def gather_kernel(flags, wg, wu, wd, tok, og, ou, od, fx, fdy, close, *scratch):
    n = len(UNITS)
    zbuf, sbuf = scratch[:n], scratch[n : 2 * n]
    fbuf, fsend, tmid, rows, mine = scratch[2 * n : 2 * n + 5]
    ys, yr, zs, zr, xs, xr, own, fs, fr, gs, gr, ts, tr, tl, ms, mr, ml = scratch[2 * n + 5 :]
    p, h, x, z = place()
    at, zline, plane, parts = peers_of(p, h, x, z)
    over = at(1 - h, x, z)
    xline = [at(h, around(x, d, NX), z) for d in range(1, NX)]
    greet(zline + [q for _, q in plane] + [q for _, q in parts])
    weights = (wg, wu, wd)
    outs = (og, ou, od)
    sends, waits, local = [], [], []
    cross, near, later = {}, {}, {}

    def begin(u):
        w, c0, width = UNITS[u] if u < n else FLIP
        c = pl.ds(c0, width)
        if u < n:
            theirs = zbuf[u].at[:, h, rows16(z), :]
        else:
            theirs = fbuf.at[:, h, x]
        cross[u] = remote(
            weights[w].at[pl.ds(1 - h, 2), :, c], theirs, ys.at[u], yr.at[u], over
        )
        sends.append(cross[u])
        theirs[...] = weights[w][pl.ds(h, 2), :, c]

    def first(u):
        cross[u].wait_recv()
        v = zbuf[u].at[:, :, rows16(z), :]
        near[u] = [
            remote(v, v, zs.at[u, i], zr.at[u, i], zline[d % NZ - 1])
            for i, d in ((2, 2), (3, -2), (0, 1), (1, -1))
        ]
        sends.extend(near[u])

    def second(u):
        ahead, behind = near[u][:2]
        later[u] = near[u][2:]
        for i, (got, by) in enumerate(((ahead, 1), (behind, -1))):
            got.wait_recv()
            chunk = rows16(around(z, -2 * by, NZ))
            v = zbuf[u].at[:, :, chunk, :]
            a = remote(v, v, zs.at[u, 4 + i], zr.at[u, 4 + i], zline[by % NZ - 1])
            v = zbuf[u].at[:, i, chunk, :]
            b = remote(v, v, zs.at[u, 6 + i], zr.at[u, 6 + i], zline[2 * by % NZ - 1])
            later[u].extend([a, b])
            sends.extend([a, b])

    def spread(u):
        for c in later[u]:
            c.wait_recv()
        w, c0, width = UNITS[u]
        out = outs[w].at[:, x, :, pl.ds(c0, width)]
        for d in (2, 1, 3, 0):
            f = flags[h * HALF + around(x, d, NX) * NZ + z]
            sbuf[u][d] = zbuf[u][f]
            if d == 0:
                a = pltpu.make_async_copy(sbuf[u].at[0], out, own.at[u])
                a.start()
                local.append(a)
            else:
                a = remote(sbuf[u].at[d], out, xs.at[u, d], xr.at[u, d], xline[d - 1])
                sends.append(a)
                waits.append(a)

    def flip_first():
        cross[n].wait_recv()
        v = fbuf.at[:, :, x]
        near[n] = [remote(v, v, fs.at[d], fr.at[d], xline[d - 1]) for d in (2, 1, 3)]
        sends.extend(near[n])

    def flip_second():
        for c in near[n]:
            c.wait_recv()
        w, c0, width = FLIP
        out = outs[w].at[:, :, rows16(z), pl.ds(c0, width)]
        for d in (4, 3, 5, 2, 6, 1, 7, 0):
            f = flags[h * HALF + x * NZ + around(z, d, NZ)]
            fsend[d] = fbuf[f]
            if d == 0:
                a = pltpu.make_async_copy(fsend.at[0], out, own.at[n])
                a.start()
                local.append(a)
            else:
                a = remote(fsend.at[d], out, gs.at[d], gr.at[d], zline[d - 1])
                sends.append(a)
                waits.append(a)

    yx = h * NX + x
    stage = {}

    def tokens_z():
        stage["z"] = []
        for d in range(1, NZ):
            to = around(z, d, NZ)
            stage["z"].append(
                remote(tok.at[:, to], tmid.at[z], ts.at[d], tr.at[d], zline[d - 1])
            )
        a = pltpu.make_async_copy(tok.at[:, z], tmid.at[z], tl.at[0])
        a.start()
        stage["zl"] = a

    def tokens_plane():
        stage["zl"].wait()
        for c in stage["z"]:
            c.wait_recv()
        sends.extend(stage["z"])
        stage["p"] = []
        to = rows.at[pl.ds(yx * NZ, NZ)]
        for d in range(1, 2 * NX):
            k, peer = plane[d - 1]
            stage["p"].append(
                remote(tmid.at[:, k], to, ts.at[NZ + d], tr.at[NZ + d], peer)
            )
        a = pltpu.make_async_copy(tmid.at[:, yx], to, tl.at[1])
        a.start()
        stage["pl"] = a

    def compact():
        stage["pl"].wait()
        for c in stage["p"]:
            c.wait_recv()
        sends.extend(stage["p"])
        groups = rows.shape[0]
        spot = lax.broadcasted_iota(jnp.int32, (groups, SLOT, 128), 1)
        head = rows[:, :, 0:128].astype(F32)
        count = jnp.sum(jnp.where(spot == CAP, head, 0.0), axis=1)
        i = lax.broadcasted_iota(jnp.int32, (groups, groups), 0)
        j = lax.broadcasted_iota(jnp.int32, (groups, groups), 1)
        lower = jnp.where(i > j, 1.0, 0.0).astype(BF)
        before = jnp.dot(lower, count.astype(BF), preferred_element_type=F32)
        spot = spot.astype(F32)
        rank = jnp.where(spot < count[:, None, :], before[:, None, :] + spot, -1.0)
        rank = rank.reshape(groups * SLOT, 128)
        lane = lax.broadcasted_iota(jnp.int32, (groups * SLOT, 128), 1)
        for b in range(close.shape[1] // 128):
            hit = rank == (lane + b * 128).astype(F32)
            close[:, b * 128 : (b + 1) * 128] = jnp.where(hit, 1.0, 0.0).astype(BF)
        feats = rows.shape[2] // 2
        for b in range(2):
            part = rows[:, :, b * feats : (b + 1) * feats].reshape(groups * SLOT, feats)
            picked = lax.dot_general(
                close[...], part, (((0,), (0,)), ((), ())), preferred_element_type=F32
            )
            mine[b] = picked.astype(BF)
        here = lanes_of(p, feats)
        stage["m"] = []
        for b, full in enumerate((fx, fdy)):
            a = pltpu.make_async_copy(mine.at[b], full.at[:, here], ml.at[b])
            a.start()
            local.append(a)
            for i in (1, 0):
                a = remote(mine.at[b], full.at[:, here], ms.at[i, b], mr.at[i, b], parts[i][1])
                sends.append(a)
                stage["m"].append(a)

    def share():
        for c in stage["m"]:
            c.wait_recv()
        there = lanes_of(parts[1][0], fx.shape[1] // 4)
        for b, full in enumerate((fx, fdy)):
            view = full.at[:, there]
            a = remote(view, view, ms.at[2, b], mr.at[2, b], parts[0][1])
            sends.append(a)
            waits.append(a)

    for u in range(n + 1):
        begin(u)
    first(0)
    flip_first()
    second(0)
    first(1)
    tokens_z()
    spread(0)
    second(1)
    first(2)
    spread(1)
    second(2)
    flip_second()
    first(3)
    spread(2)
    tokens_plane()
    second(3)
    first(4)
    spread(3)
    second(4)
    first(5)
    compact()
    spread(4)
    second(5)
    share()
    spread(5)
    for c in waits:
        c.wait_recv()
    for c in sends:
        c.wait_send()
    for c in local:
        c.wait()


def gather_all(flags, wg, wu, wd, tok, rows, feats):
    cols = wg.shape[2]
    n = len(UNITS)
    vm = pl.BlockSpec(memory_space=pltpu.VMEM)
    hbm = pl.BlockSpec(memory_space=pl.ANY)
    dma = pltpu.SemaphoreType.DMA
    out = jax.ShapeDtypeStruct((2, NX, 16 * NZ, cols), BF)
    full = jax.ShapeDtypeStruct((rows, 4 * feats), BF)
    close = jax.ShapeDtypeStruct((2 * HALF * SLOT, rows), BF)
    return pl.pallas_call(
        gather_kernel,
        out_shape=(out, out, out, full, full, close),
        in_specs=[pl.BlockSpec(memory_space=pltpu.SMEM), vm, vm, vm, vm],
        out_specs=[hbm] * 5 + [vm],
        scratch_shapes=[pltpu.VMEM((2, 2, 16 * NZ, u[2]), BF) for u in UNITS]
        + [pltpu.VMEM((4, 2, 16 * NZ, u[2]), BF) for u in UNITS]
        + [
            pltpu.VMEM((2, 2, NX, 16, FLIP[2]), BF),
            pltpu.VMEM((NZ, 2, NX, 16, FLIP[2]), BF),
            pltpu.VMEM((NZ, 2 * NX, SLOT, 2 * feats), BF),
            pltpu.VMEM((2 * HALF, SLOT, 2 * feats), BF),
            pltpu.VMEM((2, rows, feats), BF),
            dma((n + 1,)),
            dma((n + 1,)),
            dma((n, 8)),
            dma((n, 8)),
            dma((n, 4)),
            dma((n, 4)),
            dma((n + 1,)),
            dma((4,)),
            dma((4,)),
            dma((8,)),
            dma((8,)),
            dma((16,)),
            dma((16,)),
            dma((2,)),
            dma((3, 2)),
            dma((3, 2)),
            dma((2,)),
        ],
        compiler_params=pltpu.CompilerParams(
            collective_id=0, has_side_effects=True, vmem_limit_bytes=48 * 1024 * 1024
        ),
        cost_estimate=pl.CostEstimate(flops=0, bytes_accessed=200_000_000, transcendentals=0),
        name="gather_all",
    )(flags, wg, wu, wd, tok.reshape(2 * NX, NZ, SLOT, 2 * feats))


def reduce_kernel(flags, gg, gu, gd, res, dx, close, og, ou, od, back, *scratch):
    n = len(UNITS)
    per = 10
    bufs = [scratch[per * u : per * u + per] for u in range(n)]
    ends = [b[7:] for b in bufs] + [scratch[per * n + 3 : per * n + 6]]
    fin, fsum, fgot = scratch[per * n : per * n + 3]
    pin, spread_rows, tmid = scratch[per * n + 6 : per * n + 9]
    ys, yr, zs, zr, xs, xr, own, fs, fr, gs, gr, ts, tr, tl, ms, mr, ml = scratch[per * n + 9 :]
    p, h, x, z = place()
    at, zline, plane, parts = peers_of(p, h, x, z)
    over = at(1 - h, x, z)
    xline = [at(h, around(x, d, NX), z) for d in range(1, NX)]
    greet(zline + [q for _, q in plane] + [q for _, q in parts])
    grads = (gg, gu, gd)
    outs = (og, ou, od)
    order = UNITS[::-1]
    sends = []
    arriving, stepping, cross, stage = {}, {}, {}, {}

    def spread(u):
        w, c0, width = order[u]
        g, c = grads[w], pl.ds(c0, width)
        rbuf = bufs[u][0]
        arriving[u] = []
        for d in (2, 1, 3):
            a = remote(
                g.at[:, around(x, d, NX), :, c],
                rbuf.at[d],
                xs.at[u, d],
                xr.at[u, d],
                xline[d - 1],
            )
            arriving[u].append(a)
            sends.append(a)
        a = pltpu.make_async_copy(g.at[:, x, :, c], rbuf.at[0], own.at[u])
        a.start()
        arriving[u].append(a)

    def arrive(u):
        for c in arriving[u][:3]:
            c.wait_recv()
        arriving[u][3].wait()

    def binned(terms, marks):
        low = high = None
        for v, m in zip(terms, marks):
            v = v.astype(F32)
            b = v * m
            a = v - b
            low = a if low is None else low + a
            high = b if high is None else high + b
        return low.astype(BF), high.astype(BF)

    xmarks = [
        flags[h * HALF + around(x, -d, NX) * NZ + z].astype(F32) for d in range(NX)
    ]

    def bins(u):
        rbuf, zsum = bufs[u][:2]

        def body(i, _):
            y = lax.div(i, NZ)
            r = rows16(lax.rem(i, NZ))
            low, high = binned([rbuf[k, y, r, :] for k in range(NX)], xmarks)
            zsum[0, y, r, :] = low
            zsum[1, y, r, :] = high
            return 0

        lax.fori_loop(0, 2 * NZ, body, 0)

    def first(u):
        zsum, dbuf, tbuf, hbuf = bufs[u][1:5]
        stepping[u] = []
        for i, by in enumerate((1, -1)):
            a = remote(
                zsum.at[:, :, rows16(around(z, 3 * by, NZ)), :],
                tbuf.at[i],
                zs.at[u, i],
                zr.at[u, i],
                zline[by % NZ - 1],
            )
            b = remote(
                zsum.at[:, i, rows16(around(z, 4, NZ)), :],
                hbuf.at[i],
                zs.at[u, 2 + i],
                zr.at[u, 2 + i],
                zline[2 * by % NZ - 1],
            )
            stepping[u].append((a, b))
            sends.extend([a, b])
        for i, by in enumerate((1, -1)):
            a = remote(
                zsum.at[:, :, rows16(around(z, by, NZ)), :],
                dbuf.at[i],
                zs.at[u, 4 + i],
                zr.at[u, 4 + i],
                zline[by % NZ - 1],
            )
            stepping[u].append(a)
            sends.append(a)

    def second(u):
        zsum, dbuf, tbuf, hbuf, obuf, ebuf = bufs[u][1:7]
        waits = stepping[u][2:]
        for i, by in enumerate((1, -1)):
            for c in stepping[u][i]:
                c.wait_recv()
            part = rows16(around(z, 2 * by, NZ))
            for y in range(2):
                v = zsum[:, y, part, :].astype(F32) + tbuf[i, :, y].astype(F32)
                if y == i:
                    v = v + hbuf[i].astype(F32)
                obuf[i, :, y] = v.astype(BF)
            a = remote(
                obuf.at[i], ebuf.at[i], zs.at[u, 6 + i], zr.at[u, 6 + i], zline[2 * by % NZ - 1]
            )
            waits.append(a)
            sends.append(a)
        stepping[u] = waits

    def swap(u):
        for c in stepping[u]:
            c.wait_recv()
        keep, ysend, yin = ends[u]

        def total(y):
            if u == n:
                v = fsum[:, y, x].astype(F32)
                for d in range(1, NX):
                    v = v + fgot[d, :, y].astype(F32)
                return v
            zsum, dbuf, ebuf = bufs[u][1], bufs[u][2], bufs[u][6]
            v = zsum[:, y, rows16(z), :].astype(F32)
            for b in (dbuf, ebuf):
                v = v + b[0, :, y].astype(F32) + b[1, :, y].astype(F32)
            return v

        ysend[...] = total(1 - h).astype(BF)
        cross[u] = remote(ysend, yin, ys.at[u], yr.at[u], over)
        sends.append(cross[u])
        keep[...] = total(h)

    def finish(u):
        w, c0, width = order[u] if u < n else FLIP
        c = pl.ds(c0, width)
        keep, ysend, yin = ends[u]
        cross[u].wait_recv()
        out = outs[w]
        out[2 * h, :, c] = keep[h]
        out[1, :, c] = keep[1 - h] + yin[h].astype(F32)
        out[2 - 2 * h, :, c] = yin[1 - h].astype(F32)

    def flip_spread():
        w, c0, width = FLIP
        g, c = grads[w], pl.ds(c0, width)
        arriving[n] = []
        for d in (4, 3, 5, 2, 6, 1, 7):
            a = remote(
                g.at[:, :, rows16(around(z, d, NZ)), c],
                fin.at[d],
                gs.at[d],
                gr.at[d],
                zline[d - 1],
            )
            arriving[n].append(a)
            sends.append(a)
        a = pltpu.make_async_copy(g.at[:, :, rows16(z), c], fin.at[0], own.at[n])
        a.start()
        arriving[n].append(a)

    def flip_second():
        for c in arriving[n][:-1]:
            c.wait_recv()
        arriving[n][-1].wait()
        marks = [flags[h * HALF + x * NZ + around(z, -d, NZ)].astype(F32) for d in range(NZ)]

        def body(i, _):
            y = lax.div(i, NX)
            k = lax.rem(i, NX)
            low, high = binned([fin[d, y, k] for d in range(NZ)], marks)
            fsum[0, y, k] = low
            fsum[1, y, k] = high
            return 0

        lax.fori_loop(0, 2 * NX, body, 0)
        stepping[n] = []
        for d in (2, 1, 3):
            a = remote(
                fsum.at[:, :, around(x, d, NX)], fgot.at[d], fs.at[d], fr.at[d], xline[d - 1]
            )
            stepping[n].append(a)
            sends.append(a)

    yx = h * NX + x
    feats = res.shape[1] // 4

    def sums_out():
        stage["m"] = []
        for i in (1, 2, 0):
            q, peer = parts[i]
            for b, v in enumerate((res, dx)):
                stage["m"].append(
                    remote(v.at[:, lanes_of(q, feats)], pin.at[i, b], ms.at[i, b], mr.at[i, b], peer)
                )
        here = lanes_of(p, feats)
        stage["ml"] = []
        for b, v in enumerate((res, dx)):
            a = pltpu.make_async_copy(v.at[:, here], pin.at[3, b], ml.at[b])
            a.start()
            stage["ml"].append(a)

    def widen():
        for c in stage["ml"]:
            c.wait()
        for c in stage["m"]:
            c.wait_recv()
        sends.extend(stage["m"])
        groups = spread_rows.shape[0]
        for b in range(2):
            v = pin[3, b].astype(F32)
            for i in range(3):
                v = v + pin[i, b].astype(F32)
            v = jnp.dot(close[...], v.astype(BF), preferred_element_type=F32).astype(BF)
            spread_rows[:, :, b * feats : (b + 1) * feats] = v.reshape(groups, SLOT, feats)
        stage["p"] = []
        for d in range(1, 2 * NX):
            k, peer = plane[d - 1]
            stage["p"].append(
                remote(
                    spread_rows.at[pl.ds(k * NZ, NZ)],
                    tmid.at[:, yx],
                    ts.at[NZ + d],
                    tr.at[NZ + d],
                    peer,
                )
            )
        a = pltpu.make_async_copy(spread_rows.at[pl.ds(yx * NZ, NZ)], tmid.at[:, yx], tl.at[0])
        a.start()
        stage["pl"] = a

    def homeward():
        stage["pl"].wait()
        for c in stage["p"]:
            c.wait_recv()
        sends.extend(stage["p"])
        stage["z"] = []
        for d in range(1, NZ):
            to = around(z, d, NZ)
            stage["z"].append(
                remote(tmid.at[to], back.at[:, z], ts.at[d], tr.at[d], zline[d - 1])
            )
        a = pltpu.make_async_copy(tmid.at[z], back.at[:, z], tl.at[1])
        a.start()
        stage["zl"] = a

    spread(0)
    sums_out()
    flip_spread()
    spread(1)
    for u in range(n):
        arrive(u)
        if u + 2 < n:
            spread(u + 2)
        bins(u)
        first(u)
        if u > 0:
            swap(u - 1)
        second(u)
        if u == 0:
            widen()
        elif u == 2:
            homeward()
            flip_second()
        elif u == 4:
            swap(n)
    swap(n - 1)
    for u in range(n + 1):
        finish((n + u) % (n + 1))
    stage["zl"].wait()
    for c in stage["z"]:
        c.wait_recv()
        c.wait_send()
    for c in sends:
        c.wait_send()


def reduce_all(flags, gg, gu, gd, res, dx, close):
    cols = gg.shape[1]
    rows = res.shape[0]
    feats = res.shape[1] // 4
    n = len(UNITS)
    shape = (2, NX, 16 * NZ, cols)
    vm = pl.BlockSpec(memory_space=pltpu.VMEM)
    hbm = pl.BlockSpec(memory_space=pl.ANY)
    dma = pltpu.SemaphoreType.DMA
    out = jax.ShapeDtypeStruct((3, 16, cols), F32)
    back = jax.ShapeDtypeStruct((2 * NX, NZ, SLOT, 2 * feats), BF)
    bufs = []
    for _, _, wide in UNITS[::-1]:
        bufs += [
            pltpu.VMEM((NX, 2, 16 * NZ, wide), BF),
            pltpu.VMEM((2, 2, 16 * NZ, wide), BF),
            pltpu.VMEM((2, 2, 2, 16, wide), BF),
            pltpu.VMEM((2, 2, 2, 16, wide), BF),
            pltpu.VMEM((2, 2, 16, wide), BF),
            pltpu.VMEM((2, 2, 2, 16, wide), BF),
            pltpu.VMEM((2, 2, 2, 16, wide), BF),
            pltpu.VMEM((2, 16, wide), F32),
            pltpu.VMEM((2, 16, wide), BF),
            pltpu.VMEM((2, 16, wide), BF),
        ]
    wide = FLIP[2]
    bufs += [
        pltpu.VMEM((NZ, 2, NX, 16, wide), BF),
        pltpu.VMEM((2, 2, NX, 16, wide), BF),
        pltpu.VMEM((NX, 2, 2, 16, wide), BF),
        pltpu.VMEM((2, 16, wide), F32),
        pltpu.VMEM((2, 16, wide), BF),
        pltpu.VMEM((2, 16, wide), BF),
    ]
    return pl.pallas_call(
        reduce_kernel,
        out_shape=(out, out, out, back),
        in_specs=[pl.BlockSpec(memory_space=pltpu.SMEM)] + [hbm] * 5 + [vm],
        out_specs=[vm] * 3 + [hbm],
        scratch_shapes=bufs
        + [
            pltpu.VMEM((4, 2, rows, feats), BF),
            pltpu.VMEM((2 * HALF, SLOT, 2 * feats), BF),
            pltpu.VMEM((NZ, 2 * NX, SLOT, 2 * feats), BF),
            dma((n + 1,)),
            dma((n + 1,)),
            dma((n, 8)),
            dma((n, 8)),
            dma((n, 4)),
            dma((n, 4)),
            dma((n + 1,)),
            dma((4,)),
            dma((4,)),
            dma((8,)),
            dma((8,)),
            dma((16,)),
            dma((16,)),
            dma((2,)),
            dma((3, 2)),
            dma((3, 2)),
            dma((2,)),
        ],
        compiler_params=pltpu.CompilerParams(
            collective_id=1, has_side_effects=True, vmem_limit_bytes=48 * 1024 * 1024
        ),
        cost_estimate=pl.CostEstimate(flops=0, bytes_accessed=200_000_000, transcendentals=0),
        name="reduce_all",
    )(flags, gg.reshape(shape), gu.reshape(shape), gd.reshape(shape), res, dx, close)


def project_rows(x, dy, wg, wu, wd):
    gate = jnp.dot(x, wg, preferred_element_type=F32)
    up = jnp.dot(x, wu, preferred_element_type=F32)
    sig = jax.nn.sigmoid(gate)
    silu = gate * sig
    hidden = (silu * up).astype(BF)
    out = lax.dot_general(hidden, wd, (((1,), (1,)), ((), ())), preferred_element_type=F32)
    dhidden = jnp.dot(dy, wd, preferred_element_type=F32)
    dgate = (dhidden * up * sig * (1.0 + gate * (1.0 - sig))).astype(BF)
    dup = (dhidden * silu).astype(BF)
    dx = lax.dot_general(dgate, wg, (((1,), (1,)), ((), ())), preferred_element_type=F32)
    dx = dx + lax.dot_general(dup, wu, (((1,), (1,)), ((), ())), preferred_element_type=F32)
    over_rows = (((0,), (0,)), ((), ()))
    grad_g = lax.dot_general(x, dgate, over_rows, preferred_element_type=F32).astype(BF)
    grad_u = lax.dot_general(x, dup, over_rows, preferred_element_type=F32).astype(BF)
    grad_d = lax.dot_general(dy, hidden, over_rows, preferred_element_type=F32).astype(BF)
    return out, dx, grad_g, grad_u, grad_d


def shards(tokens, cotangent, tags, counts, target, gate_weight, up_weight, down_weight):
    groups = lax.axis_size("group")
    rows, feats = tokens.shape
    total = rows * groups
    start_b = groups * counts[0] // total
    start_c = groups * (counts[0] + counts[1]) // total
    devices = jnp.arange(groups, dtype=jnp.int32)
    device_mod = (devices >= start_b).astype(jnp.int32) + (devices >= start_c).astype(jnp.int32)
    flags = device_mod - devices // HALF
    base = jnp.where(tags == 0, 0, jnp.where(tags == 1, start_b, start_c))
    dest = base + target
    onehot = (dest[:, None] == devices[None, :]).astype(BF)
    places = jnp.arange(rows, dtype=jnp.int32)
    lower = (places[:, None] > places[None, :]).astype(BF)
    earlier = jnp.dot(lower, onehot, preferred_element_type=F32)
    slot = jnp.sum(earlier * onehot.astype(F32), axis=1).astype(jnp.int32)
    sent = jnp.sum(onehot.astype(F32), axis=0)
    position = dest * SLOT + slot
    wide = groups * SLOT
    lanes = jnp.arange(wide, dtype=jnp.int32)
    both = jnp.concatenate([tokens, cotangent], axis=1)
    into = (lanes[:, None] == position[None, :]).astype(BF)
    send = jnp.dot(into, both, preferred_element_type=F32).reshape(groups, SLOT, 2 * feats)
    tail = (jnp.arange(SLOT, dtype=jnp.int32) >= CAP)[None, :, None]
    send = jnp.where(tail, sent[:, None, None], send).astype(BF).reshape(wide, 2 * feats)
    w_gate, w_up, w_down, full_x, full_dy, close = gather_all(
        flags, gate_weight, up_weight, down_weight, send, rows, feats
    )
    depth = full_x.shape[1]
    w_gate, w_up, w_down = (w.reshape(depth, -1) for w in (w_gate, w_up, w_down))
    out, dx, grad_g, grad_u, grad_d = project_rows(full_x, full_dy, w_gate, w_up, w_down)
    gate_grad, up_grad, down_grad, back = reduce_all(
        flags, grad_g, grad_u, grad_d, out.astype(BF), dx.astype(BF), close
    )
    out_of = (position[:, None] == lanes[None, :]).astype(BF)
    result = jnp.dot(out_of, back.reshape(wide, 2 * feats), preferred_element_type=F32).astype(BF)
    return result[:, :feats], result[:, feats:], gate_grad, up_grad, down_grad


def solution(mesh):
    in_specs = (
        P("group", "mp"),
        P("group", "mp"),
        P("group"),
        P(),
        P("group"),
        P(None, "group", "mp"),
        P(None, "group", "mp"),
        P(None, "group", "mp"),
    )
    out_specs = (
        P("group", "mp"),
        P("group", "mp"),
        P(None, "group", "mp"),
        P(None, "group", "mp"),
        P(None, "group", "mp"),
    )
    return jax.shard_map(shards, mesh=mesh, in_specs=in_specs, out_specs=out_specs, check_vma=False)
```

```python
import jax
import jax.numpy as jnp
from jax import lax
from jax.experimental import pallas as pl
from jax.experimental.pallas import tpu as pltpu
from jax.sharding import PartitionSpec as P

BF = jnp.bfloat16
F32 = jnp.float32
NX, NZ = 4, 8
HALF = NX * NZ
CAP = 12
SLOT = 16
UNITS = (
    (0, 0, 256),
    (0, 256, 384),
    (0, 640, 384),
    (1, 0, 512),
    (1, 512, 512),
    (2, 0, 640),
)
FLIP = (2, 640, 384)


def place():
    g = lax.axis_index("group")
    p = lax.axis_index("mp")
    h = lax.div(g, HALF)
    x = lax.rem(lax.div(g, NZ), NX)
    z = lax.rem(g, NZ)
    return p, h, x, z


def around(v, by, size):
    return lax.rem(v + (by + size), size)


def rows16(c):
    return pl.ds(pl.multiple_of(c * 16, 16), 16)


def greet(peers):
    barrier = pltpu.get_barrier_semaphore()
    for peer in peers:
        pl.semaphore_signal(barrier, inc=1, device_id=peer, device_id_type=pl.DeviceIdType.MESH)
    pl.semaphore_wait(barrier, len(peers))


def remote(src, dst, send, recv, peer):
    copy = pltpu.make_async_remote_copy(
        src_ref=src,
        dst_ref=dst,
        send_sem=send,
        recv_sem=recv,
        device_id=peer,
        device_id_type=pl.DeviceIdType.MESH,
    )
    copy.start()
    return copy


def peers_of(p, h, x, z):
    def at(hh, xx, zz):
        return (hh * HALF + xx * NZ + zz, p)

    zline = [at(h, x, around(z, d, NZ)) for d in range(1, NZ)]
    yx = h * NX + x
    plane = []
    for d in range(1, 2 * NX):
        k = around(yx, d, 2 * NX)
        plane.append((k, at(lax.div(k, NX), lax.rem(k, NX), z)))
    g = h * HALF + x * NZ + z
    core = p + 1 - 2 * lax.rem(p, 2)
    opposite = around(p, 2, 4)
    both = around(core, 2, 4)
    parts = [(core, (g, core)), (opposite, (g, opposite)), (both, (g, both))]
    return at, zline, plane, parts


def lanes_of(p, feats):
    return pl.ds(pl.multiple_of(p * feats, 128), feats)


def gather_kernel(flags, wg, wu, wd, tok, og, ou, od, fx, fdy, close, *scratch):
    n = len(UNITS)
    zbuf, sbuf = scratch[:n], scratch[n : 2 * n]
    fbuf, fsend, tmid, rows, mine = scratch[2 * n : 2 * n + 5]
    ys, yr, zs, zr, xs, xr, own, fs, fr, gs, gr, ts, tr, tl, ms, mr, ml = scratch[2 * n + 5 :]
    p, h, x, z = place()
    at, zline, plane, parts = peers_of(p, h, x, z)
    over = at(1 - h, x, z)
    xline = [at(h, around(x, d, NX), z) for d in range(1, NX)]
    greet(zline + [q for _, q in plane] + [q for _, q in parts])
    weights = (wg, wu, wd)
    outs = (og, ou, od)
    sends, waits, local = [], [], []
    cross, near, later = {}, {}, {}

    def begin(u):
        w, c0, width = UNITS[u] if u < n else FLIP
        c = pl.ds(c0, width)
        if u < n:
            theirs = zbuf[u].at[:, h, rows16(z), :]
        else:
            theirs = fbuf.at[:, h, x]
        cross[u] = remote(
            weights[w].at[pl.ds(1 - h, 2), :, c], theirs, ys.at[u], yr.at[u], over
        )
        sends.append(cross[u])
        theirs[...] = weights[w][pl.ds(h, 2), :, c]

    def first(u):
        cross[u].wait_recv()
        v = zbuf[u].at[:, :, rows16(z), :]
        hops = ((2, 2), (3, -2), (0, 1), (1, -1))
        near[u] = {
            i: remote(v, v, zs.at[u, i], zr.at[u, i], zline[d % NZ - 1]) for i, d in hops
        }
        sends.extend(near[u].values())

    def second(u):
        later[u] = [near[u][0], near[u][1]]
        for i, by in enumerate((1, -1)):
            near[u][2 + i].wait_recv()
            chunk = rows16(around(z, -2 * by, NZ))
            v = zbuf[u].at[:, :, chunk, :]
            a = remote(v, v, zs.at[u, 4 + i], zr.at[u, 4 + i], zline[by % NZ - 1])
            v = zbuf[u].at[:, i, chunk, :]
            b = remote(v, v, zs.at[u, 6 + i], zr.at[u, 6 + i], zline[2 * by % NZ - 1])
            later[u].extend([a, b])
            sends.extend([a, b])

    def spread(u):
        for c in later[u]:
            c.wait_recv()
        w, c0, width = UNITS[u]
        out = outs[w].at[:, x, :, pl.ds(c0, width)]
        for d in (2, 1, 3, 0):
            f = flags[h * HALF + around(x, d, NX) * NZ + z]
            sbuf[u][d] = zbuf[u][f]
            if d == 0:
                a = pltpu.make_async_copy(sbuf[u].at[0], out, own.at[u])
                a.start()
                local.append(a)
            else:
                a = remote(sbuf[u].at[d], out, xs.at[u, d], xr.at[u, d], xline[d - 1])
                sends.append(a)
                waits.append(a)

    def flip_first():
        cross[n].wait_recv()
        v = fbuf.at[:, :, x]
        near[n] = [remote(v, v, fs.at[d], fr.at[d], xline[d - 1]) for d in (2, 1, 3)]
        sends.extend(near[n])

    def flip_second():
        for c in near[n]:
            c.wait_recv()
        w, c0, width = FLIP
        out = outs[w].at[:, :, rows16(z), pl.ds(c0, width)]
        for d in (4, 3, 5, 2, 6, 1, 7, 0):
            f = flags[h * HALF + x * NZ + around(z, d, NZ)]
            fsend[d] = fbuf[f]
            if d == 0:
                a = pltpu.make_async_copy(fsend.at[0], out, own.at[n])
                a.start()
                local.append(a)
            else:
                a = remote(fsend.at[d], out, gs.at[d], gr.at[d], zline[d - 1])
                sends.append(a)
                waits.append(a)

    yx = h * NX + x
    stage = {}

    def tokens_plane():
        stage["p"] = []
        for d in range(1, 2 * NX):
            k, peer = plane[d - 1]
            stage["p"].append(
                remote(tok.at[k], tmid.at[yx], ts.at[NZ + d], tr.at[NZ + d], peer)
            )
        sends.extend(stage["p"])
        a = pltpu.make_async_copy(tok.at[yx], tmid.at[yx], tl.at[1])
        a.start()
        stage["pl"] = a

    def tokens_z():
        stage["pl"].wait()
        for c in stage["p"]:
            c.wait_recv()
        stage["z"] = []
        for d in (4, 3, 5, 2, 6, 1, 7):
            to = around(z, d, NZ)
            stage["z"].append(
                remote(tmid.at[:, to], rows.at[:, z], ts.at[d], tr.at[d], zline[d - 1])
            )
        sends.extend(stage["z"])
        a = pltpu.make_async_copy(tmid.at[:, z], rows.at[:, z], tl.at[0])
        a.start()
        stage["zl"] = a

    def compact():
        stage["zl"].wait()
        for c in stage["z"]:
            c.wait_recv()
        groups = 2 * HALF
        spot = lax.broadcasted_iota(jnp.int32, (groups, SLOT, 128), 1)
        head = rows[:, :, :, 0:128].reshape(groups, SLOT, 128).astype(F32)
        count = jnp.sum(jnp.where(spot == CAP, head, 0.0), axis=1)
        i = lax.broadcasted_iota(jnp.int32, (groups, groups), 0)
        j = lax.broadcasted_iota(jnp.int32, (groups, groups), 1)
        lower = jnp.where(i > j, 1.0, 0.0).astype(BF)
        before = jnp.dot(lower, count.astype(BF), preferred_element_type=F32)
        spot = spot.astype(F32)
        rank = jnp.where(spot < count[:, None, :], before[:, None, :] + spot, -1.0)
        rank = rank.reshape(groups * SLOT, 128)
        lane = lax.broadcasted_iota(jnp.int32, (groups * SLOT, 128), 1)
        for b in range(close.shape[1] // 128):
            hit = rank == (lane + b * 128).astype(F32)
            close[:, b * 128 : (b + 1) * 128] = jnp.where(hit, 1.0, 0.0).astype(BF)
        feats = rows.shape[3] // 2
        for b in range(2):
            part = rows[:, :, :, b * feats : (b + 1) * feats].reshape(groups * SLOT, feats)
            picked = lax.dot_general(
                close[...], part, (((0,), (0,)), ((), ())), preferred_element_type=F32
            )
            mine[b] = picked.astype(BF)
        here = lanes_of(p, feats)
        stage["m"] = []
        for b, full in enumerate((fx, fdy)):
            a = pltpu.make_async_copy(mine.at[b], full.at[:, here], ml.at[b])
            a.start()
            local.append(a)
            for i in (1, 0):
                a = remote(mine.at[b], full.at[:, here], ms.at[i, b], mr.at[i, b], parts[i][1])
                sends.append(a)
                stage["m"].append(a)

    def share():
        for c in stage["m"]:
            c.wait_recv()
        there = lanes_of(parts[1][0], fx.shape[1] // 4)
        for b, full in enumerate((fx, fdy)):
            view = full.at[:, there]
            a = remote(view, view, ms.at[2, b], mr.at[2, b], parts[0][1])
            sends.append(a)
            waits.append(a)

    for u in range(n + 1):
        begin(u)
    tokens_plane()
    first(0)
    flip_first()
    second(0)
    first(1)
    spread(0)
    second(1)
    first(2)
    tokens_z()
    spread(1)
    second(2)
    first(3)
    spread(2)
    second(3)
    first(4)
    spread(3)
    second(4)
    first(5)
    compact()
    spread(4)
    second(5)
    flip_second()
    spread(5)
    share()
    for c in waits:
        c.wait_recv()
    for c in sends:
        c.wait_send()
    for c in local:
        c.wait()


def gather_all(flags, wg, wu, wd, tok, rows, feats):
    cols = wg.shape[2]
    n = len(UNITS)
    vm = pl.BlockSpec(memory_space=pltpu.VMEM)
    hbm = pl.BlockSpec(memory_space=pl.ANY)
    dma = pltpu.SemaphoreType.DMA
    out = jax.ShapeDtypeStruct((2, NX, 16 * NZ, cols), BF)
    full = jax.ShapeDtypeStruct((rows, 4 * feats), BF)
    close = jax.ShapeDtypeStruct((2 * HALF * SLOT, rows), BF)
    return pl.pallas_call(
        gather_kernel,
        out_shape=(out, out, out, full, full, close),
        in_specs=[pl.BlockSpec(memory_space=pltpu.SMEM), vm, vm, vm, vm],
        out_specs=[hbm] * 5 + [vm],
        scratch_shapes=[pltpu.VMEM((2, 2, 16 * NZ, u[2]), BF) for u in UNITS]
        + [pltpu.VMEM((4, 2, 16 * NZ, u[2]), BF) for u in UNITS]
        + [
            pltpu.VMEM((2, 2, NX, 16, FLIP[2]), BF),
            pltpu.VMEM((NZ, 2, NX, 16, FLIP[2]), BF),
            pltpu.VMEM((2 * NX, NZ, SLOT, 2 * feats), BF),
            pltpu.VMEM((2 * NX, NZ, SLOT, 2 * feats), BF),
            pltpu.VMEM((2, rows, feats), BF),
            dma((n + 1,)),
            dma((n + 1,)),
            dma((n, 8)),
            dma((n, 8)),
            dma((n, 4)),
            dma((n, 4)),
            dma((n + 1,)),
            dma((4,)),
            dma((4,)),
            dma((8,)),
            dma((8,)),
            dma((16,)),
            dma((16,)),
            dma((2,)),
            dma((3, 2)),
            dma((3, 2)),
            dma((2,)),
        ],
        compiler_params=pltpu.CompilerParams(
            collective_id=0, has_side_effects=True, vmem_limit_bytes=48 * 1024 * 1024
        ),
        cost_estimate=pl.CostEstimate(flops=0, bytes_accessed=200_000_000, transcendentals=0),
        name="gather_all",
    )(flags, wg, wu, wd, tok.reshape(2 * NX, NZ, SLOT, 2 * feats))


def reduce_kernel(flags, gg, gu, gd, res, dx, close, og, ou, od, back, *scratch):
    n = len(UNITS)
    per = 10
    bufs = [scratch[per * u : per * u + per] for u in range(n)]
    ends = [b[7:] for b in bufs] + [scratch[per * n + 3 : per * n + 6]]
    fin, fsum, fgot = scratch[per * n : per * n + 3]
    pin, spread_rows, tmid = scratch[per * n + 6 : per * n + 9]
    ys, yr, zs, zr, xs, xr, own, fs, fr, gs, gr, ts, tr, tl, ms, mr, ml = scratch[per * n + 9 :]
    p, h, x, z = place()
    at, zline, plane, parts = peers_of(p, h, x, z)
    over = at(1 - h, x, z)
    xline = [at(h, around(x, d, NX), z) for d in range(1, NX)]
    greet(zline + [q for _, q in plane] + [q for _, q in parts])
    grads = (gg, gu, gd)
    outs = (og, ou, od)
    order = UNITS[::-1]
    sends = []
    arriving, stepping, cross, stage = {}, {}, {}, {}

    def spread(u):
        w, c0, width = order[u]
        g, c = grads[w], pl.ds(c0, width)
        rbuf = bufs[u][0]
        arriving[u] = []
        for d in (2, 1, 3):
            a = remote(
                g.at[:, around(x, d, NX), :, c],
                rbuf.at[d],
                xs.at[u, d],
                xr.at[u, d],
                xline[d - 1],
            )
            arriving[u].append(a)
            sends.append(a)
        a = pltpu.make_async_copy(g.at[:, x, :, c], rbuf.at[0], own.at[u])
        a.start()
        arriving[u].append(a)

    def arrive(u):
        for c in arriving[u][:3]:
            c.wait_recv()
        arriving[u][3].wait()

    def binned(terms, marks):
        low = high = None
        for v, m in zip(terms, marks):
            v = v.astype(F32)
            b = v * m
            a = v - b
            low = a if low is None else low + a
            high = b if high is None else high + b
        return low.astype(BF), high.astype(BF)

    xmarks = [
        flags[h * HALF + around(x, -d, NX) * NZ + z].astype(F32) for d in range(NX)
    ]

    def bins(u):
        rbuf, zsum = bufs[u][:2]

        def body(i, _):
            y = lax.div(i, NZ)
            r = rows16(lax.rem(i, NZ))
            low, high = binned([rbuf[k, y, r, :] for k in range(NX)], xmarks)
            zsum[0, y, r, :] = low
            zsum[1, y, r, :] = high
            return 0

        lax.fori_loop(0, 2 * NZ, body, 0)

    def first(u):
        zsum, dbuf, tbuf, hbuf = bufs[u][1:5]
        stepping[u] = []
        for i, by in enumerate((1, -1)):
            a = remote(
                zsum.at[:, :, rows16(around(z, 3 * by, NZ)), :],
                tbuf.at[i],
                zs.at[u, i],
                zr.at[u, i],
                zline[by % NZ - 1],
            )
            b = remote(
                zsum.at[:, i, rows16(around(z, 4, NZ)), :],
                hbuf.at[i],
                zs.at[u, 2 + i],
                zr.at[u, 2 + i],
                zline[2 * by % NZ - 1],
            )
            stepping[u].append((a, b))
            sends.extend([a, b])
        for i, by in enumerate((1, -1)):
            a = remote(
                zsum.at[:, :, rows16(around(z, by, NZ)), :],
                dbuf.at[i],
                zs.at[u, 4 + i],
                zr.at[u, 4 + i],
                zline[by % NZ - 1],
            )
            stepping[u].append(a)
            sends.append(a)

    def second(u):
        zsum, dbuf, tbuf, hbuf, obuf, ebuf = bufs[u][1:7]
        waits = stepping[u][2:]
        for i, by in enumerate((1, -1)):
            for c in stepping[u][i]:
                c.wait_recv()
            part = rows16(around(z, 2 * by, NZ))
            for y in range(2):
                v = zsum[:, y, part, :].astype(F32) + tbuf[i, :, y].astype(F32)
                if y == i:
                    v = v + hbuf[i].astype(F32)
                obuf[i, :, y] = v.astype(BF)
            a = remote(
                obuf.at[i], ebuf.at[i], zs.at[u, 6 + i], zr.at[u, 6 + i], zline[2 * by % NZ - 1]
            )
            waits.append(a)
            sends.append(a)
        stepping[u] = waits

    def swap(u):
        for c in stepping[u]:
            c.wait_recv()
        keep, ysend, yin = ends[u]

        def total(y):
            if u == n:
                v = fsum[:, y, x].astype(F32)
                for d in range(1, NX):
                    v = v + fgot[d, :, y].astype(F32)
                return v
            zsum, dbuf, ebuf = bufs[u][1], bufs[u][2], bufs[u][6]
            v = zsum[:, y, rows16(z), :].astype(F32)
            for b in (dbuf, ebuf):
                v = v + b[0, :, y].astype(F32) + b[1, :, y].astype(F32)
            return v

        ysend[...] = total(1 - h).astype(BF)
        cross[u] = remote(ysend, yin, ys.at[u], yr.at[u], over)
        sends.append(cross[u])
        keep[...] = total(h)

    def finish(u):
        w, c0, width = order[u] if u < n else FLIP
        c = pl.ds(c0, width)
        keep, ysend, yin = ends[u]
        cross[u].wait_recv()
        out = outs[w]
        out[2 * h, :, c] = keep[h]
        out[1, :, c] = keep[1 - h] + yin[h].astype(F32)
        out[2 - 2 * h, :, c] = yin[1 - h].astype(F32)

    def flip_spread():
        w, c0, width = FLIP
        g, c = grads[w], pl.ds(c0, width)
        arriving[n] = []
        for d in (4, 3, 5, 2, 6, 1, 7):
            a = remote(
                g.at[:, :, rows16(around(z, d, NZ)), c],
                fin.at[d],
                gs.at[d],
                gr.at[d],
                zline[d - 1],
            )
            arriving[n].append(a)
            sends.append(a)
        a = pltpu.make_async_copy(g.at[:, :, rows16(z), c], fin.at[0], own.at[n])
        a.start()
        arriving[n].append(a)

    def flip_second():
        for c in arriving[n][:-1]:
            c.wait_recv()
        arriving[n][-1].wait()
        marks = [flags[h * HALF + x * NZ + around(z, -d, NZ)].astype(F32) for d in range(NZ)]

        def body(i, _):
            y = lax.div(i, NX)
            k = lax.rem(i, NX)
            low, high = binned([fin[d, y, k] for d in range(NZ)], marks)
            fsum[0, y, k] = low
            fsum[1, y, k] = high
            return 0

        lax.fori_loop(0, 2 * NX, body, 0)
        stepping[n] = []
        for d in (2, 1, 3):
            a = remote(
                fsum.at[:, :, around(x, d, NX)], fgot.at[d], fs.at[d], fr.at[d], xline[d - 1]
            )
            stepping[n].append(a)
            sends.append(a)

    yx = h * NX + x
    feats = res.shape[1] // 4

    def sums_out():
        stage["m"] = []
        for i in (1, 2, 0):
            q, peer = parts[i]
            for b, v in enumerate((res, dx)):
                stage["m"].append(
                    remote(v.at[:, lanes_of(q, feats)], pin.at[i, b], ms.at[i, b], mr.at[i, b], peer)
                )
        here = lanes_of(p, feats)
        stage["ml"] = []
        for b, v in enumerate((res, dx)):
            a = pltpu.make_async_copy(v.at[:, here], pin.at[3, b], ml.at[b])
            a.start()
            stage["ml"].append(a)

    def widen():
        for c in stage["ml"]:
            c.wait()
        for c in stage["m"]:
            c.wait_recv()
        sends.extend(stage["m"])
        for b in range(2):
            v = pin[3, b].astype(F32)
            for i in range(3):
                v = v + pin[i, b].astype(F32)
            v = jnp.dot(close[...], v.astype(BF), preferred_element_type=F32).astype(BF)
            spread_rows[:, :, :, b * feats : (b + 1) * feats] = v.reshape(
                2 * NX, NZ, SLOT, feats
            )
        stage["z"] = []
        for d in (4, 3, 5, 2, 6, 1, 7):
            stage["z"].append(
                remote(
                    spread_rows.at[:, around(z, d, NZ)],
                    tmid.at[z],
                    ts.at[d],
                    tr.at[d],
                    zline[d - 1],
                )
            )
        sends.extend(stage["z"])
        a = pltpu.make_async_copy(spread_rows.at[:, z], tmid.at[z], tl.at[0])
        a.start()
        stage["zl"] = a

    def homeward():
        stage["zl"].wait()
        for c in stage["z"]:
            c.wait_recv()
        stage["p"] = []
        for d in range(1, 2 * NX):
            k, peer = plane[d - 1]
            stage["p"].append(
                remote(tmid.at[:, k], back.at[yx], ts.at[NZ + d], tr.at[NZ + d], peer)
            )
        sends.extend(stage["p"])
        a = pltpu.make_async_copy(tmid.at[:, yx], back.at[yx], tl.at[1])
        a.start()
        stage["pl"] = a

    sums_out()
    spread(0)
    flip_spread()
    spread(1)
    spread(2)
    spread(3)
    spread(4)
    spread(5)
    arrive(0)
    bins(0)
    first(0)
    widen()
    second(0)
    arrive(1)
    bins(1)
    first(1)
    swap(0)
    second(1)
    arrive(2)
    bins(2)
    first(2)
    swap(1)
    second(2)
    homeward()
    flip_second()
    arrive(3)
    bins(3)
    first(3)
    swap(2)
    second(3)
    arrive(4)
    bins(4)
    first(4)
    swap(3)
    second(4)
    swap(n)
    arrive(5)
    bins(5)
    first(5)
    swap(4)
    second(5)
    swap(n - 1)
    for u in range(n + 1):
        finish((n + u) % (n + 1))
    stage["pl"].wait()
    for c in stage["p"]:
        c.wait_recv()
    for c in sends:
        c.wait_send()


def reduce_all(flags, gg, gu, gd, res, dx, close):
    cols = gg.shape[1]
    rows = res.shape[0]
    feats = res.shape[1] // 4
    n = len(UNITS)
    shape = (2, NX, 16 * NZ, cols)
    vm = pl.BlockSpec(memory_space=pltpu.VMEM)
    hbm = pl.BlockSpec(memory_space=pl.ANY)
    dma = pltpu.SemaphoreType.DMA
    out = jax.ShapeDtypeStruct((3, 16, cols), F32)
    back = jax.ShapeDtypeStruct((2 * NX, NZ, SLOT, 2 * feats), BF)
    bufs = []
    for _, _, wide in UNITS[::-1]:
        bufs += [
            pltpu.VMEM((NX, 2, 16 * NZ, wide), BF),
            pltpu.VMEM((2, 2, 16 * NZ, wide), BF),
            pltpu.VMEM((2, 2, 2, 16, wide), BF),
            pltpu.VMEM((2, 2, 2, 16, wide), BF),
            pltpu.VMEM((2, 2, 16, wide), BF),
            pltpu.VMEM((2, 2, 2, 16, wide), BF),
            pltpu.VMEM((2, 2, 2, 16, wide), BF),
            pltpu.VMEM((2, 16, wide), F32),
            pltpu.VMEM((2, 16, wide), BF),
            pltpu.VMEM((2, 16, wide), BF),
        ]
    wide = FLIP[2]
    bufs += [
        pltpu.VMEM((NZ, 2, NX, 16, wide), BF),
        pltpu.VMEM((2, 2, NX, 16, wide), BF),
        pltpu.VMEM((NX, 2, 2, 16, wide), BF),
        pltpu.VMEM((2, 16, wide), F32),
        pltpu.VMEM((2, 16, wide), BF),
        pltpu.VMEM((2, 16, wide), BF),
    ]
    return pl.pallas_call(
        reduce_kernel,
        out_shape=(out, out, out, back),
        in_specs=[pl.BlockSpec(memory_space=pltpu.SMEM)] + [hbm] * 5 + [vm],
        out_specs=[vm] * 3 + [hbm],
        scratch_shapes=bufs
        + [
            pltpu.VMEM((4, 2, rows, feats), BF),
            pltpu.VMEM((2 * NX, NZ, SLOT, 2 * feats), BF),
            pltpu.VMEM((NZ, 2 * NX, SLOT, 2 * feats), BF),
            dma((n + 1,)),
            dma((n + 1,)),
            dma((n, 8)),
            dma((n, 8)),
            dma((n, 4)),
            dma((n, 4)),
            dma((n + 1,)),
            dma((4,)),
            dma((4,)),
            dma((8,)),
            dma((8,)),
            dma((16,)),
            dma((16,)),
            dma((2,)),
            dma((3, 2)),
            dma((3, 2)),
            dma((2,)),
        ],
        compiler_params=pltpu.CompilerParams(
            collective_id=1, has_side_effects=True, vmem_limit_bytes=48 * 1024 * 1024
        ),
        cost_estimate=pl.CostEstimate(flops=0, bytes_accessed=200_000_000, transcendentals=0),
        name="reduce_all",
    )(flags, gg.reshape(shape), gu.reshape(shape), gd.reshape(shape), res, dx, close)


def project_rows(x, dy, wg, wu, wd):
    gate = jnp.dot(x, wg, preferred_element_type=F32)
    up = jnp.dot(x, wu, preferred_element_type=F32)
    sig = jax.nn.sigmoid(gate)
    silu = gate * sig
    hidden = (silu * up).astype(BF)
    out = lax.dot_general(hidden, wd, (((1,), (1,)), ((), ())), preferred_element_type=F32)
    dhidden = jnp.dot(dy, wd, preferred_element_type=F32)
    dgate = (dhidden * up * sig * (1.0 + gate * (1.0 - sig))).astype(BF)
    dup = (dhidden * silu).astype(BF)
    dx = lax.dot_general(dgate, wg, (((1,), (1,)), ((), ())), preferred_element_type=F32)
    dx = dx + lax.dot_general(dup, wu, (((1,), (1,)), ((), ())), preferred_element_type=F32)
    over_rows = (((0,), (0,)), ((), ()))
    grad_g = lax.dot_general(x, dgate, over_rows, preferred_element_type=F32).astype(BF)
    grad_u = lax.dot_general(x, dup, over_rows, preferred_element_type=F32).astype(BF)
    grad_d = lax.dot_general(dy, hidden, over_rows, preferred_element_type=F32).astype(BF)
    return out, dx, grad_g, grad_u, grad_d


def shards(tokens, cotangent, tags, counts, target, gate_weight, up_weight, down_weight):
    groups = lax.axis_size("group")
    rows, feats = tokens.shape
    total = rows * groups
    start_b = groups * counts[0] // total
    start_c = groups * (counts[0] + counts[1]) // total
    devices = jnp.arange(groups, dtype=jnp.int32)
    device_mod = (devices >= start_b).astype(jnp.int32) + (devices >= start_c).astype(jnp.int32)
    flags = device_mod - devices // HALF
    base = jnp.where(tags == 0, 0, jnp.where(tags == 1, start_b, start_c))
    dest = base + target
    onehot = (dest[:, None] == devices[None, :]).astype(BF)
    places = jnp.arange(rows, dtype=jnp.int32)
    lower = (places[:, None] > places[None, :]).astype(BF)
    earlier = jnp.dot(lower, onehot, preferred_element_type=F32)
    slot = jnp.sum(earlier * onehot.astype(F32), axis=1).astype(jnp.int32)
    sent = jnp.sum(onehot.astype(F32), axis=0)
    position = dest * SLOT + slot
    wide = groups * SLOT
    lanes = jnp.arange(wide, dtype=jnp.int32)
    both = jnp.concatenate([tokens, cotangent], axis=1)
    into = (lanes[:, None] == position[None, :]).astype(BF)
    send = jnp.dot(into, both, preferred_element_type=F32).reshape(groups, SLOT, 2 * feats)
    tail = (jnp.arange(SLOT, dtype=jnp.int32) >= CAP)[None, :, None]
    send = jnp.where(tail, sent[:, None, None], send).astype(BF).reshape(wide, 2 * feats)
    w_gate, w_up, w_down, full_x, full_dy, close = gather_all(
        flags, gate_weight, up_weight, down_weight, send, rows, feats
    )
    depth = full_x.shape[1]
    w_gate, w_up, w_down = (w.reshape(depth, -1) for w in (w_gate, w_up, w_down))
    out, dx, grad_g, grad_u, grad_d = project_rows(full_x, full_dy, w_gate, w_up, w_down)
    gate_grad, up_grad, down_grad, back = reduce_all(
        flags, grad_g, grad_u, grad_d, out.astype(BF), dx.astype(BF), close
    )
    out_of = (position[:, None] == lanes[None, :]).astype(BF)
    result = jnp.dot(out_of, back.reshape(wide, 2 * feats), preferred_element_type=F32).astype(BF)
    return result[:, :feats], result[:, feats:], gate_grad, up_grad, down_grad


def solution(mesh):
    in_specs = (
        P("group", "mp"),
        P("group", "mp"),
        P("group"),
        P(),
        P("group"),
        P(None, "group", "mp"),
        P(None, "group", "mp"),
        P(None, "group", "mp"),
    )
    out_specs = (
        P("group", "mp"),
        P("group", "mp"),
        P(None, "group", "mp"),
        P(None, "group", "mp"),
        P(None, "group", "mp"),
    )
    return jax.shard_map(shards, mesh=mesh, in_specs=in_specs, out_specs=out_specs, check_vma=False)
```

```python
import jax
import jax.numpy as jnp
from jax import lax
from jax.experimental import pallas as pl
from jax.experimental.pallas import tpu as pltpu
from jax.sharding import PartitionSpec as P

BF = jnp.bfloat16
F32 = jnp.float32
NX, NZ = 4, 8
HALF = NX * NZ
CAP = 12
SLOT = 16
UNITS = (
    (0, 0, 256),
    (0, 256, 384),
    (0, 640, 384),
    (1, 0, 512),
    (1, 512, 512),
    (2, 0, 640),
)
FLIP = (2, 640, 384)


def place():
    g = lax.axis_index("group")
    p = lax.axis_index("mp")
    h = lax.div(g, HALF)
    x = lax.rem(lax.div(g, NZ), NX)
    z = lax.rem(g, NZ)
    return p, h, x, z


def around(v, by, size):
    return lax.rem(v + (by + size), size)


def rows16(c):
    return pl.ds(pl.multiple_of(c * 16, 16), 16)


def greet(peers):
    barrier = pltpu.get_barrier_semaphore()
    for peer in peers:
        pl.semaphore_signal(barrier, inc=1, device_id=peer, device_id_type=pl.DeviceIdType.MESH)
    pl.semaphore_wait(barrier, len(peers))


def remote(src, dst, send, recv, peer):
    copy = pltpu.make_async_remote_copy(
        src_ref=src,
        dst_ref=dst,
        send_sem=send,
        recv_sem=recv,
        device_id=peer,
        device_id_type=pl.DeviceIdType.MESH,
    )
    copy.start()
    return copy


def peers_of(p, h, x, z):
    def at(hh, xx, zz):
        return (hh * HALF + xx * NZ + zz, p)

    zline = [at(h, x, around(z, d, NZ)) for d in range(1, NZ)]
    yx = h * NX + x
    plane = []
    for d in range(1, 2 * NX):
        k = around(yx, d, 2 * NX)
        plane.append((k, at(lax.div(k, NX), lax.rem(k, NX), z)))
    g = h * HALF + x * NZ + z
    core = p + 1 - 2 * lax.rem(p, 2)
    opposite = around(p, 2, 4)
    both = around(core, 2, 4)
    parts = [(core, (g, core)), (opposite, (g, opposite)), (both, (g, both))]
    return at, zline, plane, parts


def starts(counts, rows):
    b = lax.div(counts[0], rows)
    return b, lax.div(counts[0] + counts[1], rows)


def flag_of(begin, g):
    b, c = begin
    mod = (g >= b).astype(jnp.int32) + (g >= c).astype(jnp.int32)
    return jnp.clip(mod - lax.div(g, HALF), 0, 1)


def lanes_of(p, feats):
    return pl.ds(pl.multiple_of(p * feats, 128), feats)


def gather_kernel(
    counts, wg, wu, wd, xin, dyin, tags, target, og, ou, od, fx, fdy, close, position, *scratch
):
    n = len(UNITS)
    zbuf, sbuf = scratch[:n], scratch[n : 2 * n]
    begins = starts(counts, xin.shape[0])
    fbuf, fsend, tmid, rows, mine, tok = scratch[2 * n : 2 * n + 6]
    ys, yr, zs, zr, xs, xr, own, fs, fr, gs, gr, ts, tr, tl, ms, mr, ml = scratch[2 * n + 6 :]
    p, h, x, z = place()
    at, zline, plane, parts = peers_of(p, h, x, z)
    over = at(1 - h, x, z)
    xline = [at(h, around(x, d, NX), z) for d in range(1, NX)]
    greet(zline + [q for _, q in plane] + [q for _, q in parts])
    weights = (wg, wu, wd)
    outs = (og, ou, od)
    sends, waits, local = [], [], []
    cross, near, later = {}, {}, {}

    def begin(u):
        w, c0, width = UNITS[u] if u < n else FLIP
        c = pl.ds(c0, width)
        if u < n:
            theirs = zbuf[u].at[:, h, rows16(z), :]
        else:
            theirs = fbuf.at[:, h, x]
        cross[u] = remote(
            weights[w].at[pl.ds(1 - h, 2), :, c], theirs, ys.at[u], yr.at[u], over
        )
        sends.append(cross[u])
        theirs[...] = weights[w][pl.ds(h, 2), :, c]

    def first(u):
        cross[u].wait_recv()
        v = zbuf[u].at[:, :, rows16(z), :]
        hops = ((2, 2), (3, -2), (0, 1), (1, -1))
        near[u] = {
            i: remote(v, v, zs.at[u, i], zr.at[u, i], zline[d % NZ - 1]) for i, d in hops
        }
        sends.extend(near[u].values())

    def second(u):
        later[u] = [near[u][0], near[u][1]]
        for i, by in enumerate((1, -1)):
            near[u][2 + i].wait_recv()
            chunk = rows16(around(z, -2 * by, NZ))
            v = zbuf[u].at[:, :, chunk, :]
            a = remote(v, v, zs.at[u, 4 + i], zr.at[u, 4 + i], zline[by % NZ - 1])
            v = zbuf[u].at[:, i, chunk, :]
            b = remote(v, v, zs.at[u, 6 + i], zr.at[u, 6 + i], zline[2 * by % NZ - 1])
            later[u].extend([a, b])
            sends.extend([a, b])

    def spread(u):
        for c in later[u]:
            c.wait_recv()
        w, c0, width = UNITS[u]
        out = outs[w].at[:, x, :, pl.ds(c0, width)]
        for d in (2, 1, 3, 0):
            f = flag_of(begins, h * HALF + around(x, d, NX) * NZ + z)
            sbuf[u][d] = zbuf[u][f]
            if d == 0:
                a = pltpu.make_async_copy(sbuf[u].at[0], out, own.at[u])
                a.start()
                local.append(a)
            else:
                a = remote(sbuf[u].at[d], out, xs.at[u, d], xr.at[u, d], xline[d - 1])
                sends.append(a)
                waits.append(a)

    def flip_first():
        cross[n].wait_recv()
        v = fbuf.at[:, :, x]
        near[n] = [remote(v, v, fs.at[d], fr.at[d], xline[d - 1]) for d in (2, 1, 3)]
        sends.extend(near[n])

    def flip_second():
        for c in near[n]:
            c.wait_recv()
        w, c0, width = FLIP
        out = outs[w].at[:, :, rows16(z), pl.ds(c0, width)]
        for d in (4, 3, 5, 2, 6, 1, 7, 0):
            f = flag_of(begins, h * HALF + x * NZ + around(z, d, NZ))
            fsend[d] = fbuf[f]
            if d == 0:
                a = pltpu.make_async_copy(fsend.at[0], out, own.at[n])
                a.start()
                local.append(a)
            else:
                a = remote(fsend.at[d], out, gs.at[d], gr.at[d], zline[d - 1])
                sends.append(a)
                waits.append(a)

    yx = h * NX + x
    stage = {}

    def address():
        count = xin.shape[0]
        groups = 2 * HALF
        wide = groups * SLOT
        kind = tags[...]
        base = jnp.where(kind == 0, 0, jnp.where(kind == 1, begins[0], begins[1]))
        dest = base + target[...]
        spread_dest = jnp.broadcast_to(dest.astype(F32), (count, count))
        i = lax.broadcasted_iota(jnp.int32, (count, count), 0)
        j = lax.broadcasted_iota(jnp.int32, (count, count), 1)
        same = (spread_dest == spread_dest.T) & (i < j)
        slot = jnp.sum(jnp.where(same, 1.0, 0.0), axis=0, keepdims=True)
        place_row = dest * SLOT + slot.astype(jnp.int32)
        position[...] = place_row
        i = lax.broadcasted_iota(jnp.int32, (wide, count), 0)
        into = jnp.where(i == place_row, 1.0, 0.0).astype(BF)
        feats = xin.shape[1]
        i = lax.broadcasted_iota(jnp.int32, (groups, count), 0)
        goes = jnp.where(i == dest, 1.0, 0.0).astype(BF)
        sent = jnp.dot(goes, jnp.ones((count, feats), BF), preferred_element_type=F32)
        spot = lax.broadcasted_iota(jnp.int32, (groups, SLOT, feats), 1)
        for b, v in enumerate((xin, dyin)):
            part = jnp.dot(into, v[...], preferred_element_type=F32)
            part = part.reshape(groups, SLOT, feats)
            if b == 0:
                part = jnp.where(spot >= CAP, sent[:, None, :], part)
            tok[:, :, :, b * feats : (b + 1) * feats] = part.astype(BF).reshape(
                2 * NX, NZ, SLOT, feats
            )

    def tokens_plane():
        stage["p"] = []
        for d in range(1, 2 * NX):
            k, peer = plane[d - 1]
            stage["p"].append(
                remote(tok.at[k], tmid.at[yx], ts.at[NZ + d], tr.at[NZ + d], peer)
            )
        sends.extend(stage["p"])
        a = pltpu.make_async_copy(tok.at[yx], tmid.at[yx], tl.at[1])
        a.start()
        stage["pl"] = a

    def tokens_z():
        stage["pl"].wait()
        for c in stage["p"]:
            c.wait_recv()
        stage["z"] = []
        for d in (4, 3, 5, 2, 6, 1, 7):
            to = around(z, d, NZ)
            stage["z"].append(
                remote(tmid.at[:, to], rows.at[:, z], ts.at[d], tr.at[d], zline[d - 1])
            )
        sends.extend(stage["z"])
        a = pltpu.make_async_copy(tmid.at[:, z], rows.at[:, z], tl.at[0])
        a.start()
        stage["zl"] = a

    def compact():
        stage["zl"].wait()
        for c in stage["z"]:
            c.wait_recv()
        groups = 2 * HALF
        spot = lax.broadcasted_iota(jnp.int32, (groups, SLOT, 128), 1)
        head = rows[:, :, :, 0:128].reshape(groups, SLOT, 128).astype(F32)
        count = jnp.sum(jnp.where(spot == CAP, head, 0.0), axis=1)
        i = lax.broadcasted_iota(jnp.int32, (groups, groups), 0)
        j = lax.broadcasted_iota(jnp.int32, (groups, groups), 1)
        lower = jnp.where(i > j, 1.0, 0.0).astype(BF)
        before = jnp.dot(lower, count.astype(BF), preferred_element_type=F32)
        spot = spot.astype(F32)
        rank = jnp.where(spot < count[:, None, :], before[:, None, :] + spot, -1.0)
        rank = rank.reshape(groups * SLOT, 128)
        lane = lax.broadcasted_iota(jnp.int32, (groups * SLOT, 128), 1)
        for b in range(close.shape[1] // 128):
            hit = rank == (lane + b * 128).astype(F32)
            close[:, b * 128 : (b + 1) * 128] = jnp.where(hit, 1.0, 0.0).astype(BF)
        feats = rows.shape[3] // 2
        for b in range(2):
            part = rows[:, :, :, b * feats : (b + 1) * feats].reshape(groups * SLOT, feats)
            picked = lax.dot_general(
                close[...], part, (((0,), (0,)), ((), ())), preferred_element_type=F32
            )
            mine[b] = picked.astype(BF)
        here = lanes_of(p, feats)
        stage["m"] = []
        for b, full in enumerate((fx, fdy)):
            a = pltpu.make_async_copy(mine.at[b], full.at[:, here], ml.at[b])
            a.start()
            local.append(a)
            for i in (1, 0):
                a = remote(mine.at[b], full.at[:, here], ms.at[i, b], mr.at[i, b], parts[i][1])
                sends.append(a)
                stage["m"].append(a)

    def share():
        for c in stage["m"]:
            c.wait_recv()
        there = lanes_of(parts[1][0], fx.shape[1] // 4)
        for b, full in enumerate((fx, fdy)):
            view = full.at[:, there]
            a = remote(view, view, ms.at[2, b], mr.at[2, b], parts[0][1])
            sends.append(a)
            waits.append(a)

    for u in range(n + 1):
        begin(u)
    first(0)
    flip_first()
    address()
    tokens_plane()
    second(0)
    first(1)
    spread(0)
    second(1)
    first(2)
    tokens_z()
    spread(1)
    second(2)
    first(3)
    spread(2)
    second(3)
    first(4)
    spread(3)
    second(4)
    first(5)
    compact()
    spread(4)
    second(5)
    flip_second()
    spread(5)
    share()
    for c in waits:
        c.wait_recv()
    for c in sends:
        c.wait_send()
    for c in local:
        c.wait()


def gather_all(counts, wg, wu, wd, tokens, cotangent, tags, target):
    cols = wg.shape[2]
    rows, feats = tokens.shape
    n = len(UNITS)
    vm = pl.BlockSpec(memory_space=pltpu.VMEM)
    hbm = pl.BlockSpec(memory_space=pl.ANY)
    dma = pltpu.SemaphoreType.DMA
    out = jax.ShapeDtypeStruct((2, NX, 16 * NZ, cols), BF)
    full = jax.ShapeDtypeStruct((rows, 4 * feats), BF)
    close = jax.ShapeDtypeStruct((2 * HALF * SLOT, rows), BF)
    return pl.pallas_call(
        gather_kernel,
        out_shape=(out, out, out, full, full, close, jax.ShapeDtypeStruct((1, rows), jnp.int32)),
        in_specs=[pl.BlockSpec(memory_space=pltpu.SMEM)] + [vm] * 7,
        out_specs=[hbm] * 5 + [vm] * 2,
        scratch_shapes=[pltpu.VMEM((2, 2, 16 * NZ, u[2]), BF) for u in UNITS]
        + [pltpu.VMEM((4, 2, 16 * NZ, u[2]), BF) for u in UNITS]
        + [
            pltpu.VMEM((2, 2, NX, 16, FLIP[2]), BF),
            pltpu.VMEM((NZ, 2, NX, 16, FLIP[2]), BF),
            pltpu.VMEM((2 * NX, NZ, SLOT, 2 * feats), BF),
            pltpu.VMEM((2 * NX, NZ, SLOT, 2 * feats), BF),
            pltpu.VMEM((2, rows, feats), BF),
            pltpu.VMEM((2 * NX, NZ, SLOT, 2 * feats), BF),
            dma((n + 1,)),
            dma((n + 1,)),
            dma((n, 8)),
            dma((n, 8)),
            dma((n, 4)),
            dma((n, 4)),
            dma((n + 1,)),
            dma((4,)),
            dma((4,)),
            dma((8,)),
            dma((8,)),
            dma((16,)),
            dma((16,)),
            dma((2,)),
            dma((3, 2)),
            dma((3, 2)),
            dma((2,)),
        ],
        compiler_params=pltpu.CompilerParams(
            collective_id=0, has_side_effects=True, vmem_limit_bytes=48 * 1024 * 1024
        ),
        cost_estimate=pl.CostEstimate(flops=0, bytes_accessed=200_000_000, transcendentals=0),
        name="gather_all",
    )(counts, wg, wu, wd, tokens, cotangent, tags.reshape(1, rows), target.reshape(1, rows))


def reduce_kernel(
    counts, xf, dyf, dgate, dup, hidden, res, dx, close, og, ou, od, back, *scratch
):
    n = len(UNITS)
    per = 10
    bufs = [scratch[per * u : per * u + per] for u in range(n)]
    ends = [b[7:] for b in bufs] + [scratch[per * n + 3 : per * n + 6]]
    fin, fsum, fgot = scratch[per * n : per * n + 3]
    pin, spread_rows, tmid = scratch[per * n + 6 : per * n + 9]
    made = scratch[per * n + 9 : per * n + 10 + n]
    ys, yr, zs, zr, xs, xr, own, fs, fr, gs, gr, ts, tr, tl, ms, mr, ml = scratch[
        per * n + 10 + n :
    ]
    begins = starts(counts, xf.shape[0])
    p, h, x, z = place()
    at, zline, plane, parts = peers_of(p, h, x, z)
    over = at(1 - h, x, z)
    xline = [at(h, around(x, d, NX), z) for d in range(1, NX)]
    greet(zline + [q for _, q in plane] + [q for _, q in parts])
    pairs = ((xf, dgate), (xf, dup), (dyf, hidden))
    outs = (og, ou, od)
    order = UNITS[::-1]
    sends = []
    arriving, stepping, cross, stage = {}, {}, {}, {}

    def make(u):
        w, c0, width = order[u] if u < n else FLIP
        left, right = pairs[w]
        deep = 32 * NZ

        def body(i, _):
            cut = pl.ds(pl.multiple_of(i * deep, deep), deep)
            v = lax.dot_general(
                left[:, cut],
                right[:, c0 : c0 + width],
                (((0,), (0,)), ((), ())),
                preferred_element_type=F32,
            ).astype(BF)
            y = lax.div(i, 2)
            k = lax.rem(i, 2) * 2
            made[u][y, k] = v[: deep // 2]
            made[u][y, k + 1] = v[deep // 2 :]
            return 0

        lax.fori_loop(0, 4, body, 0)

    def spread(u):
        make(u)
        g = made[u]
        rbuf = bufs[u][0]
        arriving[u] = []
        for d in (2, 1, 3):
            a = remote(
                g.at[:, around(x, d, NX)],
                rbuf.at[d],
                xs.at[u, d],
                xr.at[u, d],
                xline[d - 1],
            )
            arriving[u].append(a)
            sends.append(a)
        a = pltpu.make_async_copy(g.at[:, x], rbuf.at[0], own.at[u])
        a.start()
        arriving[u].append(a)

    def arrive(u):
        for c in arriving[u][:3]:
            c.wait_recv()
        arriving[u][3].wait()

    def binned(terms, marks):
        low = high = None
        for v, m in zip(terms, marks):
            v = v.astype(F32)
            b = v * m
            a = v - b
            low = a if low is None else low + a
            high = b if high is None else high + b
        return low.astype(BF), high.astype(BF)

    xmarks = [
        flag_of(begins, h * HALF + around(x, -d, NX) * NZ + z).astype(F32) for d in range(NX)
    ]

    def bins(u):
        rbuf, zsum = bufs[u][:2]

        def body(i, _):
            y = lax.div(i, NZ)
            r = rows16(lax.rem(i, NZ))
            low, high = binned([rbuf[k, y, r, :] for k in range(NX)], xmarks)
            zsum[0, y, r, :] = low
            zsum[1, y, r, :] = high
            return 0

        lax.fori_loop(0, 2 * NZ, body, 0)

    def first(u):
        zsum, dbuf, tbuf, hbuf = bufs[u][1:5]
        stepping[u] = []
        for i, by in enumerate((1, -1)):
            a = remote(
                zsum.at[:, :, rows16(around(z, 3 * by, NZ)), :],
                tbuf.at[i],
                zs.at[u, i],
                zr.at[u, i],
                zline[by % NZ - 1],
            )
            b = remote(
                zsum.at[:, i, rows16(around(z, 4, NZ)), :],
                hbuf.at[i],
                zs.at[u, 2 + i],
                zr.at[u, 2 + i],
                zline[2 * by % NZ - 1],
            )
            stepping[u].append((a, b))
            sends.extend([a, b])
        for i, by in enumerate((1, -1)):
            a = remote(
                zsum.at[:, :, rows16(around(z, by, NZ)), :],
                dbuf.at[i],
                zs.at[u, 4 + i],
                zr.at[u, 4 + i],
                zline[by % NZ - 1],
            )
            stepping[u].append(a)
            sends.append(a)

    def second(u):
        zsum, dbuf, tbuf, hbuf, obuf, ebuf = bufs[u][1:7]
        waits = stepping[u][2:]
        for i, by in enumerate((1, -1)):
            for c in stepping[u][i]:
                c.wait_recv()
            part = rows16(around(z, 2 * by, NZ))
            for y in range(2):
                v = zsum[:, y, part, :].astype(F32) + tbuf[i, :, y].astype(F32)
                if y == i:
                    v = v + hbuf[i].astype(F32)
                obuf[i, :, y] = v.astype(BF)
            a = remote(
                obuf.at[i], ebuf.at[i], zs.at[u, 6 + i], zr.at[u, 6 + i], zline[2 * by % NZ - 1]
            )
            waits.append(a)
            sends.append(a)
        stepping[u] = waits

    def swap(u):
        for c in stepping[u]:
            c.wait_recv()
        keep, ysend, yin = ends[u]

        def total(y):
            if u == n:
                v = fsum[:, y, x].astype(F32)
                for d in range(1, NX):
                    v = v + fgot[d, :, y].astype(F32)
                return v
            zsum, dbuf, ebuf = bufs[u][1], bufs[u][2], bufs[u][6]
            v = zsum[:, y, rows16(z), :].astype(F32)
            for b in (dbuf, ebuf):
                v = v + b[0, :, y].astype(F32) + b[1, :, y].astype(F32)
            return v

        ysend[...] = total(1 - h).astype(BF)
        cross[u] = remote(ysend, yin, ys.at[u], yr.at[u], over)
        sends.append(cross[u])
        keep[...] = total(h)

    def finish(u):
        w, c0, width = order[u] if u < n else FLIP
        c = pl.ds(c0, width)
        keep, ysend, yin = ends[u]
        cross[u].wait_recv()
        out = outs[w]
        out[2 * h, :, c] = keep[h]
        out[1, :, c] = keep[1 - h] + yin[h].astype(F32)
        out[2 - 2 * h, :, c] = yin[1 - h].astype(F32)

    def flip_spread():
        make(n)
        g = made[n]
        arriving[n] = []
        for d in (4, 3, 5, 2, 6, 1, 7):
            a = remote(
                g.at[:, :, rows16(around(z, d, NZ)), :],
                fin.at[d],
                gs.at[d],
                gr.at[d],
                zline[d - 1],
            )
            arriving[n].append(a)
            sends.append(a)
        a = pltpu.make_async_copy(g.at[:, :, rows16(z), :], fin.at[0], own.at[n])
        a.start()
        arriving[n].append(a)

    def flip_second():
        for c in arriving[n][:-1]:
            c.wait_recv()
        arriving[n][-1].wait()
        marks = [
            flag_of(begins, h * HALF + x * NZ + around(z, -d, NZ)).astype(F32)
            for d in range(NZ)
        ]

        def body(i, _):
            y = lax.div(i, NX)
            k = lax.rem(i, NX)
            low, high = binned([fin[d, y, k] for d in range(NZ)], marks)
            fsum[0, y, k] = low
            fsum[1, y, k] = high
            return 0

        lax.fori_loop(0, 2 * NX, body, 0)
        stepping[n] = []
        for d in (2, 1, 3):
            a = remote(
                fsum.at[:, :, around(x, d, NX)], fgot.at[d], fs.at[d], fr.at[d], xline[d - 1]
            )
            stepping[n].append(a)
            sends.append(a)

    yx = h * NX + x
    feats = res.shape[1] // 4

    def sums_out():
        stage["m"] = []
        for i in (1, 2, 0):
            q, peer = parts[i]
            for b, v in enumerate((res, dx)):
                stage["m"].append(
                    remote(v.at[:, lanes_of(q, feats)], pin.at[i, b], ms.at[i, b], mr.at[i, b], peer)
                )
        here = lanes_of(p, feats)
        stage["ml"] = []
        for b, v in enumerate((res, dx)):
            a = pltpu.make_async_copy(v.at[:, here], pin.at[3, b], ml.at[b])
            a.start()
            stage["ml"].append(a)

    def widen():
        for c in stage["ml"]:
            c.wait()
        for c in stage["m"]:
            c.wait_recv()
        sends.extend(stage["m"])
        for b in range(2):
            v = pin[3, b].astype(F32)
            for i in range(3):
                v = v + pin[i, b].astype(F32)
            v = jnp.dot(close[...], v.astype(BF), preferred_element_type=F32).astype(BF)
            spread_rows[:, :, :, b * feats : (b + 1) * feats] = v.reshape(
                2 * NX, NZ, SLOT, feats
            )
        stage["z"] = []
        for d in (4, 3, 5, 2, 6, 1, 7):
            stage["z"].append(
                remote(
                    spread_rows.at[:, around(z, d, NZ)],
                    tmid.at[z],
                    ts.at[d],
                    tr.at[d],
                    zline[d - 1],
                )
            )
        sends.extend(stage["z"])
        a = pltpu.make_async_copy(spread_rows.at[:, z], tmid.at[z], tl.at[0])
        a.start()
        stage["zl"] = a

    def homeward():
        stage["zl"].wait()
        for c in stage["z"]:
            c.wait_recv()
        stage["p"] = []
        for d in range(1, 2 * NX):
            k, peer = plane[d - 1]
            stage["p"].append(
                remote(tmid.at[:, k], back.at[yx], ts.at[NZ + d], tr.at[NZ + d], peer)
            )
        sends.extend(stage["p"])
        a = pltpu.make_async_copy(tmid.at[:, yx], back.at[yx], tl.at[1])
        a.start()
        stage["pl"] = a

    sums_out()
    spread(0)
    flip_spread()
    spread(1)
    spread(2)
    spread(3)
    spread(4)
    spread(5)
    arrive(0)
    bins(0)
    first(0)
    widen()
    second(0)
    arrive(1)
    bins(1)
    first(1)
    swap(0)
    second(1)
    arrive(2)
    bins(2)
    first(2)
    swap(1)
    second(2)
    homeward()
    flip_second()
    arrive(3)
    bins(3)
    first(3)
    swap(2)
    second(3)
    arrive(4)
    bins(4)
    first(4)
    swap(3)
    second(4)
    swap(n)
    arrive(5)
    bins(5)
    first(5)
    swap(4)
    second(5)
    swap(n - 1)
    for u in range(n + 1):
        finish((n + u) % (n + 1))
    stage["pl"].wait()
    for c in stage["p"]:
        c.wait_recv()
    for c in sends:
        c.wait_send()


def reduce_all(counts, xf, dyf, dgate, dup, hidden, res, dx, close):
    cols = dgate.shape[1]
    rows = res.shape[0]
    feats = res.shape[1] // 4
    n = len(UNITS)
    vm = pl.BlockSpec(memory_space=pltpu.VMEM)
    hbm = pl.BlockSpec(memory_space=pl.ANY)
    dma = pltpu.SemaphoreType.DMA
    out = jax.ShapeDtypeStruct((3, 16, cols), F32)
    back = jax.ShapeDtypeStruct((2 * NX, NZ, SLOT, 2 * feats), BF)
    bufs = []
    for _, _, wide in UNITS[::-1]:
        bufs += [
            pltpu.VMEM((NX, 2, 16 * NZ, wide), BF),
            pltpu.VMEM((2, 2, 16 * NZ, wide), BF),
            pltpu.VMEM((2, 2, 2, 16, wide), BF),
            pltpu.VMEM((2, 2, 2, 16, wide), BF),
            pltpu.VMEM((2, 2, 16, wide), BF),
            pltpu.VMEM((2, 2, 2, 16, wide), BF),
            pltpu.VMEM((2, 2, 2, 16, wide), BF),
            pltpu.VMEM((2, 16, wide), F32),
            pltpu.VMEM((2, 16, wide), BF),
            pltpu.VMEM((2, 16, wide), BF),
        ]
    wide = FLIP[2]
    bufs += [
        pltpu.VMEM((NZ, 2, NX, 16, wide), BF),
        pltpu.VMEM((2, 2, NX, 16, wide), BF),
        pltpu.VMEM((NX, 2, 2, 16, wide), BF),
        pltpu.VMEM((2, 16, wide), F32),
        pltpu.VMEM((2, 16, wide), BF),
        pltpu.VMEM((2, 16, wide), BF),
    ]
    return pl.pallas_call(
        reduce_kernel,
        out_shape=(out, out, out, back),
        in_specs=[pl.BlockSpec(memory_space=pltpu.SMEM)] + [vm] * 5 + [hbm] * 2 + [vm],
        out_specs=[vm] * 3 + [hbm],
        scratch_shapes=bufs
        + [
            pltpu.VMEM((4, 2, rows, feats), BF),
            pltpu.VMEM((2 * NX, NZ, SLOT, 2 * feats), BF),
            pltpu.VMEM((NZ, 2 * NX, SLOT, 2 * feats), BF),
        ]
        + [pltpu.VMEM((2, NX, 16 * NZ, u[2]), BF) for u in UNITS[::-1] + (FLIP,)]
        + [
            dma((n + 1,)),
            dma((n + 1,)),
            dma((n, 8)),
            dma((n, 8)),
            dma((n, 4)),
            dma((n, 4)),
            dma((n + 1,)),
            dma((4,)),
            dma((4,)),
            dma((8,)),
            dma((8,)),
            dma((16,)),
            dma((16,)),
            dma((2,)),
            dma((3, 2)),
            dma((3, 2)),
            dma((2,)),
        ],
        compiler_params=pltpu.CompilerParams(
            collective_id=1, has_side_effects=True, vmem_limit_bytes=48 * 1024 * 1024
        ),
        cost_estimate=pl.CostEstimate(flops=0, bytes_accessed=200_000_000, transcendentals=0),
        name="reduce_all",
    )(counts, xf, dyf, dgate, dup, hidden, res, dx, close)


def project_rows(x, dy, wg, wu, wd):
    gate = jnp.dot(x, wg, preferred_element_type=F32)
    up = jnp.dot(x, wu, preferred_element_type=F32)
    sig = jax.nn.sigmoid(gate)
    silu = gate * sig
    hidden = (silu * up).astype(BF)
    out = lax.dot_general(hidden, wd, (((1,), (1,)), ((), ())), preferred_element_type=F32)
    dhidden = jnp.dot(dy, wd, preferred_element_type=F32)
    dgate = (dhidden * up * sig * (1.0 + gate * (1.0 - sig))).astype(BF)
    dup = (dhidden * silu).astype(BF)
    dx = lax.dot_general(dgate, wg, (((1,), (1,)), ((), ())), preferred_element_type=F32)
    dx = dx + lax.dot_general(dup, wu, (((1,), (1,)), ((), ())), preferred_element_type=F32)
    return out.astype(BF), dx.astype(BF), hidden, dgate, dup


def shards(tokens, cotangent, tags, counts, target, gate_weight, up_weight, down_weight):
    feats = tokens.shape[1]
    w_gate, w_up, w_down, full_x, full_dy, close, position = gather_all(
        counts, gate_weight, up_weight, down_weight, tokens, cotangent, tags, target
    )
    depth = full_x.shape[1]
    w_gate, w_up, w_down = (w.reshape(depth, -1) for w in (w_gate, w_up, w_down))
    out, dx, hidden, dgate, dup = project_rows(full_x, full_dy, w_gate, w_up, w_down)
    gate_grad, up_grad, down_grad, back = reduce_all(
        counts, full_x, full_dy, dgate, dup, hidden, out, dx, close
    )
    wide = close.shape[0]
    lanes = jnp.arange(wide, dtype=jnp.int32)
    out_of = (position[0][:, None] == lanes[None, :]).astype(BF)
    result = jnp.dot(out_of, back.reshape(wide, 2 * feats), preferred_element_type=F32).astype(BF)
    return result[:, :feats], result[:, feats:], gate_grad, up_grad, down_grad


def solution(mesh):
    in_specs = (
        P("group", "mp"),
        P("group", "mp"),
        P("group"),
        P(),
        P("group"),
        P(None, "group", "mp"),
        P(None, "group", "mp"),
        P(None, "group", "mp"),
    )
    out_specs = (
        P("group", "mp"),
        P("group", "mp"),
        P(None, "group", "mp"),
        P(None, "group", "mp"),
        P(None, "group", "mp"),
    )
    return jax.shard_map(shards, mesh=mesh, in_specs=in_specs, out_specs=out_specs, check_vma=False)
```

```python
import jax
import jax.numpy as jnp
from jax import lax
from jax.experimental import pallas as pl
from jax.experimental.pallas import tpu as pltpu
from jax.sharding import PartitionSpec as P

BF = jnp.bfloat16
F32 = jnp.float32
NX, NZ = 4, 8
HALF = NX * NZ
CAP = 12
SLOT = 16
UNITS = (
    (0, 0, 256),
    (0, 256, 384),
    (0, 640, 384),
    (1, 0, 512),
    (1, 512, 512),
    (2, 0, 640),
)
FLIP = (2, 640, 384)


def place():
    g = lax.axis_index("group")
    p = lax.axis_index("mp")
    h = lax.div(g, HALF)
    x = lax.rem(lax.div(g, NZ), NX)
    z = lax.rem(g, NZ)
    return p, h, x, z


def around(v, by, size):
    return lax.rem(v + (by + size), size)


def rows16(c):
    return pl.ds(pl.multiple_of(c * 16, 16), 16)


def greet(peers):
    barrier = pltpu.get_barrier_semaphore()
    for peer in peers:
        pl.semaphore_signal(barrier, inc=1, device_id=peer, device_id_type=pl.DeviceIdType.MESH)
    pl.semaphore_wait(barrier, len(peers))


def remote(src, dst, send, recv, peer):
    copy = pltpu.make_async_remote_copy(
        src_ref=src,
        dst_ref=dst,
        send_sem=send,
        recv_sem=recv,
        device_id=peer,
        device_id_type=pl.DeviceIdType.MESH,
    )
    copy.start()
    return copy


def peers_of(p, h, x, z):
    def at(hh, xx, zz):
        return (hh * HALF + xx * NZ + zz, p)

    zline = [at(h, x, around(z, d, NZ)) for d in range(1, NZ)]
    yx = h * NX + x
    plane = []
    for d in range(1, 2 * NX):
        k = around(yx, d, 2 * NX)
        plane.append((k, at(lax.div(k, NX), lax.rem(k, NX), z)))
    g = h * HALF + x * NZ + z
    core = p + 1 - 2 * lax.rem(p, 2)
    opposite = around(p, 2, 4)
    both = around(core, 2, 4)
    parts = [(core, (g, core)), (opposite, (g, opposite)), (both, (g, both))]
    return at, zline, plane, parts


def starts(counts, rows):
    b = lax.div(counts[0], rows)
    return b, lax.div(counts[0] + counts[1], rows)


def flag_of(begin, g):
    b, c = begin
    mod = (g >= b).astype(jnp.int32) + (g >= c).astype(jnp.int32)
    return jnp.clip(mod - lax.div(g, HALF), 0, 1)


def lanes_of(p, feats):
    return pl.ds(pl.multiple_of(p * feats, 128), feats)


def gather_kernel(
    counts, wg, wu, wd, xhbm, dyhbm, code, og, ou, od, fx, fdy, close, position, *scratch
):
    n = len(UNITS)
    zbuf, sbuf = scratch[:n], scratch[n : 2 * n]
    begins = starts(counts, xhbm.shape[0])
    fbuf, fsend, tmid, rows, mine, tok, xin, dyin = scratch[2 * n : 2 * n + 8]
    ys, yr, zs, zr, xs, xr, own, fs, fr, gs, gr, ts, tr, tl, ms, mr, ml, il = scratch[
        2 * n + 8 :
    ]
    p, h, x, z = place()
    at, zline, plane, parts = peers_of(p, h, x, z)
    over = at(1 - h, x, z)
    xline = [at(h, around(x, d, NX), z) for d in range(1, NX)]
    loads = [pltpu.make_async_copy(xhbm, xin, il.at[0]), pltpu.make_async_copy(dyhbm, dyin, il.at[1])]
    for c in loads:
        c.start()
    placed = {}
    for u in range(n + 1):
        w, c0, width = UNITS[u] if u < n else FLIP
        ours = zbuf[u].at[:, h, rows16(z), :] if u < n else fbuf.at[:, h, x]
        placed[u] = pltpu.make_async_copy(
            (wg, wu, wd)[w].at[pl.ds(h, 2), :, pl.ds(c0, width)], ours, il.at[2 + u]
        )
        placed[u].start()
    greet(zline + [q for _, q in plane] + [q for _, q in parts])
    weights = (wg, wu, wd)
    outs = (og, ou, od)
    sends, waits, local = [], [], []
    cross, near, later = {}, {}, {}

    def begin(u):
        w, c0, width = UNITS[u] if u < n else FLIP
        c = pl.ds(c0, width)
        if u < n:
            theirs = zbuf[u].at[:, h, rows16(z), :]
        else:
            theirs = fbuf.at[:, h, x]
        cross[u] = remote(
            weights[w].at[pl.ds(1 - h, 2), :, c], theirs, ys.at[u], yr.at[u], over
        )
        sends.append(cross[u])

    def first(u):
        placed[u].wait()
        cross[u].wait_recv()
        v = zbuf[u].at[:, :, rows16(z), :]
        hops = ((2, 2), (3, -2), (0, 1), (1, -1))
        near[u] = {
            i: remote(v, v, zs.at[u, i], zr.at[u, i], zline[d % NZ - 1]) for i, d in hops
        }
        sends.extend(near[u].values())

    def second(u):
        later[u] = [near[u][0], near[u][1]]
        for i, by in enumerate((1, -1)):
            near[u][2 + i].wait_recv()
            chunk = rows16(around(z, -2 * by, NZ))
            v = zbuf[u].at[:, :, chunk, :]
            a = remote(v, v, zs.at[u, 4 + i], zr.at[u, 4 + i], zline[by % NZ - 1])
            v = zbuf[u].at[:, i, chunk, :]
            b = remote(v, v, zs.at[u, 6 + i], zr.at[u, 6 + i], zline[2 * by % NZ - 1])
            later[u].extend([a, b])
            sends.extend([a, b])

    def spread(u):
        for c in later[u]:
            c.wait_recv()
        w, c0, width = UNITS[u]
        out = outs[w].at[:, x, :, pl.ds(c0, width)]
        for d in (2, 1, 3, 0):
            f = flag_of(begins, h * HALF + around(x, d, NX) * NZ + z)
            sbuf[u][d] = zbuf[u][f]
            if d == 0:
                a = pltpu.make_async_copy(sbuf[u].at[0], out, own.at[u])
                a.start()
                local.append(a)
            else:
                a = remote(sbuf[u].at[d], out, xs.at[u, d], xr.at[u, d], xline[d - 1])
                sends.append(a)
                waits.append(a)

    def flip_first():
        placed[n].wait()
        cross[n].wait_recv()
        v = fbuf.at[:, :, x]
        near[n] = [remote(v, v, fs.at[d], fr.at[d], xline[d - 1]) for d in (2, 1, 3)]
        sends.extend(near[n])

    def flip_second():
        for c in near[n]:
            c.wait_recv()
        w, c0, width = FLIP
        out = outs[w].at[:, :, rows16(z), pl.ds(c0, width)]
        for d in (4, 3, 5, 2, 6, 1, 7, 0):
            f = flag_of(begins, h * HALF + x * NZ + around(z, d, NZ))
            fsend[d] = fbuf[f]
            if d == 0:
                a = pltpu.make_async_copy(fsend.at[0], out, own.at[n])
                a.start()
                local.append(a)
            else:
                a = remote(fsend.at[d], out, gs.at[d], gr.at[d], zline[d - 1])
                sends.append(a)
                waits.append(a)

    yx = h * NX + x
    stage = {}

    def address():
        count = xin.shape[0]
        groups = 2 * HALF
        wide = groups * SLOT
        for c in loads:
            c.wait()
        kind = code[...] & 3
        base = jnp.where(kind == 0, 0, jnp.where(kind == 1, begins[0], begins[1]))
        dest = base + lax.shift_right_logical(code[...], 2)
        spread_dest = jnp.broadcast_to(dest.astype(F32), (count, count))
        i = lax.broadcasted_iota(jnp.int32, (count, count), 0)
        j = lax.broadcasted_iota(jnp.int32, (count, count), 1)
        same = (spread_dest == spread_dest.T) & (i < j)
        slot = jnp.sum(jnp.where(same, 1.0, 0.0), axis=0, keepdims=True)
        place_row = dest * SLOT + slot.astype(jnp.int32)
        position[...] = place_row
        i = lax.broadcasted_iota(jnp.int32, (wide, count), 0)
        into = jnp.where(i == place_row, 1.0, 0.0).astype(BF)
        feats = xin.shape[1]
        i = lax.broadcasted_iota(jnp.int32, (groups, count), 0)
        goes = jnp.where(i == dest, 1.0, 0.0).astype(BF)
        sent = jnp.dot(goes, jnp.ones((count, feats), BF), preferred_element_type=F32)
        spot = lax.broadcasted_iota(jnp.int32, (groups, SLOT, feats), 1)
        for b, v in enumerate((xin, dyin)):
            part = jnp.dot(into, v[...], preferred_element_type=F32)
            part = part.reshape(groups, SLOT, feats)
            if b == 0:
                part = jnp.where(spot >= CAP, sent[:, None, :], part)
            tok[:, :, :, b * feats : (b + 1) * feats] = part.astype(BF).reshape(
                2 * NX, NZ, SLOT, feats
            )

    def tokens_plane():
        stage["p"] = []
        for d in range(1, 2 * NX):
            k, peer = plane[d - 1]
            stage["p"].append(
                remote(tok.at[k], tmid.at[yx], ts.at[NZ + d], tr.at[NZ + d], peer)
            )
        sends.extend(stage["p"])
        a = pltpu.make_async_copy(tok.at[yx], tmid.at[yx], tl.at[1])
        a.start()
        stage["pl"] = a

    def tokens_z():
        stage["pl"].wait()
        for c in stage["p"]:
            c.wait_recv()
        stage["z"] = []
        for d in (4, 3, 5, 2, 6, 1, 7):
            to = around(z, d, NZ)
            stage["z"].append(
                remote(tmid.at[:, to], rows.at[:, z], ts.at[d], tr.at[d], zline[d - 1])
            )
        sends.extend(stage["z"])
        a = pltpu.make_async_copy(tmid.at[:, z], rows.at[:, z], tl.at[0])
        a.start()
        stage["zl"] = a

    def compact():
        stage["zl"].wait()
        for c in stage["z"]:
            c.wait_recv()
        groups = 2 * HALF
        spot = lax.broadcasted_iota(jnp.int32, (groups, SLOT, 128), 1)
        head = rows[:, :, :, 0:128].reshape(groups, SLOT, 128).astype(F32)
        count = jnp.sum(jnp.where(spot == CAP, head, 0.0), axis=1)
        i = lax.broadcasted_iota(jnp.int32, (groups, groups), 0)
        j = lax.broadcasted_iota(jnp.int32, (groups, groups), 1)
        lower = jnp.where(i > j, 1.0, 0.0).astype(BF)
        before = jnp.dot(lower, count.astype(BF), preferred_element_type=F32)
        spot = spot.astype(F32)
        rank = jnp.where(spot < count[:, None, :], before[:, None, :] + spot, -1.0)
        rank = rank.reshape(groups * SLOT, 128)
        lane = lax.broadcasted_iota(jnp.int32, (groups * SLOT, 128), 1)
        for b in range(close.shape[1] // 128):
            hit = rank == (lane + b * 128).astype(F32)
            close[:, b * 128 : (b + 1) * 128] = jnp.where(hit, 1.0, 0.0).astype(BF)
        feats = rows.shape[3] // 2
        for b in range(2):
            part = rows[:, :, :, b * feats : (b + 1) * feats].reshape(groups * SLOT, feats)
            picked = lax.dot_general(
                close[...], part, (((0,), (0,)), ((), ())), preferred_element_type=F32
            )
            mine[b] = picked.astype(BF)
        here = lanes_of(p, feats)
        stage["m"] = []
        for b, full in enumerate((fx, fdy)):
            a = pltpu.make_async_copy(mine.at[b], full.at[:, here], ml.at[b])
            a.start()
            local.append(a)
            for i in (1, 0):
                a = remote(mine.at[b], full.at[:, here], ms.at[i, b], mr.at[i, b], parts[i][1])
                sends.append(a)
                stage["m"].append(a)

    def share():
        for c in stage["m"]:
            c.wait_recv()
        there = lanes_of(parts[1][0], fx.shape[1] // 4)
        for b, full in enumerate((fx, fdy)):
            view = full.at[:, there]
            a = remote(view, view, ms.at[2, b], mr.at[2, b], parts[0][1])
            sends.append(a)
            waits.append(a)

    for u in range(n + 1):
        begin(u)
    first(0)
    flip_first()
    address()
    tokens_plane()
    second(0)
    first(1)
    spread(0)
    second(1)
    first(2)
    tokens_z()
    spread(1)
    second(2)
    first(3)
    spread(2)
    second(3)
    first(4)
    spread(3)
    second(4)
    first(5)
    compact()
    spread(4)
    second(5)
    flip_second()
    spread(5)
    share()
    for c in waits:
        c.wait_recv()
    for c in sends:
        c.wait_send()
    for c in local:
        c.wait()


def gather_all(counts, wg, wu, wd, tokens, cotangent, tags, target):
    cols = wg.shape[2]
    rows, feats = tokens.shape
    n = len(UNITS)
    vm = pl.BlockSpec(memory_space=pltpu.VMEM)
    hbm = pl.BlockSpec(memory_space=pl.ANY)
    dma = pltpu.SemaphoreType.DMA
    out = jax.ShapeDtypeStruct((2, NX, 16 * NZ, cols), BF)
    full = jax.ShapeDtypeStruct((rows, 4 * feats), BF)
    close = jax.ShapeDtypeStruct((2 * HALF * SLOT, rows), BF)
    return pl.pallas_call(
        gather_kernel,
        out_shape=(out, out, out, full, full, close, jax.ShapeDtypeStruct((1, rows), jnp.int32)),
        in_specs=[pl.BlockSpec(memory_space=pltpu.SMEM)] + [hbm] * 5 + [vm],
        out_specs=[hbm] * 5 + [vm] * 2,
        scratch_shapes=[pltpu.VMEM((2, 2, 16 * NZ, u[2]), BF) for u in UNITS]
        + [pltpu.VMEM((4, 2, 16 * NZ, u[2]), BF) for u in UNITS]
        + [
            pltpu.VMEM((2, 2, NX, 16, FLIP[2]), BF),
            pltpu.VMEM((NZ, 2, NX, 16, FLIP[2]), BF),
            pltpu.VMEM((2 * NX, NZ, SLOT, 2 * feats), BF),
            pltpu.VMEM((2 * NX, NZ, SLOT, 2 * feats), BF),
            pltpu.VMEM((2, rows, feats), BF),
            pltpu.VMEM((2 * NX, NZ, SLOT, 2 * feats), BF),
            pltpu.VMEM((rows, feats), BF),
            pltpu.VMEM((rows, feats), BF),
            dma((n + 1,)),
            dma((n + 1,)),
            dma((n, 8)),
            dma((n, 8)),
            dma((n, 4)),
            dma((n, 4)),
            dma((n + 1,)),
            dma((4,)),
            dma((4,)),
            dma((8,)),
            dma((8,)),
            dma((16,)),
            dma((16,)),
            dma((2,)),
            dma((3, 2)),
            dma((3, 2)),
            dma((2,)),
            dma((n + 3,)),
        ],
        compiler_params=pltpu.CompilerParams(
            collective_id=0, has_side_effects=True, vmem_limit_bytes=60 * 1024 * 1024
        ),
        cost_estimate=pl.CostEstimate(flops=0, bytes_accessed=200_000_000, transcendentals=0),
        name="gather_all",
    )(counts, wg, wu, wd, tokens, cotangent, (target * 4 + tags).reshape(1, rows))


def reduce_kernel(
    counts, xf, dyf, dgate, dup, hidden, res, dx, close, og, ou, od, back, *scratch
):
    n = len(UNITS)
    per = 10
    bufs = [scratch[per * u : per * u + per] for u in range(n)]
    ends = [b[7:] for b in bufs] + [scratch[per * n + 3 : per * n + 6]]
    fin, fsum, fgot = scratch[per * n : per * n + 3]
    pin, spread_rows, tmid = scratch[per * n + 6 : per * n + 9]
    made = scratch[per * n + 9 : per * n + 10 + n]
    ys, yr, zs, zr, xs, xr, own, fs, fr, gs, gr, ts, tr, tl, ms, mr, ml = scratch[
        per * n + 10 + n :
    ]
    begins = starts(counts, xf.shape[0])
    p, h, x, z = place()
    at, zline, plane, parts = peers_of(p, h, x, z)
    over = at(1 - h, x, z)
    xline = [at(h, around(x, d, NX), z) for d in range(1, NX)]
    greet(zline + [q for _, q in plane] + [q for _, q in parts])
    pairs = ((xf, dgate), (xf, dup), (dyf, hidden))
    outs = (og, ou, od)
    order = UNITS[::-1]
    sends = []
    arriving, stepping, cross, stage = {}, {}, {}, {}

    def make(u):
        w, c0, width = order[u] if u < n else FLIP
        left, right = pairs[w]
        deep = 32 * NZ

        def body(i, _):
            cut = pl.ds(pl.multiple_of(i * deep, deep), deep)
            v = lax.dot_general(
                left[:, cut],
                right[:, c0 : c0 + width],
                (((0,), (0,)), ((), ())),
                preferred_element_type=F32,
            ).astype(BF)
            y = lax.div(i, 2)
            k = lax.rem(i, 2) * 2
            made[u][y, k] = v[: deep // 2]
            made[u][y, k + 1] = v[deep // 2 :]
            return 0

        lax.fori_loop(0, 4, body, 0)

    def spread(u):
        make(u)
        g = made[u]
        rbuf = bufs[u][0]
        arriving[u] = []
        for d in (2, 1, 3):
            a = remote(
                g.at[:, around(x, d, NX)],
                rbuf.at[d],
                xs.at[u, d],
                xr.at[u, d],
                xline[d - 1],
            )
            arriving[u].append(a)
            sends.append(a)
        a = pltpu.make_async_copy(g.at[:, x], rbuf.at[0], own.at[u])
        a.start()
        arriving[u].append(a)

    def arrive(u):
        for c in arriving[u][:3]:
            c.wait_recv()
        arriving[u][3].wait()

    def binned(terms, marks):
        low = high = None
        for v, m in zip(terms, marks):
            v = v.astype(F32)
            b = v * m
            a = v - b
            low = a if low is None else low + a
            high = b if high is None else high + b
        return low.astype(BF), high.astype(BF)

    xmarks = [
        flag_of(begins, h * HALF + around(x, -d, NX) * NZ + z).astype(F32) for d in range(NX)
    ]

    def bins(u):
        rbuf, zsum = bufs[u][:2]

        def body(i, _):
            y = lax.div(i, NZ)
            r = rows16(lax.rem(i, NZ))
            low, high = binned([rbuf[k, y, r, :] for k in range(NX)], xmarks)
            zsum[0, y, r, :] = low
            zsum[1, y, r, :] = high
            return 0

        lax.fori_loop(0, 2 * NZ, body, 0)

    def first(u):
        zsum, dbuf, tbuf, hbuf = bufs[u][1:5]
        stepping[u] = []
        for i, by in enumerate((1, -1)):
            a = remote(
                zsum.at[:, :, rows16(around(z, 3 * by, NZ)), :],
                tbuf.at[i],
                zs.at[u, i],
                zr.at[u, i],
                zline[by % NZ - 1],
            )
            b = remote(
                zsum.at[:, i, rows16(around(z, 4, NZ)), :],
                hbuf.at[i],
                zs.at[u, 2 + i],
                zr.at[u, 2 + i],
                zline[2 * by % NZ - 1],
            )
            stepping[u].append((a, b))
            sends.extend([a, b])
        for i, by in enumerate((1, -1)):
            a = remote(
                zsum.at[:, :, rows16(around(z, by, NZ)), :],
                dbuf.at[i],
                zs.at[u, 4 + i],
                zr.at[u, 4 + i],
                zline[by % NZ - 1],
            )
            stepping[u].append(a)
            sends.append(a)

    def second(u):
        zsum, dbuf, tbuf, hbuf, obuf, ebuf = bufs[u][1:7]
        waits = stepping[u][2:]
        for i, by in enumerate((1, -1)):
            for c in stepping[u][i]:
                c.wait_recv()
            part = rows16(around(z, 2 * by, NZ))
            for y in range(2):
                v = zsum[:, y, part, :].astype(F32) + tbuf[i, :, y].astype(F32)
                if y == i:
                    v = v + hbuf[i].astype(F32)
                obuf[i, :, y] = v.astype(BF)
            a = remote(
                obuf.at[i], ebuf.at[i], zs.at[u, 6 + i], zr.at[u, 6 + i], zline[2 * by % NZ - 1]
            )
            waits.append(a)
            sends.append(a)
        stepping[u] = waits

    def swap(u):
        for c in stepping[u]:
            c.wait_recv()
        keep, ysend, yin = ends[u]

        def total(y):
            if u == n:
                v = fsum[:, y, x].astype(F32)
                for d in range(1, NX):
                    v = v + fgot[d, :, y].astype(F32)
                return v
            zsum, dbuf, ebuf = bufs[u][1], bufs[u][2], bufs[u][6]
            v = zsum[:, y, rows16(z), :].astype(F32)
            for b in (dbuf, ebuf):
                v = v + b[0, :, y].astype(F32) + b[1, :, y].astype(F32)
            return v

        ysend[...] = total(1 - h).astype(BF)
        cross[u] = remote(ysend, yin, ys.at[u], yr.at[u], over)
        sends.append(cross[u])
        keep[...] = total(h)

    def finish(u):
        w, c0, width = order[u] if u < n else FLIP
        c = pl.ds(c0, width)
        keep, ysend, yin = ends[u]
        cross[u].wait_recv()
        out = outs[w]
        out[2 * h, :, c] = keep[h]
        out[1, :, c] = keep[1 - h] + yin[h].astype(F32)
        out[2 - 2 * h, :, c] = yin[1 - h].astype(F32)

    def flip_spread():
        make(n)
        g = made[n]
        arriving[n] = []
        for d in (4, 3, 5, 2, 6, 1, 7):
            a = remote(
                g.at[:, :, rows16(around(z, d, NZ)), :],
                fin.at[d],
                gs.at[d],
                gr.at[d],
                zline[d - 1],
            )
            arriving[n].append(a)
            sends.append(a)
        a = pltpu.make_async_copy(g.at[:, :, rows16(z), :], fin.at[0], own.at[n])
        a.start()
        arriving[n].append(a)

    def flip_second():
        for c in arriving[n][:-1]:
            c.wait_recv()
        arriving[n][-1].wait()
        marks = [
            flag_of(begins, h * HALF + x * NZ + around(z, -d, NZ)).astype(F32)
            for d in range(NZ)
        ]

        def body(i, _):
            y = lax.div(i, NX)
            k = lax.rem(i, NX)
            low, high = binned([fin[d, y, k] for d in range(NZ)], marks)
            fsum[0, y, k] = low
            fsum[1, y, k] = high
            return 0

        lax.fori_loop(0, 2 * NX, body, 0)
        stepping[n] = []
        for d in (2, 1, 3):
            a = remote(
                fsum.at[:, :, around(x, d, NX)], fgot.at[d], fs.at[d], fr.at[d], xline[d - 1]
            )
            stepping[n].append(a)
            sends.append(a)

    yx = h * NX + x
    feats = res.shape[1] // 4

    def sums_out():
        stage["m"] = []
        for i in (1, 2, 0):
            q, peer = parts[i]
            for b, v in enumerate((res, dx)):
                stage["m"].append(
                    remote(v.at[:, lanes_of(q, feats)], pin.at[i, b], ms.at[i, b], mr.at[i, b], peer)
                )
        here = lanes_of(p, feats)
        stage["ml"] = []
        for b, v in enumerate((res, dx)):
            a = pltpu.make_async_copy(v.at[:, here], pin.at[3, b], ml.at[b])
            a.start()
            stage["ml"].append(a)

    def widen():
        for c in stage["ml"]:
            c.wait()
        for c in stage["m"]:
            c.wait_recv()
        sends.extend(stage["m"])
        for b in range(2):
            v = pin[3, b].astype(F32)
            for i in range(3):
                v = v + pin[i, b].astype(F32)
            v = jnp.dot(close[...], v.astype(BF), preferred_element_type=F32).astype(BF)
            spread_rows[:, :, :, b * feats : (b + 1) * feats] = v.reshape(
                2 * NX, NZ, SLOT, feats
            )
        stage["z"] = []
        for d in (4, 3, 5, 2, 6, 1, 7):
            stage["z"].append(
                remote(
                    spread_rows.at[:, around(z, d, NZ)],
                    tmid.at[z],
                    ts.at[d],
                    tr.at[d],
                    zline[d - 1],
                )
            )
        sends.extend(stage["z"])
        a = pltpu.make_async_copy(spread_rows.at[:, z], tmid.at[z], tl.at[0])
        a.start()
        stage["zl"] = a

    def homeward():
        stage["zl"].wait()
        for c in stage["z"]:
            c.wait_recv()
        stage["p"] = []
        for d in range(1, 2 * NX):
            k, peer = plane[d - 1]
            stage["p"].append(
                remote(tmid.at[:, k], back.at[yx], ts.at[NZ + d], tr.at[NZ + d], peer)
            )
        sends.extend(stage["p"])
        a = pltpu.make_async_copy(tmid.at[:, yx], back.at[yx], tl.at[1])
        a.start()
        stage["pl"] = a

    sums_out()
    spread(0)
    flip_spread()
    spread(1)
    spread(2)
    spread(3)
    spread(4)
    spread(5)
    arrive(0)
    bins(0)
    first(0)
    widen()
    second(0)
    arrive(1)
    bins(1)
    first(1)
    swap(0)
    second(1)
    arrive(2)
    bins(2)
    first(2)
    swap(1)
    second(2)
    homeward()
    flip_second()
    arrive(3)
    bins(3)
    first(3)
    swap(2)
    second(3)
    arrive(4)
    bins(4)
    first(4)
    swap(3)
    second(4)
    swap(n)
    arrive(5)
    bins(5)
    first(5)
    swap(4)
    second(5)
    swap(n - 1)
    for u in range(n + 1):
        finish((n + u) % (n + 1))
    stage["pl"].wait()
    for c in stage["p"]:
        c.wait_recv()
    for c in sends:
        c.wait_send()


def reduce_all(counts, xf, dyf, dgate, dup, hidden, res, dx, close):
    cols = dgate.shape[1]
    rows = res.shape[0]
    feats = res.shape[1] // 4
    n = len(UNITS)
    vm = pl.BlockSpec(memory_space=pltpu.VMEM)
    hbm = pl.BlockSpec(memory_space=pl.ANY)
    dma = pltpu.SemaphoreType.DMA
    out = jax.ShapeDtypeStruct((3, 16, cols), F32)
    back = jax.ShapeDtypeStruct((2 * NX, NZ, SLOT, 2 * feats), BF)
    bufs = []
    for _, _, wide in UNITS[::-1]:
        bufs += [
            pltpu.VMEM((NX, 2, 16 * NZ, wide), BF),
            pltpu.VMEM((2, 2, 16 * NZ, wide), BF),
            pltpu.VMEM((2, 2, 2, 16, wide), BF),
            pltpu.VMEM((2, 2, 2, 16, wide), BF),
            pltpu.VMEM((2, 2, 16, wide), BF),
            pltpu.VMEM((2, 2, 2, 16, wide), BF),
            pltpu.VMEM((2, 2, 2, 16, wide), BF),
            pltpu.VMEM((2, 16, wide), F32),
            pltpu.VMEM((2, 16, wide), BF),
            pltpu.VMEM((2, 16, wide), BF),
        ]
    wide = FLIP[2]
    bufs += [
        pltpu.VMEM((NZ, 2, NX, 16, wide), BF),
        pltpu.VMEM((2, 2, NX, 16, wide), BF),
        pltpu.VMEM((NX, 2, 2, 16, wide), BF),
        pltpu.VMEM((2, 16, wide), F32),
        pltpu.VMEM((2, 16, wide), BF),
        pltpu.VMEM((2, 16, wide), BF),
    ]
    return pl.pallas_call(
        reduce_kernel,
        out_shape=(out, out, out, back),
        in_specs=[pl.BlockSpec(memory_space=pltpu.SMEM)] + [vm] * 5 + [hbm] * 2 + [vm],
        out_specs=[vm] * 3 + [hbm],
        scratch_shapes=bufs
        + [
            pltpu.VMEM((4, 2, rows, feats), BF),
            pltpu.VMEM((2 * NX, NZ, SLOT, 2 * feats), BF),
            pltpu.VMEM((NZ, 2 * NX, SLOT, 2 * feats), BF),
        ]
        + [pltpu.VMEM((2, NX, 16 * NZ, u[2]), BF) for u in UNITS[::-1] + (FLIP,)]
        + [
            dma((n + 1,)),
            dma((n + 1,)),
            dma((n, 8)),
            dma((n, 8)),
            dma((n, 4)),
            dma((n, 4)),
            dma((n + 1,)),
            dma((4,)),
            dma((4,)),
            dma((8,)),
            dma((8,)),
            dma((16,)),
            dma((16,)),
            dma((2,)),
            dma((3, 2)),
            dma((3, 2)),
            dma((2,)),
        ],
        compiler_params=pltpu.CompilerParams(
            collective_id=1, has_side_effects=True, vmem_limit_bytes=48 * 1024 * 1024
        ),
        cost_estimate=pl.CostEstimate(flops=0, bytes_accessed=200_000_000, transcendentals=0),
        name="reduce_all",
    )(counts, xf, dyf, dgate, dup, hidden, res, dx, close)


def project_rows(x, dy, wg, wu, wd):
    gate = jnp.dot(x, wg, preferred_element_type=F32)
    up = jnp.dot(x, wu, preferred_element_type=F32)
    sig = jax.nn.sigmoid(gate)
    silu = gate * sig
    hidden = (silu * up).astype(BF)
    out = lax.dot_general(hidden, wd, (((1,), (1,)), ((), ())), preferred_element_type=F32)
    dhidden = jnp.dot(dy, wd, preferred_element_type=F32)
    dgate = (dhidden * up * sig * (1.0 + gate * (1.0 - sig))).astype(BF)
    dup = (dhidden * silu).astype(BF)
    dx = lax.dot_general(dgate, wg, (((1,), (1,)), ((), ())), preferred_element_type=F32)
    dx = dx + lax.dot_general(dup, wu, (((1,), (1,)), ((), ())), preferred_element_type=F32)
    return out.astype(BF), dx.astype(BF), hidden, dgate, dup


def shards(tokens, cotangent, tags, counts, target, gate_weight, up_weight, down_weight):
    feats = tokens.shape[1]
    w_gate, w_up, w_down, full_x, full_dy, close, position = gather_all(
        counts, gate_weight, up_weight, down_weight, tokens, cotangent, tags, target
    )
    depth = full_x.shape[1]
    w_gate, w_up, w_down = (w.reshape(depth, -1) for w in (w_gate, w_up, w_down))
    out, dx, hidden, dgate, dup = project_rows(full_x, full_dy, w_gate, w_up, w_down)
    gate_grad, up_grad, down_grad, back = reduce_all(
        counts, full_x, full_dy, dgate, dup, hidden, out, dx, close
    )
    wide = close.shape[0]
    lanes = jnp.arange(wide, dtype=jnp.int32)
    out_of = (position[0][:, None] == lanes[None, :]).astype(BF)
    result = jnp.dot(out_of, back.reshape(wide, 2 * feats), preferred_element_type=F32).astype(BF)
    return result[:, :feats], result[:, feats:], gate_grad, up_grad, down_grad


def solution(mesh):
    in_specs = (
        P("group", "mp"),
        P("group", "mp"),
        P("group"),
        P(),
        P("group"),
        P(None, "group", "mp"),
        P(None, "group", "mp"),
        P(None, "group", "mp"),
    )
    out_specs = (
        P("group", "mp"),
        P("group", "mp"),
        P(None, "group", "mp"),
        P(None, "group", "mp"),
        P(None, "group", "mp"),
    )
    return jax.shard_map(shards, mesh=mesh, in_specs=in_specs, out_specs=out_specs, check_vma=False)
```

```python
import jax
import jax.numpy as jnp
from jax import lax
from jax.experimental import pallas as pl
from jax.experimental.pallas import tpu as pltpu
from jax.sharding import PartitionSpec as P

BF = jnp.bfloat16
F32 = jnp.float32
NX, NZ = 4, 8
HALF = NX * NZ
CAP = 12
SLOT = 16
UNITS = (
    (0, 0, 384),
    (0, 384, 640),
    (1, 0, 512),
    (1, 512, 512),
    (2, 0, 384),
    (2, 384, 256),
)
FLIP = (2, 640, 384)


def place():
    g = lax.axis_index("group")
    p = lax.axis_index("mp")
    h = lax.div(g, HALF)
    x = lax.rem(lax.div(g, NZ), NX)
    z = lax.rem(g, NZ)
    return p, h, x, z


def around(v, by, size):
    return lax.rem(v + (by + size), size)


def rows16(c):
    return pl.ds(pl.multiple_of(c * 16, 16), 16)


def greet(peers):
    barrier = pltpu.get_barrier_semaphore()
    for peer in peers:
        pl.semaphore_signal(barrier, inc=1, device_id=peer, device_id_type=pl.DeviceIdType.MESH)
    pl.semaphore_wait(barrier, len(peers))


def remote(src, dst, send, recv, peer):
    copy = pltpu.make_async_remote_copy(
        src_ref=src,
        dst_ref=dst,
        send_sem=send,
        recv_sem=recv,
        device_id=peer,
        device_id_type=pl.DeviceIdType.MESH,
    )
    copy.start()
    return copy


def peers_of(p, h, x, z):
    def at(hh, xx, zz):
        return (hh * HALF + xx * NZ + zz, p)

    zline = [at(h, x, around(z, d, NZ)) for d in range(1, NZ)]
    yx = h * NX + x
    plane = []
    for d in range(1, 2 * NX):
        k = around(yx, d, 2 * NX)
        plane.append((k, at(lax.div(k, NX), lax.rem(k, NX), z)))
    g = h * HALF + x * NZ + z
    core = p + 1 - 2 * lax.rem(p, 2)
    opposite = around(p, 2, 4)
    both = around(core, 2, 4)
    parts = [(core, (g, core)), (opposite, (g, opposite)), (both, (g, both))]
    return at, zline, plane, parts


def starts(counts, rows):
    b = lax.div(counts[0], rows)
    return b, lax.div(counts[0] + counts[1], rows)


def flag_of(begin, g):
    b, c = begin
    mod = (g >= b).astype(jnp.int32) + (g >= c).astype(jnp.int32)
    return jnp.clip(mod - lax.div(g, HALF), 0, 1)


def lanes_of(p, feats):
    return pl.ds(pl.multiple_of(p * feats, 128), feats)


def gather_kernel(
    counts, wg, wu, wd, xhbm, dyhbm, code, og, ou, od, fx, fdy, close, position, *scratch
):
    n = len(UNITS)
    zbuf, sbuf = scratch[:n], scratch[n : 2 * n]
    begins = starts(counts, xhbm.shape[0])
    fbuf, fsend, tmid, rows, mine, tok, xin, dyin = scratch[2 * n : 2 * n + 8]
    ys, yr, zs, zr, xs, xr, own, fs, fr, gs, gr, ts, tr, tl, ms, mr, ml, il = scratch[
        2 * n + 8 :
    ]
    p, h, x, z = place()
    at, zline, plane, parts = peers_of(p, h, x, z)
    over = at(1 - h, x, z)
    xline = [at(h, around(x, d, NX), z) for d in range(1, NX)]
    loads = [pltpu.make_async_copy(xhbm, xin, il.at[0]), pltpu.make_async_copy(dyhbm, dyin, il.at[1])]
    for c in loads:
        c.start()
    placed = {}
    for u in range(n + 1):
        w, c0, width = UNITS[u] if u < n else FLIP
        ours = zbuf[u].at[:, h, rows16(z), :] if u < n else fbuf.at[:, h, x]
        placed[u] = pltpu.make_async_copy(
            (wg, wu, wd)[w].at[pl.ds(h, 2), :, pl.ds(c0, width)], ours, il.at[2 + u]
        )
        placed[u].start()
    greet(zline + [q for _, q in plane] + [q for _, q in parts])
    weights = (wg, wu, wd)
    outs = (og, ou, od)
    sends, waits, local = [], [], []
    cross, near, later = {}, {}, {}

    def begin(u):
        w, c0, width = UNITS[u] if u < n else FLIP
        c = pl.ds(c0, width)
        if u < n:
            theirs = zbuf[u].at[:, h, rows16(z), :]
        else:
            theirs = fbuf.at[:, h, x]
        cross[u] = remote(
            weights[w].at[pl.ds(1 - h, 2), :, c], theirs, ys.at[u], yr.at[u], over
        )
        sends.append(cross[u])

    def first(u):
        placed[u].wait()
        cross[u].wait_recv()
        v = zbuf[u].at[:, :, rows16(z), :]
        hops = ((2, 2), (3, -2), (0, 1), (1, -1))
        near[u] = {
            i: remote(v, v, zs.at[u, i], zr.at[u, i], zline[d % NZ - 1]) for i, d in hops
        }
        sends.extend(near[u].values())

    def second(u):
        later[u] = [near[u][0], near[u][1]]
        for i, by in enumerate((1, -1)):
            near[u][2 + i].wait_recv()
            chunk = rows16(around(z, -2 * by, NZ))
            v = zbuf[u].at[:, :, chunk, :]
            a = remote(v, v, zs.at[u, 4 + i], zr.at[u, 4 + i], zline[by % NZ - 1])
            v = zbuf[u].at[:, i, chunk, :]
            b = remote(v, v, zs.at[u, 6 + i], zr.at[u, 6 + i], zline[2 * by % NZ - 1])
            later[u].extend([a, b])
            sends.extend([a, b])

    def spread(u):
        for c in later[u]:
            c.wait_recv()
        w, c0, width = UNITS[u]
        out = outs[w].at[:, x, :, pl.ds(c0, width)]
        for d in (2, 1, 3, 0):
            f = flag_of(begins, h * HALF + around(x, d, NX) * NZ + z)
            sbuf[u][d] = zbuf[u][f]
            if d == 0:
                a = pltpu.make_async_copy(sbuf[u].at[0], out, own.at[u])
                a.start()
                local.append(a)
            else:
                a = remote(sbuf[u].at[d], out, xs.at[u, d], xr.at[u, d], xline[d - 1])
                sends.append(a)
                waits.append(a)

    def flip_first():
        placed[n].wait()
        cross[n].wait_recv()
        v = fbuf.at[:, :, x]
        near[n] = [remote(v, v, fs.at[d], fr.at[d], xline[d - 1]) for d in (2, 1, 3)]
        sends.extend(near[n])

    def flip_second():
        for c in near[n]:
            c.wait_recv()
        w, c0, width = FLIP
        out = outs[w].at[:, :, rows16(z), pl.ds(c0, width)]
        for d in (4, 3, 5, 2, 6, 1, 7, 0):
            f = flag_of(begins, h * HALF + x * NZ + around(z, d, NZ))
            fsend[d] = fbuf[f]
            if d == 0:
                a = pltpu.make_async_copy(fsend.at[0], out, own.at[n])
                a.start()
                local.append(a)
            else:
                a = remote(fsend.at[d], out, gs.at[d], gr.at[d], zline[d - 1])
                sends.append(a)
                waits.append(a)

    yx = h * NX + x
    stage = {}

    def address():
        count = xin.shape[0]
        groups = 2 * HALF
        wide = groups * SLOT
        for c in loads:
            c.wait()
        kind = code[...] & 3
        base = jnp.where(kind == 0, 0, jnp.where(kind == 1, begins[0], begins[1]))
        dest = base + lax.shift_right_logical(code[...], 2)
        spread_dest = jnp.broadcast_to(dest.astype(F32), (count, count))
        i = lax.broadcasted_iota(jnp.int32, (count, count), 0)
        j = lax.broadcasted_iota(jnp.int32, (count, count), 1)
        same = (spread_dest == spread_dest.T) & (i < j)
        slot = jnp.sum(jnp.where(same, 1.0, 0.0), axis=0, keepdims=True)
        place_row = dest * SLOT + slot.astype(jnp.int32)
        position[...] = place_row
        i = lax.broadcasted_iota(jnp.int32, (wide, count), 0)
        into = jnp.where(i == place_row, 1.0, 0.0).astype(BF)
        feats = xin.shape[1]
        i = lax.broadcasted_iota(jnp.int32, (groups, count), 0)
        goes = jnp.where(i == dest, 1.0, 0.0).astype(BF)
        sent = jnp.dot(goes, jnp.ones((count, feats), BF), preferred_element_type=F32)
        spot = lax.broadcasted_iota(jnp.int32, (groups, SLOT, feats), 1)
        for b, v in enumerate((xin, dyin)):
            part = jnp.dot(into, v[...], preferred_element_type=F32)
            part = part.reshape(groups, SLOT, feats)
            if b == 0:
                part = jnp.where(spot >= CAP, sent[:, None, :], part)
            tok[:, :, :, b * feats : (b + 1) * feats] = part.astype(BF).reshape(
                2 * NX, NZ, SLOT, feats
            )

    def tokens_plane():
        stage["p"] = []
        for d in range(1, 2 * NX):
            k, peer = plane[d - 1]
            stage["p"].append(
                remote(tok.at[k], tmid.at[yx], ts.at[NZ + d], tr.at[NZ + d], peer)
            )
        sends.extend(stage["p"])
        a = pltpu.make_async_copy(tok.at[yx], tmid.at[yx], tl.at[1])
        a.start()
        stage["pl"] = a

    def tokens_z():
        stage["pl"].wait()
        for c in stage["p"]:
            c.wait_recv()
        stage["z"] = []
        for d in (4, 3, 5, 2, 6, 1, 7):
            to = around(z, d, NZ)
            stage["z"].append(
                remote(tmid.at[:, to], rows.at[:, z], ts.at[d], tr.at[d], zline[d - 1])
            )
        sends.extend(stage["z"])
        a = pltpu.make_async_copy(tmid.at[:, z], rows.at[:, z], tl.at[0])
        a.start()
        stage["zl"] = a

    def compact():
        stage["zl"].wait()
        for c in stage["z"]:
            c.wait_recv()
        groups = 2 * HALF
        spot = lax.broadcasted_iota(jnp.int32, (groups, SLOT, 128), 1)
        head = rows[:, :, :, 0:128].reshape(groups, SLOT, 128).astype(F32)
        count = jnp.sum(jnp.where(spot == CAP, head, 0.0), axis=1)
        i = lax.broadcasted_iota(jnp.int32, (groups, groups), 0)
        j = lax.broadcasted_iota(jnp.int32, (groups, groups), 1)
        lower = jnp.where(i > j, 1.0, 0.0).astype(BF)
        before = jnp.dot(lower, count.astype(BF), preferred_element_type=F32)
        spot = spot.astype(F32)
        rank = jnp.where(spot < count[:, None, :], before[:, None, :] + spot, -1.0)
        rank = rank.reshape(groups * SLOT, 128)
        lane = lax.broadcasted_iota(jnp.int32, (groups * SLOT, 128), 1)
        for b in range(close.shape[1] // 128):
            hit = rank == (lane + b * 128).astype(F32)
            close[:, b * 128 : (b + 1) * 128] = jnp.where(hit, 1.0, 0.0).astype(BF)
        feats = rows.shape[3] // 2
        for b in range(2):
            part = rows[:, :, :, b * feats : (b + 1) * feats].reshape(groups * SLOT, feats)
            picked = lax.dot_general(
                close[...], part, (((0,), (0,)), ((), ())), preferred_element_type=F32
            )
            mine[b] = picked.astype(BF)
        here = lanes_of(p, feats)
        stage["m"] = []
        for b, full in enumerate((fx, fdy)):
            a = pltpu.make_async_copy(mine.at[b], full.at[:, here], ml.at[b])
            a.start()
            local.append(a)
            for i in (1, 0):
                a = remote(mine.at[b], full.at[:, here], ms.at[i, b], mr.at[i, b], parts[i][1])
                sends.append(a)
                stage["m"].append(a)

    def share():
        for c in stage["m"]:
            c.wait_recv()
        there = lanes_of(parts[1][0], fx.shape[1] // 4)
        for b, full in enumerate((fx, fdy)):
            view = full.at[:, there]
            a = remote(view, view, ms.at[2, b], mr.at[2, b], parts[0][1])
            sends.append(a)
            waits.append(a)

    for u in range(n + 1):
        begin(u)
    first(0)
    flip_first()
    address()
    tokens_plane()
    second(0)
    first(1)
    spread(0)
    second(1)
    first(2)
    tokens_z()
    spread(1)
    second(2)
    first(3)
    spread(2)
    second(3)
    first(4)
    spread(3)
    second(4)
    first(5)
    compact()
    spread(4)
    second(5)
    flip_second()
    spread(5)
    share()
    for c in waits:
        c.wait_recv()
    for c in sends:
        c.wait_send()
    for c in local:
        c.wait()


def gather_all(counts, wg, wu, wd, tokens, cotangent, tags, target):
    cols = wg.shape[2]
    rows, feats = tokens.shape
    n = len(UNITS)
    vm = pl.BlockSpec(memory_space=pltpu.VMEM)
    hbm = pl.BlockSpec(memory_space=pl.ANY)
    dma = pltpu.SemaphoreType.DMA
    out = jax.ShapeDtypeStruct((2, NX, 16 * NZ, cols), BF)
    full = jax.ShapeDtypeStruct((rows, 4 * feats), BF)
    close = jax.ShapeDtypeStruct((2 * HALF * SLOT, rows), BF)
    return pl.pallas_call(
        gather_kernel,
        out_shape=(out, out, out, full, full, close, jax.ShapeDtypeStruct((1, rows), jnp.int32)),
        in_specs=[pl.BlockSpec(memory_space=pltpu.SMEM)] + [hbm] * 5 + [vm],
        out_specs=[hbm] * 5 + [vm] * 2,
        scratch_shapes=[pltpu.VMEM((2, 2, 16 * NZ, u[2]), BF) for u in UNITS]
        + [pltpu.VMEM((4, 2, 16 * NZ, u[2]), BF) for u in UNITS]
        + [
            pltpu.VMEM((2, 2, NX, 16, FLIP[2]), BF),
            pltpu.VMEM((NZ, 2, NX, 16, FLIP[2]), BF),
            pltpu.VMEM((2 * NX, NZ, SLOT, 2 * feats), BF),
            pltpu.VMEM((2 * NX, NZ, SLOT, 2 * feats), BF),
            pltpu.VMEM((2, rows, feats), BF),
            pltpu.VMEM((2 * NX, NZ, SLOT, 2 * feats), BF),
            pltpu.VMEM((rows, feats), BF),
            pltpu.VMEM((rows, feats), BF),
            dma((n + 1,)),
            dma((n + 1,)),
            dma((n, 8)),
            dma((n, 8)),
            dma((n, 4)),
            dma((n, 4)),
            dma((n + 1,)),
            dma((4,)),
            dma((4,)),
            dma((8,)),
            dma((8,)),
            dma((16,)),
            dma((16,)),
            dma((2,)),
            dma((3, 2)),
            dma((3, 2)),
            dma((2,)),
            dma((n + 3,)),
        ],
        compiler_params=pltpu.CompilerParams(
            collective_id=0, has_side_effects=True, vmem_limit_bytes=60 * 1024 * 1024
        ),
        cost_estimate=pl.CostEstimate(flops=0, bytes_accessed=200_000_000, transcendentals=0),
        name="gather_all",
    )(counts, wg, wu, wd, tokens, cotangent, (target * 4 + tags).reshape(1, rows))


def reduce_kernel(
    counts, xf, dyf, dgate, dup, hidden, res, dx, close, og, ou, od, back, *scratch
):
    n = len(UNITS)
    per = 10
    bufs = [scratch[per * u : per * u + per] for u in range(n)]
    ends = [b[7:] for b in bufs] + [scratch[per * n + 3 : per * n + 6]]
    fin, fsum, fgot = scratch[per * n : per * n + 3]
    pin, spread_rows, tmid = scratch[per * n + 6 : per * n + 9]
    made = scratch[per * n + 9 : per * n + 10 + n]
    ys, yr, zs, zr, xs, xr, own, fs, fr, gs, gr, ts, tr, tl, ms, mr, ml = scratch[
        per * n + 10 + n :
    ]
    begins = starts(counts, xf.shape[0])
    p, h, x, z = place()
    at, zline, plane, parts = peers_of(p, h, x, z)
    over = at(1 - h, x, z)
    xline = [at(h, around(x, d, NX), z) for d in range(1, NX)]
    greet(zline + [q for _, q in plane] + [q for _, q in parts])
    pairs = ((xf, dgate), (xf, dup), (dyf, hidden))
    outs = (og, ou, od)
    order = UNITS[::-1]
    sends = []
    arriving, stepping, cross, stage = {}, {}, {}, {}

    def make(u):
        w, c0, width = order[u] if u < n else FLIP
        left, right = pairs[w]
        deep = 32 * NZ

        def body(i, _):
            cut = pl.ds(pl.multiple_of(i * deep, deep), deep)
            v = lax.dot_general(
                left[:, cut],
                right[:, c0 : c0 + width],
                (((0,), (0,)), ((), ())),
                preferred_element_type=F32,
            ).astype(BF)
            y = lax.div(i, 2)
            k = lax.rem(i, 2) * 2
            made[u][y, k] = v[: deep // 2]
            made[u][y, k + 1] = v[deep // 2 :]
            return 0

        lax.fori_loop(0, 4, body, 0)

    def spread(u):
        make(u)
        g = made[u]
        rbuf = bufs[u][0]
        arriving[u] = []
        for d in (2, 1, 3):
            a = remote(
                g.at[:, around(x, d, NX)],
                rbuf.at[d],
                xs.at[u, d],
                xr.at[u, d],
                xline[d - 1],
            )
            arriving[u].append(a)
            sends.append(a)
        a = pltpu.make_async_copy(g.at[:, x], rbuf.at[0], own.at[u])
        a.start()
        arriving[u].append(a)

    def arrive(u):
        for c in arriving[u][:3]:
            c.wait_recv()
        arriving[u][3].wait()

    def binned(terms, marks):
        low = high = None
        for v, m in zip(terms, marks):
            v = v.astype(F32)
            b = v * m
            a = v - b
            low = a if low is None else low + a
            high = b if high is None else high + b
        return low.astype(BF), high.astype(BF)

    xmarks = [
        flag_of(begins, h * HALF + around(x, -d, NX) * NZ + z).astype(F32) for d in range(NX)
    ]

    def bins(u):
        rbuf, zsum = bufs[u][:2]

        def body(i, _):
            y = lax.div(i, NZ)
            r = rows16(lax.rem(i, NZ))
            low, high = binned([rbuf[k, y, r, :] for k in range(NX)], xmarks)
            zsum[0, y, r, :] = low
            zsum[1, y, r, :] = high
            return 0

        lax.fori_loop(0, 2 * NZ, body, 0)

    def first(u):
        zsum, dbuf, tbuf, hbuf = bufs[u][1:5]
        stepping[u] = []
        for i, by in enumerate((1, -1)):
            a = remote(
                zsum.at[:, :, rows16(around(z, 3 * by, NZ)), :],
                tbuf.at[i],
                zs.at[u, i],
                zr.at[u, i],
                zline[by % NZ - 1],
            )
            b = remote(
                zsum.at[:, i, rows16(around(z, 4, NZ)), :],
                hbuf.at[i],
                zs.at[u, 2 + i],
                zr.at[u, 2 + i],
                zline[2 * by % NZ - 1],
            )
            stepping[u].append((a, b))
            sends.extend([a, b])
        for i, by in enumerate((1, -1)):
            a = remote(
                zsum.at[:, :, rows16(around(z, by, NZ)), :],
                dbuf.at[i],
                zs.at[u, 4 + i],
                zr.at[u, 4 + i],
                zline[by % NZ - 1],
            )
            stepping[u].append(a)
            sends.append(a)

    def second(u):
        zsum, dbuf, tbuf, hbuf, obuf, ebuf = bufs[u][1:7]
        waits = stepping[u][2:]
        for i, by in enumerate((1, -1)):
            for c in stepping[u][i]:
                c.wait_recv()
            part = rows16(around(z, 2 * by, NZ))
            for y in range(2):
                v = zsum[:, y, part, :].astype(F32) + tbuf[i, :, y].astype(F32)
                if y == i:
                    v = v + hbuf[i].astype(F32)
                obuf[i, :, y] = v.astype(BF)
            a = remote(
                obuf.at[i], ebuf.at[i], zs.at[u, 6 + i], zr.at[u, 6 + i], zline[2 * by % NZ - 1]
            )
            waits.append(a)
            sends.append(a)
        stepping[u] = waits

    def swap(u):
        for c in stepping[u]:
            c.wait_recv()
        keep, ysend, yin = ends[u]

        def total(y):
            if u == n:
                v = fsum[:, y, x].astype(F32)
                for d in range(1, NX):
                    v = v + fgot[d, :, y].astype(F32)
                return v
            zsum, dbuf, ebuf = bufs[u][1], bufs[u][2], bufs[u][6]
            v = zsum[:, y, rows16(z), :].astype(F32)
            for b in (dbuf, ebuf):
                v = v + b[0, :, y].astype(F32) + b[1, :, y].astype(F32)
            return v

        ysend[...] = total(1 - h).astype(BF)
        cross[u] = remote(ysend, yin, ys.at[u], yr.at[u], over)
        sends.append(cross[u])
        keep[...] = total(h)

    def finish(u):
        w, c0, width = order[u] if u < n else FLIP
        c = pl.ds(c0, width)
        keep, ysend, yin = ends[u]
        cross[u].wait_recv()
        out = outs[w]
        out[2 * h, :, c] = keep[h]
        out[1, :, c] = keep[1 - h] + yin[h].astype(F32)
        out[2 - 2 * h, :, c] = yin[1 - h].astype(F32)

    def flip_spread():
        make(n)
        g = made[n]
        arriving[n] = []
        for d in (4, 3, 5, 2, 6, 1, 7):
            a = remote(
                g.at[:, :, rows16(around(z, d, NZ)), :],
                fin.at[d],
                gs.at[d],
                gr.at[d],
                zline[d - 1],
            )
            arriving[n].append(a)
            sends.append(a)
        a = pltpu.make_async_copy(g.at[:, :, rows16(z), :], fin.at[0], own.at[n])
        a.start()
        arriving[n].append(a)

    def flip_second():
        for c in arriving[n][:-1]:
            c.wait_recv()
        arriving[n][-1].wait()
        marks = [
            flag_of(begins, h * HALF + x * NZ + around(z, -d, NZ)).astype(F32)
            for d in range(NZ)
        ]

        def body(i, _):
            y = lax.div(i, NX)
            k = lax.rem(i, NX)
            low, high = binned([fin[d, y, k] for d in range(NZ)], marks)
            fsum[0, y, k] = low
            fsum[1, y, k] = high
            return 0

        lax.fori_loop(0, 2 * NX, body, 0)
        stepping[n] = []
        for d in (2, 1, 3):
            a = remote(
                fsum.at[:, :, around(x, d, NX)], fgot.at[d], fs.at[d], fr.at[d], xline[d - 1]
            )
            stepping[n].append(a)
            sends.append(a)

    yx = h * NX + x
    feats = res.shape[1] // 4

    def sums_out():
        stage["m"] = []
        for i in (1, 2, 0):
            q, peer = parts[i]
            for b, v in enumerate((res, dx)):
                stage["m"].append(
                    remote(v.at[:, lanes_of(q, feats)], pin.at[i, b], ms.at[i, b], mr.at[i, b], peer)
                )
        here = lanes_of(p, feats)
        stage["ml"] = []
        for b, v in enumerate((res, dx)):
            a = pltpu.make_async_copy(v.at[:, here], pin.at[3, b], ml.at[b])
            a.start()
            stage["ml"].append(a)

    def widen():
        for c in stage["ml"]:
            c.wait()
        for c in stage["m"]:
            c.wait_recv()
        sends.extend(stage["m"])
        for b in range(2):
            v = pin[3, b].astype(F32)
            for i in range(3):
                v = v + pin[i, b].astype(F32)
            v = jnp.dot(close[...], v.astype(BF), preferred_element_type=F32).astype(BF)
            spread_rows[:, :, :, b * feats : (b + 1) * feats] = v.reshape(
                2 * NX, NZ, SLOT, feats
            )
        stage["z"] = []
        for d in (4, 3, 5, 2, 6, 1, 7):
            stage["z"].append(
                remote(
                    spread_rows.at[:, around(z, d, NZ)],
                    tmid.at[z],
                    ts.at[d],
                    tr.at[d],
                    zline[d - 1],
                )
            )
        sends.extend(stage["z"])
        a = pltpu.make_async_copy(spread_rows.at[:, z], tmid.at[z], tl.at[0])
        a.start()
        stage["zl"] = a

    def homeward():
        stage["zl"].wait()
        for c in stage["z"]:
            c.wait_recv()
        stage["p"] = []
        for d in range(1, 2 * NX):
            k, peer = plane[d - 1]
            stage["p"].append(
                remote(tmid.at[:, k], back.at[yx], ts.at[NZ + d], tr.at[NZ + d], peer)
            )
        sends.extend(stage["p"])
        a = pltpu.make_async_copy(tmid.at[:, yx], back.at[yx], tl.at[1])
        a.start()
        stage["pl"] = a

    sums_out()
    spread(0)
    flip_spread()
    spread(1)
    spread(2)
    spread(3)
    spread(4)
    spread(5)
    arrive(0)
    bins(0)
    first(0)
    widen()
    second(0)
    arrive(1)
    bins(1)
    first(1)
    swap(0)
    second(1)
    arrive(2)
    bins(2)
    first(2)
    swap(1)
    second(2)
    homeward()
    flip_second()
    arrive(3)
    bins(3)
    first(3)
    swap(2)
    second(3)
    arrive(4)
    bins(4)
    first(4)
    swap(3)
    second(4)
    swap(n)
    arrive(5)
    bins(5)
    first(5)
    swap(4)
    second(5)
    swap(n - 1)
    for u in range(n + 1):
        finish((n + u) % (n + 1))
    stage["pl"].wait()
    for c in stage["p"]:
        c.wait_recv()
    for c in sends:
        c.wait_send()


def reduce_all(counts, xf, dyf, dgate, dup, hidden, res, dx, close):
    cols = dgate.shape[1]
    rows = res.shape[0]
    feats = res.shape[1] // 4
    n = len(UNITS)
    vm = pl.BlockSpec(memory_space=pltpu.VMEM)
    hbm = pl.BlockSpec(memory_space=pl.ANY)
    dma = pltpu.SemaphoreType.DMA
    out = jax.ShapeDtypeStruct((3, 16, cols), F32)
    back = jax.ShapeDtypeStruct((2 * NX, NZ, SLOT, 2 * feats), BF)
    bufs = []
    for _, _, wide in UNITS[::-1]:
        bufs += [
            pltpu.VMEM((NX, 2, 16 * NZ, wide), BF),
            pltpu.VMEM((2, 2, 16 * NZ, wide), BF),
            pltpu.VMEM((2, 2, 2, 16, wide), BF),
            pltpu.VMEM((2, 2, 2, 16, wide), BF),
            pltpu.VMEM((2, 2, 16, wide), BF),
            pltpu.VMEM((2, 2, 2, 16, wide), BF),
            pltpu.VMEM((2, 2, 2, 16, wide), BF),
            pltpu.VMEM((2, 16, wide), F32),
            pltpu.VMEM((2, 16, wide), BF),
            pltpu.VMEM((2, 16, wide), BF),
        ]
    wide = FLIP[2]
    bufs += [
        pltpu.VMEM((NZ, 2, NX, 16, wide), BF),
        pltpu.VMEM((2, 2, NX, 16, wide), BF),
        pltpu.VMEM((NX, 2, 2, 16, wide), BF),
        pltpu.VMEM((2, 16, wide), F32),
        pltpu.VMEM((2, 16, wide), BF),
        pltpu.VMEM((2, 16, wide), BF),
    ]
    return pl.pallas_call(
        reduce_kernel,
        out_shape=(out, out, out, back),
        in_specs=[pl.BlockSpec(memory_space=pltpu.SMEM)] + [vm] * 5 + [hbm] * 2 + [vm],
        out_specs=[vm] * 3 + [hbm],
        scratch_shapes=bufs
        + [
            pltpu.VMEM((4, 2, rows, feats), BF),
            pltpu.VMEM((2 * NX, NZ, SLOT, 2 * feats), BF),
            pltpu.VMEM((NZ, 2 * NX, SLOT, 2 * feats), BF),
        ]
        + [pltpu.VMEM((2, NX, 16 * NZ, u[2]), BF) for u in UNITS[::-1] + (FLIP,)]
        + [
            dma((n + 1,)),
            dma((n + 1,)),
            dma((n, 8)),
            dma((n, 8)),
            dma((n, 4)),
            dma((n, 4)),
            dma((n + 1,)),
            dma((4,)),
            dma((4,)),
            dma((8,)),
            dma((8,)),
            dma((16,)),
            dma((16,)),
            dma((2,)),
            dma((3, 2)),
            dma((3, 2)),
            dma((2,)),
        ],
        compiler_params=pltpu.CompilerParams(
            collective_id=1, has_side_effects=True, vmem_limit_bytes=48 * 1024 * 1024
        ),
        cost_estimate=pl.CostEstimate(flops=0, bytes_accessed=200_000_000, transcendentals=0),
        name="reduce_all",
    )(counts, xf, dyf, dgate, dup, hidden, res, dx, close)


def project_rows(x, dy, wg, wu, wd):
    gate = jnp.dot(x, wg, preferred_element_type=F32)
    up = jnp.dot(x, wu, preferred_element_type=F32)
    sig = jax.nn.sigmoid(gate)
    silu = gate * sig
    hidden = (silu * up).astype(BF)
    out = lax.dot_general(hidden, wd, (((1,), (1,)), ((), ())), preferred_element_type=F32)
    dhidden = jnp.dot(dy, wd, preferred_element_type=F32)
    dgate = (dhidden * up * sig * (1.0 + gate * (1.0 - sig))).astype(BF)
    dup = (dhidden * silu).astype(BF)
    dx = lax.dot_general(dgate, wg, (((1,), (1,)), ((), ())), preferred_element_type=F32)
    dx = dx + lax.dot_general(dup, wu, (((1,), (1,)), ((), ())), preferred_element_type=F32)
    return out.astype(BF), dx.astype(BF), hidden, dgate, dup


def shards(tokens, cotangent, tags, counts, target, gate_weight, up_weight, down_weight):
    feats = tokens.shape[1]
    w_gate, w_up, w_down, full_x, full_dy, close, position = gather_all(
        counts, gate_weight, up_weight, down_weight, tokens, cotangent, tags, target
    )
    depth = full_x.shape[1]
    w_gate, w_up, w_down = (w.reshape(depth, -1) for w in (w_gate, w_up, w_down))
    out, dx, hidden, dgate, dup = project_rows(full_x, full_dy, w_gate, w_up, w_down)
    gate_grad, up_grad, down_grad, back = reduce_all(
        counts, full_x, full_dy, dgate, dup, hidden, out, dx, close
    )
    wide = close.shape[0]
    lanes = jnp.arange(wide, dtype=jnp.int32)
    out_of = (position[0][:, None] == lanes[None, :]).astype(BF)
    result = jnp.dot(out_of, back.reshape(wide, 2 * feats), preferred_element_type=F32).astype(BF)
    return result[:, :feats], result[:, feats:], gate_grad, up_grad, down_grad


def solution(mesh):
    in_specs = (
        P("group", "mp"),
        P("group", "mp"),
        P("group"),
        P(),
        P("group"),
        P(None, "group", "mp"),
        P(None, "group", "mp"),
        P(None, "group", "mp"),
    )
    out_specs = (
        P("group", "mp"),
        P("group", "mp"),
        P(None, "group", "mp"),
        P(None, "group", "mp"),
        P(None, "group", "mp"),
    )
    return jax.shard_map(shards, mesh=mesh, in_specs=in_specs, out_specs=out_specs, check_vma=False)
```

```python
import jax
import jax.numpy as jnp
from jax import lax
from jax.experimental import pallas as pl
from jax.experimental.pallas import tpu as pltpu
from jax.sharding import PartitionSpec as P

BF = jnp.bfloat16
F32 = jnp.float32
NX, NZ = 4, 8
HALF = NX * NZ
CAP = 12
SLOT = 16
UNITS = (
    (0, 0, 384),
    (0, 384, 640),
    (1, 0, 512),
    (1, 512, 512),
    (2, 0, 384),
    (2, 384, 256),
)
FLIP = (2, 640, 384)


def place():
    g = lax.axis_index("group")
    p = lax.axis_index("mp")
    h = lax.div(g, HALF)
    x = lax.rem(lax.div(g, NZ), NX)
    z = lax.rem(g, NZ)
    return p, h, x, z


def around(v, by, size):
    return lax.rem(v + (by + size), size)


def rows16(c):
    return pl.ds(pl.multiple_of(c * 16, 16), 16)


def greet(peers):
    barrier = pltpu.get_barrier_semaphore()
    for peer in peers:
        pl.semaphore_signal(barrier, inc=1, device_id=peer, device_id_type=pl.DeviceIdType.MESH)
    pl.semaphore_wait(barrier, len(peers))


def remote(src, dst, send, recv, peer):
    copy = pltpu.make_async_remote_copy(
        src_ref=src,
        dst_ref=dst,
        send_sem=send,
        recv_sem=recv,
        device_id=peer,
        device_id_type=pl.DeviceIdType.MESH,
    )
    copy.start()
    return copy


def peers_of(p, h, x, z):
    def at(hh, xx, zz):
        return (hh * HALF + xx * NZ + zz, p)

    zline = [at(h, x, around(z, d, NZ)) for d in range(1, NZ)]
    yx = h * NX + x
    plane = []
    for d in range(1, 2 * NX):
        k = around(yx, d, 2 * NX)
        plane.append((k, at(lax.div(k, NX), lax.rem(k, NX), z)))
    g = h * HALF + x * NZ + z
    core = p + 1 - 2 * lax.rem(p, 2)
    opposite = around(p, 2, 4)
    both = around(core, 2, 4)
    parts = [(core, (g, core)), (opposite, (g, opposite)), (both, (g, both))]
    return at, zline, plane, parts


def starts(counts, rows):
    b = lax.div(counts[0], rows)
    return b, lax.div(counts[0] + counts[1], rows)


def flag_of(begin, g):
    b, c = begin
    mod = (g >= b).astype(jnp.int32) + (g >= c).astype(jnp.int32)
    return jnp.clip(mod - lax.div(g, HALF), 0, 1)


def lanes_of(p, feats):
    return pl.ds(pl.multiple_of(p * feats, 128), feats)


def gather_kernel(
    counts, wg, wu, wd, xhbm, dyhbm, code, og, ou, od, fx, fdy, close, into, *scratch
):
    n = len(UNITS)
    zbuf, sbuf = scratch[:n], scratch[n : 2 * n]
    begins = starts(counts, xhbm.shape[0])
    fbuf, fsend, tmid, rows, mine, tok, xin, dyin = scratch[2 * n : 2 * n + 8]
    ys, yr, zs, zr, xs, xr, own, fs, fr, gs, gr, ts, tr, tl, ms, mr, ml, il = scratch[
        2 * n + 8 :
    ]
    p, h, x, z = place()
    at, zline, plane, parts = peers_of(p, h, x, z)
    over = at(1 - h, x, z)
    xline = [at(h, around(x, d, NX), z) for d in range(1, NX)]
    loads = [pltpu.make_async_copy(xhbm, xin, il.at[0]), pltpu.make_async_copy(dyhbm, dyin, il.at[1])]
    for c in loads:
        c.start()
    placed = {}
    for u in range(n + 1):
        w, c0, width = UNITS[u] if u < n else FLIP
        ours = zbuf[u].at[:, h, rows16(z), :] if u < n else fbuf.at[:, h, x]
        placed[u] = pltpu.make_async_copy(
            (wg, wu, wd)[w].at[pl.ds(h, 2), :, pl.ds(c0, width)], ours, il.at[2 + u]
        )
        placed[u].start()
    greet(zline + [q for _, q in plane] + [q for _, q in parts])
    weights = (wg, wu, wd)
    outs = (og, ou, od)
    sends, waits, local = [], [], []
    cross, near, later = {}, {}, {}

    def begin(u):
        w, c0, width = UNITS[u] if u < n else FLIP
        c = pl.ds(c0, width)
        if u < n:
            theirs = zbuf[u].at[:, h, rows16(z), :]
        else:
            theirs = fbuf.at[:, h, x]
        cross[u] = remote(
            weights[w].at[pl.ds(1 - h, 2), :, c], theirs, ys.at[u], yr.at[u], over
        )
        sends.append(cross[u])

    def first(u):
        placed[u].wait()
        cross[u].wait_recv()
        v = zbuf[u].at[:, :, rows16(z), :]
        hops = ((2, 2), (3, -2), (0, 1), (1, -1))
        near[u] = {
            i: remote(v, v, zs.at[u, i], zr.at[u, i], zline[d % NZ - 1]) for i, d in hops
        }
        sends.extend(near[u].values())

    def second(u):
        later[u] = [near[u][0], near[u][1]]
        for i, by in enumerate((1, -1)):
            near[u][2 + i].wait_recv()
            chunk = rows16(around(z, -2 * by, NZ))
            v = zbuf[u].at[:, :, chunk, :]
            a = remote(v, v, zs.at[u, 4 + i], zr.at[u, 4 + i], zline[by % NZ - 1])
            v = zbuf[u].at[:, i, chunk, :]
            b = remote(v, v, zs.at[u, 6 + i], zr.at[u, 6 + i], zline[2 * by % NZ - 1])
            later[u].extend([a, b])
            sends.extend([a, b])

    def spread(u):
        for c in later[u]:
            c.wait_recv()
        w, c0, width = UNITS[u]
        out = outs[w].at[:, x, :, pl.ds(c0, width)]
        for d in (2, 1, 3, 0):
            f = flag_of(begins, h * HALF + around(x, d, NX) * NZ + z)
            sbuf[u][d] = zbuf[u][f]
            if d == 0:
                a = pltpu.make_async_copy(sbuf[u].at[0], out, own.at[u])
                a.start()
                local.append(a)
            else:
                a = remote(sbuf[u].at[d], out, xs.at[u, d], xr.at[u, d], xline[d - 1])
                sends.append(a)
                waits.append(a)

    def flip_first():
        placed[n].wait()
        cross[n].wait_recv()
        v = fbuf.at[:, :, x]
        near[n] = [remote(v, v, fs.at[d], fr.at[d], xline[d - 1]) for d in (2, 1, 3)]
        sends.extend(near[n])

    def flip_second():
        for c in near[n]:
            c.wait_recv()
        w, c0, width = FLIP
        out = outs[w].at[:, :, rows16(z), pl.ds(c0, width)]
        for d in (4, 3, 5, 2, 6, 1, 7, 0):
            f = flag_of(begins, h * HALF + x * NZ + around(z, d, NZ))
            fsend[d] = fbuf[f]
            if d == 0:
                a = pltpu.make_async_copy(fsend.at[0], out, own.at[n])
                a.start()
                local.append(a)
            else:
                a = remote(fsend.at[d], out, gs.at[d], gr.at[d], zline[d - 1])
                sends.append(a)
                waits.append(a)

    yx = h * NX + x
    stage = {}

    def address():
        count = xin.shape[0]
        groups = 2 * HALF
        wide = groups * SLOT
        for c in loads:
            c.wait()
        kind = code[...] & 3
        base = jnp.where(kind == 0, 0, jnp.where(kind == 1, begins[0], begins[1]))
        dest = base + lax.shift_right_logical(code[...], 2)
        spread_dest = jnp.broadcast_to(dest.astype(F32), (count, count))
        i = lax.broadcasted_iota(jnp.int32, (count, count), 0)
        j = lax.broadcasted_iota(jnp.int32, (count, count), 1)
        same = (spread_dest == spread_dest.T) & (i < j)
        slot = jnp.sum(jnp.where(same, 1.0, 0.0), axis=0, keepdims=True)
        place_row = dest * SLOT + slot.astype(jnp.int32)
        i = lax.broadcasted_iota(jnp.int32, (wide, count), 0)
        into[...] = jnp.where(i == place_row, 1.0, 0.0).astype(BF)
        feats = xin.shape[1]
        i = lax.broadcasted_iota(jnp.int32, (groups, count), 0)
        goes = jnp.where(i == dest, 1.0, 0.0).astype(BF)
        sent = jnp.dot(goes, jnp.ones((count, feats), BF), preferred_element_type=F32)
        spot = lax.broadcasted_iota(jnp.int32, (groups, SLOT, feats), 1)
        for b, v in enumerate((xin, dyin)):
            part = jnp.dot(into[...], v[...], preferred_element_type=F32)
            part = part.reshape(groups, SLOT, feats)
            if b == 0:
                part = jnp.where(spot >= CAP, sent[:, None, :], part)
            tok[:, :, :, b * feats : (b + 1) * feats] = part.astype(BF).reshape(
                2 * NX, NZ, SLOT, feats
            )

    def tokens_plane():
        stage["p"] = []
        for d in range(1, 2 * NX):
            k, peer = plane[d - 1]
            stage["p"].append(
                remote(tok.at[k], tmid.at[yx], ts.at[NZ + d], tr.at[NZ + d], peer)
            )
        sends.extend(stage["p"])
        a = pltpu.make_async_copy(tok.at[yx], tmid.at[yx], tl.at[1])
        a.start()
        stage["pl"] = a

    def tokens_z():
        stage["pl"].wait()
        for c in stage["p"]:
            c.wait_recv()
        stage["z"] = []
        for d in (4, 3, 5, 2, 6, 1, 7):
            to = around(z, d, NZ)
            stage["z"].append(
                remote(tmid.at[:, to], rows.at[:, z], ts.at[d], tr.at[d], zline[d - 1])
            )
        sends.extend(stage["z"])
        a = pltpu.make_async_copy(tmid.at[:, z], rows.at[:, z], tl.at[0])
        a.start()
        stage["zl"] = a

    def compact():
        stage["zl"].wait()
        for c in stage["z"]:
            c.wait_recv()
        groups = 2 * HALF
        spot = lax.broadcasted_iota(jnp.int32, (groups, SLOT, 128), 1)
        head = rows[:, :, :, 0:128].reshape(groups, SLOT, 128).astype(F32)
        count = jnp.sum(jnp.where(spot == CAP, head, 0.0), axis=1)
        i = lax.broadcasted_iota(jnp.int32, (groups, groups), 0)
        j = lax.broadcasted_iota(jnp.int32, (groups, groups), 1)
        lower = jnp.where(i > j, 1.0, 0.0).astype(BF)
        before = jnp.dot(lower, count.astype(BF), preferred_element_type=F32)
        spot = spot.astype(F32)
        rank = jnp.where(spot < count[:, None, :], before[:, None, :] + spot, -1.0)
        rank = rank.reshape(groups * SLOT, 128)
        lane = lax.broadcasted_iota(jnp.int32, (groups * SLOT, 128), 1)
        for b in range(close.shape[1] // 128):
            hit = rank == (lane + b * 128).astype(F32)
            close[:, b * 128 : (b + 1) * 128] = jnp.where(hit, 1.0, 0.0).astype(BF)
        feats = rows.shape[3] // 2
        for b in range(2):
            part = rows[:, :, :, b * feats : (b + 1) * feats].reshape(groups * SLOT, feats)
            picked = lax.dot_general(
                close[...], part, (((0,), (0,)), ((), ())), preferred_element_type=F32
            )
            mine[b] = picked.astype(BF)
        here = lanes_of(p, feats)
        stage["m"] = []
        for b, full in enumerate((fx, fdy)):
            a = pltpu.make_async_copy(mine.at[b], full.at[:, here], ml.at[b])
            a.start()
            local.append(a)
            for i in (1, 0):
                a = remote(mine.at[b], full.at[:, here], ms.at[i, b], mr.at[i, b], parts[i][1])
                sends.append(a)
                stage["m"].append(a)

    def share():
        for c in stage["m"]:
            c.wait_recv()
        there = lanes_of(parts[1][0], fx.shape[1] // 4)
        for b, full in enumerate((fx, fdy)):
            view = full.at[:, there]
            a = remote(view, view, ms.at[2, b], mr.at[2, b], parts[0][1])
            sends.append(a)
            waits.append(a)

    for u in range(n + 1):
        begin(u)
    first(0)
    flip_first()
    address()
    tokens_plane()
    second(0)
    first(1)
    spread(0)
    second(1)
    first(2)
    tokens_z()
    spread(1)
    second(2)
    first(3)
    spread(2)
    second(3)
    first(4)
    spread(3)
    second(4)
    first(5)
    compact()
    spread(4)
    second(5)
    flip_second()
    spread(5)
    share()
    for c in waits:
        c.wait_recv()
    for c in sends:
        c.wait_send()
    for c in local:
        c.wait()


def gather_all(counts, wg, wu, wd, tokens, cotangent, tags, target):
    cols = wg.shape[2]
    rows, feats = tokens.shape
    n = len(UNITS)
    vm = pl.BlockSpec(memory_space=pltpu.VMEM)
    hbm = pl.BlockSpec(memory_space=pl.ANY)
    dma = pltpu.SemaphoreType.DMA
    out = jax.ShapeDtypeStruct((2, NX, 16 * NZ, cols), BF)
    full = jax.ShapeDtypeStruct((rows, 4 * feats), BF)
    close = jax.ShapeDtypeStruct((2 * HALF * SLOT, rows), BF)
    return pl.pallas_call(
        gather_kernel,
        out_shape=(out, out, out, full, full, close, close),
        in_specs=[pl.BlockSpec(memory_space=pltpu.SMEM)] + [hbm] * 5 + [vm],
        out_specs=[hbm] * 5 + [vm] * 2,
        scratch_shapes=[pltpu.VMEM((2, 2, 16 * NZ, u[2]), BF) for u in UNITS]
        + [pltpu.VMEM((4, 2, 16 * NZ, u[2]), BF) for u in UNITS]
        + [
            pltpu.VMEM((2, 2, NX, 16, FLIP[2]), BF),
            pltpu.VMEM((NZ, 2, NX, 16, FLIP[2]), BF),
            pltpu.VMEM((2 * NX, NZ, SLOT, 2 * feats), BF),
            pltpu.VMEM((2 * NX, NZ, SLOT, 2 * feats), BF),
            pltpu.VMEM((2, rows, feats), BF),
            pltpu.VMEM((2 * NX, NZ, SLOT, 2 * feats), BF),
            pltpu.VMEM((rows, feats), BF),
            pltpu.VMEM((rows, feats), BF),
            dma((n + 1,)),
            dma((n + 1,)),
            dma((n, 8)),
            dma((n, 8)),
            dma((n, 4)),
            dma((n, 4)),
            dma((n + 1,)),
            dma((4,)),
            dma((4,)),
            dma((8,)),
            dma((8,)),
            dma((16,)),
            dma((16,)),
            dma((2,)),
            dma((3, 2)),
            dma((3, 2)),
            dma((2,)),
            dma((n + 3,)),
        ],
        compiler_params=pltpu.CompilerParams(
            collective_id=0, has_side_effects=True, vmem_limit_bytes=60 * 1024 * 1024
        ),
        cost_estimate=pl.CostEstimate(flops=0, bytes_accessed=200_000_000, transcendentals=0),
        name="gather_all",
    )(counts, wg, wu, wd, tokens, cotangent, (target * 4 + tags).reshape(1, rows))


def reduce_kernel(
    counts, xf, dyf, dgate, dup, hidden, res, dx, close, og, ou, od, back, *scratch
):
    n = len(UNITS)
    per = 10
    bufs = [scratch[per * u : per * u + per] for u in range(n)]
    ends = [b[7:] for b in bufs] + [scratch[per * n + 3 : per * n + 6]]
    fin, fsum, fgot = scratch[per * n : per * n + 3]
    pin, spread_rows, tmid = scratch[per * n + 6 : per * n + 9]
    made = scratch[per * n + 9 : per * n + 10 + n]
    ys, yr, zs, zr, xs, xr, own, fs, fr, gs, gr, ts, tr, tl, ms, mr, ml = scratch[
        per * n + 10 + n :
    ]
    begins = starts(counts, xf.shape[0])
    p, h, x, z = place()
    at, zline, plane, parts = peers_of(p, h, x, z)
    over = at(1 - h, x, z)
    xline = [at(h, around(x, d, NX), z) for d in range(1, NX)]
    greet(zline + [q for _, q in plane] + [q for _, q in parts])
    pairs = ((xf, dgate), (xf, dup), (dyf, hidden))
    outs = (og, ou, od)
    order = UNITS[::-1]
    sends = []
    arriving, stepping, cross, stage = {}, {}, {}, {}

    def make(u):
        w, c0, width = order[u] if u < n else FLIP
        left, right = pairs[w]
        deep = 32 * NZ

        def body(i, _):
            cut = pl.ds(pl.multiple_of(i * deep, deep), deep)
            v = lax.dot_general(
                left[:, cut],
                right[:, c0 : c0 + width],
                (((0,), (0,)), ((), ())),
                preferred_element_type=F32,
            ).astype(BF)
            y = lax.div(i, 2)
            k = lax.rem(i, 2) * 2
            made[u][y, k] = v[: deep // 2]
            made[u][y, k + 1] = v[deep // 2 :]
            return 0

        lax.fori_loop(0, 4, body, 0)

    def spread(u):
        make(u)
        g = made[u]
        rbuf = bufs[u][0]
        arriving[u] = []
        for d in (2, 1, 3):
            a = remote(
                g.at[:, around(x, d, NX)],
                rbuf.at[d],
                xs.at[u, d],
                xr.at[u, d],
                xline[d - 1],
            )
            arriving[u].append(a)
            sends.append(a)
        a = pltpu.make_async_copy(g.at[:, x], rbuf.at[0], own.at[u])
        a.start()
        arriving[u].append(a)

    def arrive(u):
        for c in arriving[u][:3]:
            c.wait_recv()
        arriving[u][3].wait()

    def binned(terms, marks):
        low = high = None
        for v, m in zip(terms, marks):
            v = v.astype(F32)
            b = v * m
            a = v - b
            low = a if low is None else low + a
            high = b if high is None else high + b
        return low.astype(BF), high.astype(BF)

    xmarks = [
        flag_of(begins, h * HALF + around(x, -d, NX) * NZ + z).astype(F32) for d in range(NX)
    ]

    def bins(u):
        rbuf, zsum = bufs[u][:2]

        def body(i, _):
            y = lax.div(i, NZ)
            r = rows16(lax.rem(i, NZ))
            low, high = binned([rbuf[k, y, r, :] for k in range(NX)], xmarks)
            zsum[0, y, r, :] = low
            zsum[1, y, r, :] = high
            return 0

        lax.fori_loop(0, 2 * NZ, body, 0)

    def first(u):
        zsum, dbuf, tbuf, hbuf = bufs[u][1:5]
        stepping[u] = []
        for i, by in enumerate((1, -1)):
            a = remote(
                zsum.at[:, :, rows16(around(z, 3 * by, NZ)), :],
                tbuf.at[i],
                zs.at[u, i],
                zr.at[u, i],
                zline[by % NZ - 1],
            )
            b = remote(
                zsum.at[:, i, rows16(around(z, 4, NZ)), :],
                hbuf.at[i],
                zs.at[u, 2 + i],
                zr.at[u, 2 + i],
                zline[2 * by % NZ - 1],
            )
            stepping[u].append((a, b))
            sends.extend([a, b])
        for i, by in enumerate((1, -1)):
            a = remote(
                zsum.at[:, :, rows16(around(z, by, NZ)), :],
                dbuf.at[i],
                zs.at[u, 4 + i],
                zr.at[u, 4 + i],
                zline[by % NZ - 1],
            )
            stepping[u].append(a)
            sends.append(a)

    def second(u):
        zsum, dbuf, tbuf, hbuf, obuf, ebuf = bufs[u][1:7]
        waits = stepping[u][2:]
        for i, by in enumerate((1, -1)):
            for c in stepping[u][i]:
                c.wait_recv()
            part = rows16(around(z, 2 * by, NZ))
            for y in range(2):
                v = zsum[:, y, part, :].astype(F32) + tbuf[i, :, y].astype(F32)
                if y == i:
                    v = v + hbuf[i].astype(F32)
                obuf[i, :, y] = v.astype(BF)
            a = remote(
                obuf.at[i], ebuf.at[i], zs.at[u, 6 + i], zr.at[u, 6 + i], zline[2 * by % NZ - 1]
            )
            waits.append(a)
            sends.append(a)
        stepping[u] = waits

    def swap(u):
        for c in stepping[u]:
            c.wait_recv()
        keep, ysend, yin = ends[u]

        def total(y):
            if u == n:
                v = fsum[:, y, x].astype(F32)
                for d in range(1, NX):
                    v = v + fgot[d, :, y].astype(F32)
                return v
            zsum, dbuf, ebuf = bufs[u][1], bufs[u][2], bufs[u][6]
            v = zsum[:, y, rows16(z), :].astype(F32)
            for b in (dbuf, ebuf):
                v = v + b[0, :, y].astype(F32) + b[1, :, y].astype(F32)
            return v

        ysend[...] = total(1 - h).astype(BF)
        cross[u] = remote(ysend, yin, ys.at[u], yr.at[u], over)
        sends.append(cross[u])
        keep[...] = total(h)

    def finish(u):
        w, c0, width = order[u] if u < n else FLIP
        c = pl.ds(c0, width)
        keep, ysend, yin = ends[u]
        cross[u].wait_recv()
        out = outs[w]
        out[2 * h, :, c] = keep[h]
        out[1, :, c] = keep[1 - h] + yin[h].astype(F32)
        out[2 - 2 * h, :, c] = yin[1 - h].astype(F32)

    def flip_spread():
        make(n)
        g = made[n]
        arriving[n] = []
        for d in (4, 3, 5, 2, 6, 1, 7):
            a = remote(
                g.at[:, :, rows16(around(z, d, NZ)), :],
                fin.at[d],
                gs.at[d],
                gr.at[d],
                zline[d - 1],
            )
            arriving[n].append(a)
            sends.append(a)
        a = pltpu.make_async_copy(g.at[:, :, rows16(z), :], fin.at[0], own.at[n])
        a.start()
        arriving[n].append(a)

    def flip_second():
        for c in arriving[n][:-1]:
            c.wait_recv()
        arriving[n][-1].wait()
        marks = [
            flag_of(begins, h * HALF + x * NZ + around(z, -d, NZ)).astype(F32)
            for d in range(NZ)
        ]

        def body(i, _):
            y = lax.div(i, NX)
            k = lax.rem(i, NX)
            low, high = binned([fin[d, y, k] for d in range(NZ)], marks)
            fsum[0, y, k] = low
            fsum[1, y, k] = high
            return 0

        lax.fori_loop(0, 2 * NX, body, 0)
        stepping[n] = []
        for d in (2, 1, 3):
            a = remote(
                fsum.at[:, :, around(x, d, NX)], fgot.at[d], fs.at[d], fr.at[d], xline[d - 1]
            )
            stepping[n].append(a)
            sends.append(a)

    yx = h * NX + x
    feats = res.shape[1] // 4

    def sums_out():
        stage["m"] = []
        for i in (1, 2, 0):
            q, peer = parts[i]
            for b, v in enumerate((res, dx)):
                stage["m"].append(
                    remote(v.at[:, lanes_of(q, feats)], pin.at[i, b], ms.at[i, b], mr.at[i, b], peer)
                )
        here = lanes_of(p, feats)
        stage["ml"] = []
        for b, v in enumerate((res, dx)):
            a = pltpu.make_async_copy(v.at[:, here], pin.at[3, b], ml.at[b])
            a.start()
            stage["ml"].append(a)

    def widen():
        for c in stage["ml"]:
            c.wait()
        for c in stage["m"]:
            c.wait_recv()
        sends.extend(stage["m"])
        for b in range(2):
            v = pin[3, b].astype(F32)
            for i in range(3):
                v = v + pin[i, b].astype(F32)
            v = jnp.dot(close[...], v.astype(BF), preferred_element_type=F32).astype(BF)
            spread_rows[:, :, :, b * feats : (b + 1) * feats] = v.reshape(
                2 * NX, NZ, SLOT, feats
            )
        stage["z"] = []
        for d in (4, 3, 5, 2, 6, 1, 7):
            stage["z"].append(
                remote(
                    spread_rows.at[:, around(z, d, NZ)],
                    tmid.at[z],
                    ts.at[d],
                    tr.at[d],
                    zline[d - 1],
                )
            )
        sends.extend(stage["z"])
        a = pltpu.make_async_copy(spread_rows.at[:, z], tmid.at[z], tl.at[0])
        a.start()
        stage["zl"] = a

    def homeward():
        stage["zl"].wait()
        for c in stage["z"]:
            c.wait_recv()
        stage["p"] = []
        for d in range(1, 2 * NX):
            k, peer = plane[d - 1]
            stage["p"].append(
                remote(tmid.at[:, k], back.at[yx], ts.at[NZ + d], tr.at[NZ + d], peer)
            )
        sends.extend(stage["p"])
        a = pltpu.make_async_copy(tmid.at[:, yx], back.at[yx], tl.at[1])
        a.start()
        stage["pl"] = a

    sums_out()
    spread(0)
    flip_spread()
    spread(1)
    spread(2)
    spread(3)
    spread(4)
    spread(5)
    arrive(0)
    bins(0)
    first(0)
    widen()
    second(0)
    arrive(1)
    bins(1)
    first(1)
    swap(0)
    second(1)
    arrive(2)
    bins(2)
    first(2)
    swap(1)
    second(2)
    homeward()
    flip_second()
    arrive(3)
    bins(3)
    first(3)
    swap(2)
    second(3)
    arrive(4)
    bins(4)
    first(4)
    swap(3)
    second(4)
    swap(n)
    arrive(5)
    bins(5)
    first(5)
    swap(4)
    second(5)
    swap(n - 1)
    for u in range(n + 1):
        finish((n + u) % (n + 1))
    stage["pl"].wait()
    for c in stage["p"]:
        c.wait_recv()
    for c in sends:
        c.wait_send()


def reduce_all(counts, xf, dyf, dgate, dup, hidden, res, dx, close):
    cols = dgate.shape[1]
    rows = res.shape[0]
    feats = res.shape[1] // 4
    n = len(UNITS)
    vm = pl.BlockSpec(memory_space=pltpu.VMEM)
    hbm = pl.BlockSpec(memory_space=pl.ANY)
    dma = pltpu.SemaphoreType.DMA
    out = jax.ShapeDtypeStruct((3, 16, cols), F32)
    back = jax.ShapeDtypeStruct((2 * NX, NZ, SLOT, 2 * feats), BF)
    bufs = []
    for _, _, wide in UNITS[::-1]:
        bufs += [
            pltpu.VMEM((NX, 2, 16 * NZ, wide), BF),
            pltpu.VMEM((2, 2, 16 * NZ, wide), BF),
            pltpu.VMEM((2, 2, 2, 16, wide), BF),
            pltpu.VMEM((2, 2, 2, 16, wide), BF),
            pltpu.VMEM((2, 2, 16, wide), BF),
            pltpu.VMEM((2, 2, 2, 16, wide), BF),
            pltpu.VMEM((2, 2, 2, 16, wide), BF),
            pltpu.VMEM((2, 16, wide), F32),
            pltpu.VMEM((2, 16, wide), BF),
            pltpu.VMEM((2, 16, wide), BF),
        ]
    wide = FLIP[2]
    bufs += [
        pltpu.VMEM((NZ, 2, NX, 16, wide), BF),
        pltpu.VMEM((2, 2, NX, 16, wide), BF),
        pltpu.VMEM((NX, 2, 2, 16, wide), BF),
        pltpu.VMEM((2, 16, wide), F32),
        pltpu.VMEM((2, 16, wide), BF),
        pltpu.VMEM((2, 16, wide), BF),
    ]
    return pl.pallas_call(
        reduce_kernel,
        out_shape=(out, out, out, back),
        in_specs=[pl.BlockSpec(memory_space=pltpu.SMEM)] + [vm] * 5 + [hbm] * 2 + [vm],
        out_specs=[vm] * 3 + [hbm],
        scratch_shapes=bufs
        + [
            pltpu.VMEM((4, 2, rows, feats), BF),
            pltpu.VMEM((2 * NX, NZ, SLOT, 2 * feats), BF),
            pltpu.VMEM((NZ, 2 * NX, SLOT, 2 * feats), BF),
        ]
        + [pltpu.VMEM((2, NX, 16 * NZ, u[2]), BF) for u in UNITS[::-1] + (FLIP,)]
        + [
            dma((n + 1,)),
            dma((n + 1,)),
            dma((n, 8)),
            dma((n, 8)),
            dma((n, 4)),
            dma((n, 4)),
            dma((n + 1,)),
            dma((4,)),
            dma((4,)),
            dma((8,)),
            dma((8,)),
            dma((16,)),
            dma((16,)),
            dma((2,)),
            dma((3, 2)),
            dma((3, 2)),
            dma((2,)),
        ],
        compiler_params=pltpu.CompilerParams(
            collective_id=1, has_side_effects=True, vmem_limit_bytes=48 * 1024 * 1024
        ),
        cost_estimate=pl.CostEstimate(flops=0, bytes_accessed=200_000_000, transcendentals=0),
        name="reduce_all",
    )(counts, xf, dyf, dgate, dup, hidden, res, dx, close)


def project_rows(x, dy, wg, wu, wd):
    gate = jnp.dot(x, wg, preferred_element_type=F32)
    up = jnp.dot(x, wu, preferred_element_type=F32)
    sig = jax.nn.sigmoid(gate)
    silu = gate * sig
    hidden = (silu * up).astype(BF)
    out = lax.dot_general(hidden, wd, (((1,), (1,)), ((), ())), preferred_element_type=F32)
    dhidden = jnp.dot(dy, wd, preferred_element_type=F32)
    dgate = (dhidden * up * sig * (1.0 + gate * (1.0 - sig))).astype(BF)
    dup = (dhidden * silu).astype(BF)
    dx = lax.dot_general(dgate, wg, (((1,), (1,)), ((), ())), preferred_element_type=F32)
    dx = dx + lax.dot_general(dup, wu, (((1,), (1,)), ((), ())), preferred_element_type=F32)
    return out.astype(BF), dx.astype(BF), hidden, dgate, dup


def shards(tokens, cotangent, tags, counts, target, gate_weight, up_weight, down_weight):
    feats = tokens.shape[1]
    w_gate, w_up, w_down, full_x, full_dy, close, into = gather_all(
        counts, gate_weight, up_weight, down_weight, tokens, cotangent, tags, target
    )
    depth = full_x.shape[1]
    w_gate, w_up, w_down = (w.reshape(depth, -1) for w in (w_gate, w_up, w_down))
    out, dx, hidden, dgate, dup = project_rows(full_x, full_dy, w_gate, w_up, w_down)
    gate_grad, up_grad, down_grad, back = reduce_all(
        counts, full_x, full_dy, dgate, dup, hidden, out, dx, close
    )
    wide = close.shape[0]
    result = lax.dot_general(
        into,
        back.reshape(wide, 2 * feats),
        (((0,), (0,)), ((), ())),
        preferred_element_type=F32,
    ).astype(BF)
    return result[:, :feats], result[:, feats:], gate_grad, up_grad, down_grad


def solution(mesh):
    in_specs = (
        P("group", "mp"),
        P("group", "mp"),
        P("group"),
        P(),
        P("group"),
        P(None, "group", "mp"),
        P(None, "group", "mp"),
        P(None, "group", "mp"),
    )
    out_specs = (
        P("group", "mp"),
        P("group", "mp"),
        P(None, "group", "mp"),
        P(None, "group", "mp"),
        P(None, "group", "mp"),
    )
    return jax.shard_map(shards, mesh=mesh, in_specs=in_specs, out_specs=out_specs, check_vma=False)
```

```python
import jax
import jax.numpy as jnp
from jax import lax
from jax.experimental import pallas as pl
from jax.experimental.pallas import tpu as pltpu
from jax.sharding import PartitionSpec as P

BF = jnp.bfloat16
F32 = jnp.float32
NX, NZ = 4, 8
HALF = NX * NZ
CAP = 12
SLOT = 16
UNITS = (
    (0, 0, 384),
    (0, 384, 640),
    (1, 0, 512),
    (1, 512, 512),
    (2, 0, 384),
    (2, 384, 256),
)
FLIP = (2, 640, 384)


def place():
    g = lax.axis_index("group")
    p = lax.axis_index("mp")
    h = lax.div(g, HALF)
    x = lax.rem(lax.div(g, NZ), NX)
    z = lax.rem(g, NZ)
    return p, h, x, z


def around(v, by, size):
    return lax.rem(v + (by + size), size)


def rows16(c):
    return pl.ds(pl.multiple_of(c * 16, 16), 16)


def greet(peers):
    barrier = pltpu.get_barrier_semaphore()
    for peer in peers:
        pl.semaphore_signal(barrier, inc=1, device_id=peer, device_id_type=pl.DeviceIdType.MESH)
    pl.semaphore_wait(barrier, len(peers))


def remote(src, dst, send, recv, peer):
    copy = pltpu.make_async_remote_copy(
        src_ref=src,
        dst_ref=dst,
        send_sem=send,
        recv_sem=recv,
        device_id=peer,
        device_id_type=pl.DeviceIdType.MESH,
    )
    copy.start()
    return copy


def peers_of(p, h, x, z):
    def at(hh, xx, zz):
        return (hh * HALF + xx * NZ + zz, p)

    zline = [at(h, x, around(z, d, NZ)) for d in range(1, NZ)]
    yx = h * NX + x
    plane = []
    for d in range(1, 2 * NX):
        k = around(yx, d, 2 * NX)
        plane.append((k, at(lax.div(k, NX), lax.rem(k, NX), z)))
    g = h * HALF + x * NZ + z
    core = p + 1 - 2 * lax.rem(p, 2)
    opposite = around(p, 2, 4)
    both = around(core, 2, 4)
    parts = [(core, (g, core)), (opposite, (g, opposite)), (both, (g, both))]
    return at, zline, plane, parts


def starts(counts, rows):
    b = lax.div(counts[0], rows)
    return b, lax.div(counts[0] + counts[1], rows)


def flag_of(begin, g):
    b, c = begin
    mod = (g >= b).astype(jnp.int32) + (g >= c).astype(jnp.int32)
    return jnp.clip(mod - lax.div(g, HALF), 0, 1)


def lanes_of(p, feats):
    return pl.ds(pl.multiple_of(p * feats, 128), feats)


def gather_kernel(
    counts, wg, wu, wd, xhbm, dyhbm, code, og, ou, od, fx, fdy, close, into, *scratch
):
    n = len(UNITS)
    zbuf, sbuf = scratch[:n], scratch[n : 2 * n]
    begins = starts(counts, xhbm.shape[0])
    fbuf, fsend, tmid, rows, mine, tok, xin, dyin = scratch[2 * n : 2 * n + 8]
    ys, yr, zs, zr, xs, xr, own, fs, fr, gs, gr, ts, tr, tl, ms, mr, ml, il = scratch[
        2 * n + 8 :
    ]
    p, h, x, z = place()
    at, zline, plane, parts = peers_of(p, h, x, z)
    over = at(1 - h, x, z)
    xline = [at(h, around(x, d, NX), z) for d in range(1, NX)]
    loads = [pltpu.make_async_copy(xhbm, xin, il.at[0]), pltpu.make_async_copy(dyhbm, dyin, il.at[1])]
    for c in loads:
        c.start()
    placed = {}
    for u in range(n + 1):
        w, c0, width = UNITS[u] if u < n else FLIP
        ours = zbuf[u].at[:, h, rows16(z), :] if u < n else fbuf.at[:, h, x]
        placed[u] = pltpu.make_async_copy(
            (wg, wu, wd)[w].at[pl.ds(h, 2), :, pl.ds(c0, width)], ours, il.at[2 + u]
        )
        placed[u].start()
    greet(zline + [q for _, q in plane] + [q for _, q in parts])
    weights = (wg, wu, wd)
    outs = (og, ou, od)
    sends, waits, local = [], [], []
    cross, near, later = {}, {}, {}

    def begin(u):
        w, c0, width = UNITS[u] if u < n else FLIP
        c = pl.ds(c0, width)
        if u < n:
            theirs = zbuf[u].at[:, h, rows16(z), :]
        else:
            theirs = fbuf.at[:, h, x]
        cross[u] = remote(
            weights[w].at[pl.ds(1 - h, 2), :, c], theirs, ys.at[u], yr.at[u], over
        )
        sends.append(cross[u])

    def first(u):
        placed[u].wait()
        cross[u].wait_recv()
        v = zbuf[u].at[:, :, rows16(z), :]
        hops = ((2, 2), (3, -2), (0, 1), (1, -1))
        near[u] = {
            i: remote(v, v, zs.at[u, i], zr.at[u, i], zline[d % NZ - 1]) for i, d in hops
        }
        sends.extend(near[u].values())

    def second(u):
        later[u] = [near[u][0], near[u][1]]
        for i, by in enumerate((1, -1)):
            near[u][2 + i].wait_recv()
            chunk = rows16(around(z, -2 * by, NZ))
            v = zbuf[u].at[:, :, chunk, :]
            a = remote(v, v, zs.at[u, 4 + i], zr.at[u, 4 + i], zline[by % NZ - 1])
            v = zbuf[u].at[:, i, chunk, :]
            b = remote(v, v, zs.at[u, 6 + i], zr.at[u, 6 + i], zline[2 * by % NZ - 1])
            later[u].extend([a, b])
            sends.extend([a, b])

    def spread(u):
        for c in later[u]:
            c.wait_recv()
        w, c0, width = UNITS[u]
        out = outs[w].at[:, x, :, pl.ds(c0, width)]
        for d in (2, 1, 3, 0):
            f = flag_of(begins, h * HALF + around(x, d, NX) * NZ + z)
            sbuf[u][d] = zbuf[u][f]
            if d == 0:
                a = pltpu.make_async_copy(sbuf[u].at[0], out, own.at[u])
                a.start()
                local.append(a)
            else:
                a = remote(sbuf[u].at[d], out, xs.at[u, d], xr.at[u, d], xline[d - 1])
                sends.append(a)
                waits.append(a)

    def flip_first():
        placed[n].wait()
        cross[n].wait_recv()
        v = fbuf.at[:, :, x]
        near[n] = [remote(v, v, fs.at[d], fr.at[d], xline[d - 1]) for d in (2, 1, 3)]
        sends.extend(near[n])

    def flip_second():
        for c in near[n]:
            c.wait_recv()
        w, c0, width = FLIP
        out = outs[w].at[:, :, rows16(z), pl.ds(c0, width)]
        for d in (4, 3, 5, 2, 6, 1, 7, 0):
            f = flag_of(begins, h * HALF + x * NZ + around(z, d, NZ))
            fsend[d] = fbuf[f]
            if d == 0:
                a = pltpu.make_async_copy(fsend.at[0], out, own.at[n])
                a.start()
                local.append(a)
            else:
                a = remote(fsend.at[d], out, gs.at[d], gr.at[d], zline[d - 1])
                sends.append(a)
                waits.append(a)

    yx = h * NX + x
    stage = {}

    def address():
        count = xin.shape[0]
        groups = 2 * HALF
        wide = groups * SLOT
        for c in loads:
            c.wait()
        kind = code[...] & 3
        base = jnp.where(kind == 0, 0, jnp.where(kind == 1, begins[0], begins[1]))
        dest = base + lax.shift_right_logical(code[...], 2)
        spread_dest = jnp.broadcast_to(dest.astype(F32), (count, count))
        i = lax.broadcasted_iota(jnp.int32, (count, count), 0)
        j = lax.broadcasted_iota(jnp.int32, (count, count), 1)
        same = (spread_dest == spread_dest.T) & (i < j)
        slot = jnp.sum(jnp.where(same, 1.0, 0.0), axis=0, keepdims=True)
        place_row = dest * SLOT + slot.astype(jnp.int32)
        i = lax.broadcasted_iota(jnp.int32, (wide, count), 0)
        into[...] = jnp.where(i == place_row, 1.0, 0.0).astype(BF)
        feats = xin.shape[1]
        i = lax.broadcasted_iota(jnp.int32, (groups, count), 0)
        goes = jnp.where(i == dest, 1.0, 0.0).astype(BF)
        sent = jnp.dot(goes, jnp.ones((count, feats), BF), preferred_element_type=F32)
        spot = lax.broadcasted_iota(jnp.int32, (groups, SLOT, feats), 1)
        for b, v in enumerate((xin, dyin)):
            part = jnp.dot(into[...], v[...], preferred_element_type=F32)
            part = part.reshape(groups, SLOT, feats)
            if b == 0:
                part = jnp.where(spot >= CAP, sent[:, None, :], part)
            tok[:, :, :, b * feats : (b + 1) * feats] = part.astype(BF).reshape(
                2 * NX, NZ, SLOT, feats
            )

    def tokens_plane():
        stage["p"] = []
        for d in range(1, 2 * NX):
            k, peer = plane[d - 1]
            stage["p"].append(
                remote(tok.at[k], tmid.at[yx], ts.at[NZ + d], tr.at[NZ + d], peer)
            )
        sends.extend(stage["p"])
        a = pltpu.make_async_copy(tok.at[yx], tmid.at[yx], tl.at[1])
        a.start()
        stage["pl"] = a

    def tokens_z():
        stage["pl"].wait()
        for c in stage["p"]:
            c.wait_recv()
        stage["z"] = []
        for d in (4, 3, 5, 2, 6, 1, 7):
            to = around(z, d, NZ)
            stage["z"].append(
                remote(tmid.at[:, to], rows.at[:, z], ts.at[d], tr.at[d], zline[d - 1])
            )
        sends.extend(stage["z"])
        a = pltpu.make_async_copy(tmid.at[:, z], rows.at[:, z], tl.at[0])
        a.start()
        stage["zl"] = a

    def compact():
        stage["zl"].wait()
        for c in stage["z"]:
            c.wait_recv()
        groups = 2 * HALF
        spot = lax.broadcasted_iota(jnp.int32, (groups, SLOT, 128), 1)
        head = rows[:, :, :, 0:128].reshape(groups, SLOT, 128).astype(F32)
        count = jnp.sum(jnp.where(spot == CAP, head, 0.0), axis=1)
        i = lax.broadcasted_iota(jnp.int32, (groups, groups), 0)
        j = lax.broadcasted_iota(jnp.int32, (groups, groups), 1)
        lower = jnp.where(i > j, 1.0, 0.0).astype(BF)
        before = jnp.dot(lower, count.astype(BF), preferred_element_type=F32)
        spot = spot.astype(F32)
        rank = jnp.where(spot < count[:, None, :], before[:, None, :] + spot, -1.0)
        rank = rank.reshape(groups * SLOT, 128)
        lane = lax.broadcasted_iota(jnp.int32, (groups * SLOT, 128), 1)
        for b in range(close.shape[1] // 128):
            hit = rank == (lane + b * 128).astype(F32)
            close[:, b * 128 : (b + 1) * 128] = jnp.where(hit, 1.0, 0.0).astype(BF)
        feats = rows.shape[3] // 2
        for b in range(2):
            part = rows[:, :, :, b * feats : (b + 1) * feats].reshape(groups * SLOT, feats)
            picked = lax.dot_general(
                close[...], part, (((0,), (0,)), ((), ())), preferred_element_type=F32
            )
            mine[b] = picked.astype(BF)
        here = lanes_of(p, feats)
        stage["m"] = []
        for b, full in enumerate((fx, fdy)):
            a = pltpu.make_async_copy(mine.at[b], full.at[:, here], ml.at[b])
            a.start()
            local.append(a)
            for i in (1, 0):
                a = remote(mine.at[b], full.at[:, here], ms.at[i, b], mr.at[i, b], parts[i][1])
                sends.append(a)
                stage["m"].append(a)

    def share():
        for c in stage["m"]:
            c.wait_recv()
        there = lanes_of(parts[1][0], fx.shape[1] // 4)
        for b, full in enumerate((fx, fdy)):
            view = full.at[:, there]
            a = remote(view, view, ms.at[2, b], mr.at[2, b], parts[0][1])
            sends.append(a)
            waits.append(a)

    for u in range(n + 1):
        begin(u)
    first(0)
    flip_first()
    address()
    tokens_plane()
    second(0)
    first(1)
    spread(0)
    second(1)
    first(2)
    tokens_z()
    spread(1)
    second(2)
    first(3)
    spread(2)
    second(3)
    first(4)
    spread(3)
    second(4)
    first(5)
    compact()
    spread(4)
    second(5)
    flip_second()
    spread(5)
    share()
    for c in waits:
        c.wait_recv()
    for c in sends:
        c.wait_send()
    for c in local:
        c.wait()


def gather_all(counts, wg, wu, wd, tokens, cotangent, tags, target):
    cols = wg.shape[2]
    rows, feats = tokens.shape
    n = len(UNITS)
    vm = pl.BlockSpec(memory_space=pltpu.VMEM)
    hbm = pl.BlockSpec(memory_space=pl.ANY)
    dma = pltpu.SemaphoreType.DMA
    out = jax.ShapeDtypeStruct((2, NX, 16 * NZ, cols), BF)
    full = jax.ShapeDtypeStruct((rows, 4 * feats), BF)
    close = jax.ShapeDtypeStruct((2 * HALF * SLOT, rows), BF)
    return pl.pallas_call(
        gather_kernel,
        out_shape=(out, out, out, full, full, close, close),
        in_specs=[pl.BlockSpec(memory_space=pltpu.SMEM)] + [hbm] * 5 + [vm],
        out_specs=[vm] * 7,
        scratch_shapes=[pltpu.VMEM((2, 2, 16 * NZ, u[2]), BF) for u in UNITS]
        + [pltpu.VMEM((4, 2, 16 * NZ, u[2]), BF) for u in UNITS]
        + [
            pltpu.VMEM((2, 2, NX, 16, FLIP[2]), BF),
            pltpu.VMEM((NZ, 2, NX, 16, FLIP[2]), BF),
            pltpu.VMEM((2 * NX, NZ, SLOT, 2 * feats), BF),
            pltpu.VMEM((2 * NX, NZ, SLOT, 2 * feats), BF),
            pltpu.VMEM((2, rows, feats), BF),
            pltpu.VMEM((2 * NX, NZ, SLOT, 2 * feats), BF),
            pltpu.VMEM((rows, feats), BF),
            pltpu.VMEM((rows, feats), BF),
            dma((n + 1,)),
            dma((n + 1,)),
            dma((n, 8)),
            dma((n, 8)),
            dma((n, 4)),
            dma((n, 4)),
            dma((n + 1,)),
            dma((4,)),
            dma((4,)),
            dma((8,)),
            dma((8,)),
            dma((16,)),
            dma((16,)),
            dma((2,)),
            dma((3, 2)),
            dma((3, 2)),
            dma((2,)),
            dma((n + 3,)),
        ],
        compiler_params=pltpu.CompilerParams(
            collective_id=0, has_side_effects=True, vmem_limit_bytes=60 * 1024 * 1024
        ),
        cost_estimate=pl.CostEstimate(flops=0, bytes_accessed=200_000_000, transcendentals=0),
        name="gather_all",
    )(counts, wg, wu, wd, tokens, cotangent, (target * 4 + tags).reshape(1, rows))


def reduce_kernel(
    counts, xf, dyf, dgate, dup, hidden, res, dx, close, og, ou, od, back, *scratch
):
    n = len(UNITS)
    per = 10
    bufs = [scratch[per * u : per * u + per] for u in range(n)]
    ends = [b[7:] for b in bufs] + [scratch[per * n + 3 : per * n + 6]]
    fin, fsum, fgot = scratch[per * n : per * n + 3]
    pin, spread_rows, tmid = scratch[per * n + 6 : per * n + 9]
    made = scratch[per * n + 9 : per * n + 10 + n]
    ys, yr, zs, zr, xs, xr, own, fs, fr, gs, gr, ts, tr, tl, ms, mr, ml = scratch[
        per * n + 10 + n :
    ]
    begins = starts(counts, xf.shape[0])
    p, h, x, z = place()
    at, zline, plane, parts = peers_of(p, h, x, z)
    over = at(1 - h, x, z)
    xline = [at(h, around(x, d, NX), z) for d in range(1, NX)]
    greet(zline + [q for _, q in plane] + [q for _, q in parts])
    pairs = ((xf, dgate), (xf, dup), (dyf, hidden))
    outs = (og, ou, od)
    order = UNITS[::-1]
    sends = []
    arriving, stepping, cross, stage = {}, {}, {}, {}

    def make(u):
        w, c0, width = order[u] if u < n else FLIP
        left, right = pairs[w]
        deep = 32 * NZ

        def body(i, _):
            cut = pl.ds(pl.multiple_of(i * deep, deep), deep)
            v = lax.dot_general(
                left[:, cut],
                right[:, c0 : c0 + width],
                (((0,), (0,)), ((), ())),
                preferred_element_type=F32,
            ).astype(BF)
            y = lax.div(i, 2)
            k = lax.rem(i, 2) * 2
            made[u][y, k] = v[: deep // 2]
            made[u][y, k + 1] = v[deep // 2 :]
            return 0

        lax.fori_loop(0, 4, body, 0)

    def spread(u):
        make(u)
        g = made[u]
        rbuf = bufs[u][0]
        arriving[u] = []
        for d in (2, 1, 3):
            a = remote(
                g.at[:, around(x, d, NX)],
                rbuf.at[d],
                xs.at[u, d],
                xr.at[u, d],
                xline[d - 1],
            )
            arriving[u].append(a)
            sends.append(a)
        a = pltpu.make_async_copy(g.at[:, x], rbuf.at[0], own.at[u])
        a.start()
        arriving[u].append(a)

    def arrive(u):
        for c in arriving[u][:3]:
            c.wait_recv()
        arriving[u][3].wait()

    def binned(terms, marks):
        low = high = None
        for v, m in zip(terms, marks):
            v = v.astype(F32)
            b = v * m
            a = v - b
            low = a if low is None else low + a
            high = b if high is None else high + b
        return low.astype(BF), high.astype(BF)

    xmarks = [
        flag_of(begins, h * HALF + around(x, -d, NX) * NZ + z).astype(F32) for d in range(NX)
    ]

    def bins(u):
        rbuf, zsum = bufs[u][:2]

        def body(i, _):
            y = lax.div(i, NZ)
            r = rows16(lax.rem(i, NZ))
            low, high = binned([rbuf[k, y, r, :] for k in range(NX)], xmarks)
            zsum[0, y, r, :] = low
            zsum[1, y, r, :] = high
            return 0

        lax.fori_loop(0, 2 * NZ, body, 0)

    def first(u):
        zsum, dbuf, tbuf, hbuf = bufs[u][1:5]
        stepping[u] = []
        for i, by in enumerate((1, -1)):
            a = remote(
                zsum.at[:, :, rows16(around(z, 3 * by, NZ)), :],
                tbuf.at[i],
                zs.at[u, i],
                zr.at[u, i],
                zline[by % NZ - 1],
            )
            b = remote(
                zsum.at[:, i, rows16(around(z, 4, NZ)), :],
                hbuf.at[i],
                zs.at[u, 2 + i],
                zr.at[u, 2 + i],
                zline[2 * by % NZ - 1],
            )
            stepping[u].append((a, b))
            sends.extend([a, b])
        for i, by in enumerate((1, -1)):
            a = remote(
                zsum.at[:, :, rows16(around(z, by, NZ)), :],
                dbuf.at[i],
                zs.at[u, 4 + i],
                zr.at[u, 4 + i],
                zline[by % NZ - 1],
            )
            stepping[u].append(a)
            sends.append(a)

    def second(u):
        zsum, dbuf, tbuf, hbuf, obuf, ebuf = bufs[u][1:7]
        waits = stepping[u][2:]
        for i, by in enumerate((1, -1)):
            for c in stepping[u][i]:
                c.wait_recv()
            part = rows16(around(z, 2 * by, NZ))
            for y in range(2):
                v = zsum[:, y, part, :].astype(F32) + tbuf[i, :, y].astype(F32)
                if y == i:
                    v = v + hbuf[i].astype(F32)
                obuf[i, :, y] = v.astype(BF)
            a = remote(
                obuf.at[i], ebuf.at[i], zs.at[u, 6 + i], zr.at[u, 6 + i], zline[2 * by % NZ - 1]
            )
            waits.append(a)
            sends.append(a)
        stepping[u] = waits

    def swap(u):
        for c in stepping[u]:
            c.wait_recv()
        keep, ysend, yin = ends[u]

        def total(y):
            if u == n:
                v = fsum[:, y, x].astype(F32)
                for d in range(1, NX):
                    v = v + fgot[d, :, y].astype(F32)
                return v
            zsum, dbuf, ebuf = bufs[u][1], bufs[u][2], bufs[u][6]
            v = zsum[:, y, rows16(z), :].astype(F32)
            for b in (dbuf, ebuf):
                v = v + b[0, :, y].astype(F32) + b[1, :, y].astype(F32)
            return v

        ysend[...] = total(1 - h).astype(BF)
        cross[u] = remote(ysend, yin, ys.at[u], yr.at[u], over)
        sends.append(cross[u])
        keep[...] = total(h)

    def finish(u):
        w, c0, width = order[u] if u < n else FLIP
        c = pl.ds(c0, width)
        keep, ysend, yin = ends[u]
        cross[u].wait_recv()
        out = outs[w]
        out[2 * h, :, c] = keep[h]
        out[1, :, c] = keep[1 - h] + yin[h].astype(F32)
        out[2 - 2 * h, :, c] = yin[1 - h].astype(F32)

    def flip_spread():
        make(n)
        g = made[n]
        arriving[n] = []
        for d in (4, 3, 5, 2, 6, 1, 7):
            a = remote(
                g.at[:, :, rows16(around(z, d, NZ)), :],
                fin.at[d],
                gs.at[d],
                gr.at[d],
                zline[d - 1],
            )
            arriving[n].append(a)
            sends.append(a)
        a = pltpu.make_async_copy(g.at[:, :, rows16(z), :], fin.at[0], own.at[n])
        a.start()
        arriving[n].append(a)

    def flip_second():
        for c in arriving[n][:-1]:
            c.wait_recv()
        arriving[n][-1].wait()
        marks = [
            flag_of(begins, h * HALF + x * NZ + around(z, -d, NZ)).astype(F32)
            for d in range(NZ)
        ]

        def body(i, _):
            y = lax.div(i, NX)
            k = lax.rem(i, NX)
            low, high = binned([fin[d, y, k] for d in range(NZ)], marks)
            fsum[0, y, k] = low
            fsum[1, y, k] = high
            return 0

        lax.fori_loop(0, 2 * NX, body, 0)
        stepping[n] = []
        for d in (2, 1, 3):
            a = remote(
                fsum.at[:, :, around(x, d, NX)], fgot.at[d], fs.at[d], fr.at[d], xline[d - 1]
            )
            stepping[n].append(a)
            sends.append(a)

    yx = h * NX + x
    feats = res.shape[1] // 4

    def sums_out():
        stage["m"] = []
        for i in (1, 2, 0):
            q, peer = parts[i]
            for b, v in enumerate((res, dx)):
                stage["m"].append(
                    remote(v.at[:, lanes_of(q, feats)], pin.at[i, b], ms.at[i, b], mr.at[i, b], peer)
                )
        here = lanes_of(p, feats)
        stage["ml"] = []
        for b, v in enumerate((res, dx)):
            a = pltpu.make_async_copy(v.at[:, here], pin.at[3, b], ml.at[b])
            a.start()
            stage["ml"].append(a)

    def widen():
        for c in stage["ml"]:
            c.wait()
        for c in stage["m"]:
            c.wait_recv()
        sends.extend(stage["m"])
        for b in range(2):
            v = pin[3, b].astype(F32)
            for i in range(3):
                v = v + pin[i, b].astype(F32)
            v = jnp.dot(close[...], v.astype(BF), preferred_element_type=F32).astype(BF)
            spread_rows[:, :, :, b * feats : (b + 1) * feats] = v.reshape(
                2 * NX, NZ, SLOT, feats
            )
        stage["z"] = []
        for d in (4, 3, 5, 2, 6, 1, 7):
            stage["z"].append(
                remote(
                    spread_rows.at[:, around(z, d, NZ)],
                    tmid.at[z],
                    ts.at[d],
                    tr.at[d],
                    zline[d - 1],
                )
            )
        sends.extend(stage["z"])
        a = pltpu.make_async_copy(spread_rows.at[:, z], tmid.at[z], tl.at[0])
        a.start()
        stage["zl"] = a

    def homeward():
        stage["zl"].wait()
        for c in stage["z"]:
            c.wait_recv()
        stage["p"] = []
        for d in range(1, 2 * NX):
            k, peer = plane[d - 1]
            stage["p"].append(
                remote(tmid.at[:, k], back.at[yx], ts.at[NZ + d], tr.at[NZ + d], peer)
            )
        sends.extend(stage["p"])
        a = pltpu.make_async_copy(tmid.at[:, yx], back.at[yx], tl.at[1])
        a.start()
        stage["pl"] = a

    sums_out()
    spread(0)
    flip_spread()
    spread(1)
    spread(2)
    spread(3)
    spread(4)
    spread(5)
    arrive(0)
    bins(0)
    first(0)
    widen()
    second(0)
    arrive(1)
    bins(1)
    first(1)
    swap(0)
    second(1)
    arrive(2)
    bins(2)
    first(2)
    swap(1)
    second(2)
    homeward()
    flip_second()
    arrive(3)
    bins(3)
    first(3)
    swap(2)
    second(3)
    arrive(4)
    bins(4)
    first(4)
    swap(3)
    second(4)
    swap(n)
    arrive(5)
    bins(5)
    first(5)
    swap(4)
    second(5)
    swap(n - 1)
    for u in range(n + 1):
        finish((n + u) % (n + 1))
    stage["pl"].wait()
    for c in stage["p"]:
        c.wait_recv()
    for c in sends:
        c.wait_send()


def reduce_all(counts, xf, dyf, dgate, dup, hidden, res, dx, close):
    cols = dgate.shape[1]
    rows = res.shape[0]
    feats = res.shape[1] // 4
    n = len(UNITS)
    vm = pl.BlockSpec(memory_space=pltpu.VMEM)
    hbm = pl.BlockSpec(memory_space=pl.ANY)
    dma = pltpu.SemaphoreType.DMA
    out = jax.ShapeDtypeStruct((3, 16, cols), F32)
    back = jax.ShapeDtypeStruct((2 * NX, NZ, SLOT, 2 * feats), BF)
    bufs = []
    for _, _, wide in UNITS[::-1]:
        bufs += [
            pltpu.VMEM((NX, 2, 16 * NZ, wide), BF),
            pltpu.VMEM((2, 2, 16 * NZ, wide), BF),
            pltpu.VMEM((2, 2, 2, 16, wide), BF),
            pltpu.VMEM((2, 2, 2, 16, wide), BF),
            pltpu.VMEM((2, 2, 16, wide), BF),
            pltpu.VMEM((2, 2, 2, 16, wide), BF),
            pltpu.VMEM((2, 2, 2, 16, wide), BF),
            pltpu.VMEM((2, 16, wide), F32),
            pltpu.VMEM((2, 16, wide), BF),
            pltpu.VMEM((2, 16, wide), BF),
        ]
    wide = FLIP[2]
    bufs += [
        pltpu.VMEM((NZ, 2, NX, 16, wide), BF),
        pltpu.VMEM((2, 2, NX, 16, wide), BF),
        pltpu.VMEM((NX, 2, 2, 16, wide), BF),
        pltpu.VMEM((2, 16, wide), F32),
        pltpu.VMEM((2, 16, wide), BF),
        pltpu.VMEM((2, 16, wide), BF),
    ]
    return pl.pallas_call(
        reduce_kernel,
        out_shape=(out, out, out, back),
        in_specs=[pl.BlockSpec(memory_space=pltpu.SMEM)] + [vm] * 5 + [hbm] * 2 + [vm],
        out_specs=[vm] * 4,
        scratch_shapes=bufs
        + [
            pltpu.VMEM((4, 2, rows, feats), BF),
            pltpu.VMEM((2 * NX, NZ, SLOT, 2 * feats), BF),
            pltpu.VMEM((NZ, 2 * NX, SLOT, 2 * feats), BF),
        ]
        + [pltpu.VMEM((2, NX, 16 * NZ, u[2]), BF) for u in UNITS[::-1] + (FLIP,)]
        + [
            dma((n + 1,)),
            dma((n + 1,)),
            dma((n, 8)),
            dma((n, 8)),
            dma((n, 4)),
            dma((n, 4)),
            dma((n + 1,)),
            dma((4,)),
            dma((4,)),
            dma((8,)),
            dma((8,)),
            dma((16,)),
            dma((16,)),
            dma((2,)),
            dma((3, 2)),
            dma((3, 2)),
            dma((2,)),
        ],
        compiler_params=pltpu.CompilerParams(
            collective_id=1, has_side_effects=True, vmem_limit_bytes=48 * 1024 * 1024
        ),
        cost_estimate=pl.CostEstimate(flops=0, bytes_accessed=200_000_000, transcendentals=0),
        name="reduce_all",
    )(counts, xf, dyf, dgate, dup, hidden, res, dx, close)


def project_rows(x, dy, wg, wu, wd):
    gate = jnp.dot(x, wg, preferred_element_type=F32)
    up = jnp.dot(x, wu, preferred_element_type=F32)
    sig = jax.nn.sigmoid(gate)
    silu = gate * sig
    hidden = (silu * up).astype(BF)
    out = lax.dot_general(hidden, wd, (((1,), (1,)), ((), ())), preferred_element_type=F32)
    dhidden = jnp.dot(dy, wd, preferred_element_type=F32)
    dgate = (dhidden * up * sig * (1.0 + gate * (1.0 - sig))).astype(BF)
    dup = (dhidden * silu).astype(BF)
    dx = lax.dot_general(dgate, wg, (((1,), (1,)), ((), ())), preferred_element_type=F32)
    dx = dx + lax.dot_general(dup, wu, (((1,), (1,)), ((), ())), preferred_element_type=F32)
    return out.astype(BF), dx.astype(BF), hidden, dgate, dup


def shards(tokens, cotangent, tags, counts, target, gate_weight, up_weight, down_weight):
    feats = tokens.shape[1]
    w_gate, w_up, w_down, full_x, full_dy, close, into = gather_all(
        counts, gate_weight, up_weight, down_weight, tokens, cotangent, tags, target
    )
    depth = full_x.shape[1]
    w_gate, w_up, w_down = (w.reshape(depth, -1) for w in (w_gate, w_up, w_down))
    out, dx, hidden, dgate, dup = project_rows(full_x, full_dy, w_gate, w_up, w_down)
    gate_grad, up_grad, down_grad, back = reduce_all(
        counts, full_x, full_dy, dgate, dup, hidden, out, dx, close
    )
    wide = close.shape[0]
    result = lax.dot_general(
        into,
        back.reshape(wide, 2 * feats),
        (((0,), (0,)), ((), ())),
        preferred_element_type=F32,
    ).astype(BF)
    return result[:, :feats], result[:, feats:], gate_grad, up_grad, down_grad


def solution(mesh):
    in_specs = (
        P("group", "mp"),
        P("group", "mp"),
        P("group"),
        P(),
        P("group"),
        P(None, "group", "mp"),
        P(None, "group", "mp"),
        P(None, "group", "mp"),
    )
    out_specs = (
        P("group", "mp"),
        P("group", "mp"),
        P(None, "group", "mp"),
        P(None, "group", "mp"),
        P(None, "group", "mp"),
    )
    return jax.shard_map(shards, mesh=mesh, in_specs=in_specs, out_specs=out_specs, check_vma=False)
```
